32 devices in a mesh: gx: 2 (over core), gy: 4 (over z), gz: 4 (over y, x).
Axes of the slice: x: 2, y: 2, z: 4, core: 2. Of those that a mesh axis runs over, the one named last changes fastest.
Arguments:
- populations: float32 [19, 4, 16, 1024], P(None, 'gx', 'gy', 'gz'), as said below
- grain_cell: int32 [2, 2, 8, 512], P(None, 'gx', 'gy', 'gz'), may hold values from 0 to 7, as said below
- grain_offset: float32 [3, 2, 2, 8, 512], P(None, None, 'gx', 'gy', 'gz'), may hold values from 0 to 1
- grain_radius: float32 [2, 2, 8, 512], P(None, 'gx', 'gy', 'gz'), may hold values from 0 to 0.95, as said below
- grain_velocity: float32 [3, 2, 2, 8, 512], P(None, None, 'gx', 'gy', 'gz'), may hold values from -0.5 to 0.5
- grain_spin: float32 [3, 2, 2, 8, 512], P(None, None, 'gx', 'gy', 'gz'), may hold values from -1 to 1
- intersection: float32 [27, 2, 2, 8, 512], P(None, None, 'gx', 'gy', 'gz'), may hold values from 0 to 1, as said below
Outputs:
- new_populations: float32 [19, 4, 16, 1024], P(None, 'gx', 'gy', 'gz')
- grain_loads: float32 [6, 2, 2, 8, 512], P(None, None, 'gx', 'gy', 'gz')
The draws below stay inside these ranges and needn't reach their ends.
Inputs may be any that keep to these rules, and one draw needn't show every extreme that they name: `populations`: every entry is positive. `grain_cell`: the 2 slots of one bin name different cells. `grain_radius`: 0 marks an empty slot; an occupied slot has a radius of 0.6 or more. `intersection`: all 27 values are 0 for an empty slot and 0.1 or more for an occupied one.
All inputs are finite; a program needn't handle non-finite values.
Results may differ from the reference program's by a relative error of at most 0.0001.
Values sent between devices are 32-bit elements; how exact they have to be, the bound alone decides.
No kernel may reach another device: no remote copies, remote signals or barrier semaphores. Data moves between devices by JAX's collectives and lax.ppermute only.
A program may use at most 64 MiB of HBM per device.

```python
import jax
import jax.numpy as jnp
from jax import lax

SLOTS = 2
NX = 4
NY = 16
NZ = 1024


base_density = 3.0


LATTICE_WEIGHTS = [1.0 / 3.0] + [1.0 / 18.0] * 6 + [1.0 / 36.0] * 12


def occupied_slots(key):
    picks = jax.random.randint(key, (SLOTS, NX // 2, NY // 2, NZ // 2), 0, 5)
    return (picks < 3).astype(jnp.float32)


def draw_grain_radius(key, part):
    occupied = occupied_slots(key)
    key = jax.random.fold_in(key, 11)
    radius = jax.random.uniform(key, occupied.shape, jnp.float32, 0.6, 0.95)
    return radius * occupied


def draw_intersection(key, part):
    occupied = occupied_slots(key)
    key = jax.random.fold_in(key, 12)
    fractions = jax.random.uniform(key, (27,) + occupied.shape, jnp.float32, 0.1, 1.0)
    return fractions * occupied[None]


def draw_grain_cell(key, part):
    key = jax.random.fold_in(key, 13)
    scores = jax.random.randint(key, (8, NX // 2, NY // 2, NZ // 2), 0, 2 ** 20) * 8
    scores = scores + jnp.arange(8, dtype=jnp.int32)[:, None, None, None]
    ordering = jnp.argsort(scores, axis=0, stable=True)
    return ordering[:SLOTS].astype(jnp.int32)


def draw_populations(key, part):
    key = jax.random.fold_in(key, 14)
    shape = (19, NX, NY, NZ)
    lattice = jnp.array(LATTICE_WEIGHTS, jnp.float32).reshape(19, 1, 1, 1)
    factor = jnp.exp(jax.random.uniform(key, shape, jnp.float32, -0.6, 0.6))
    return base_density * lattice * factor


def levels(rng, shape, pieces, low, top_value):
    def one(axis_at, parts):
        steps = jax.random.uniform(jax.random.fold_in(jax.random.fold_in(rng, 6), axis_at), (parts,), jnp.float32, low / len(pieces), top_value / len(pieces))
        return jnp.repeat(jnp.exp(steps), shape[axis_at] // parts).reshape((-1,) + (1,) * (len(shape) - axis_at - 1))

    factor_of = one(*pieces[0])
    for cut in pieces[1:]:
        factor_of = factor_of * one(*cut)
    return factor_of


def noise(own_key, dims, width, reach, split=(), held_as=jnp.bfloat16):
    loudness = levels(own_key, dims, split, -0.22, 0.18) if split else 1.0
    values = jax.random.normal(own_key, dims, jnp.float32) * width * loudness
    return jnp.minimum(jnp.maximum(values, -reach), reach).astype(held_as)


def setup_inputs(seed: int = 0) -> dict:
    arg_keys = jax.random.split(jax.random.key(seed), 8)
    return {
        "populations": draw_populations(jax.random.fold_in(arg_keys[7], 71), 0),
        "grain_cell": draw_grain_cell(jax.random.fold_in(arg_keys[7], 71), 0),
        "grain_offset": jnp.clip(1.0 * jax.random.uniform(arg_keys[2], (3, SLOTS, NX // 2, NY // 2, NZ // 2), jnp.float32) ** levels(arg_keys[2], (3, SLOTS, NX // 2, NY // 2, NZ // 2), ((2, 2), (3, 4), (4, 4)), -0.2, 0.2), 0.0, 1.0),
        "grain_radius": draw_grain_radius(jax.random.fold_in(arg_keys[7], 71), 0),
        "grain_velocity": noise(arg_keys[4], (3, SLOTS, NX // 2, NY // 2, NZ // 2), 0.1, 0.5, ((2, 2), (3, 4), (4, 4)), jnp.float32),
        "grain_spin": noise(arg_keys[5], (3, SLOTS, NX // 2, NY // 2, NZ // 2), 0.2, 1.0, ((2, 2), (3, 4), (4, 4)), jnp.float32),
        "intersection": draw_intersection(jax.random.fold_in(arg_keys[7], 71), 0),
    }


VELOCITIES = [(0, 0, 0), (1, 0, 0), (-1, 0, 0), (0, 1, 0), (0, -1, 0), (0, 0, 1), (0, 0, -1), (1, 1, 0), (-1, -1, 0), (1, -1, 0), (-1, 1, 0), (1, 0, 1), (-1, 0, -1), (1, 0, -1), (-1, 0, 1), (0, 1, 1), (0, -1, -1), (0, 1, -1), (0, -1, 1)]
WEIGHTS = [1.0 / 3.0] + [1.0 / 18.0] * 6 + [1.0 / 36.0] * 12
OPPOSITE = [0, 2, 1, 4, 3, 6, 5, 8, 7, 10, 9, 12, 11, 14, 13, 16, 15, 18, 17]
NEIGHBOURS = [(step_x, step_y, step_z) for step_x in (-1, 0, 1) for step_y in (-1, 0, 1) for step_z in (-1, 0, 1)]
relax_time = 0.8
fraction_floor = 0.1
distance_floor = 0.5
damp_normal = 2.0
damp_tangent = 1.0

def slot_table(grain_cell):
    cell_codes = jnp.arange(8, dtype=jnp.int32)
    return (grain_cell[:, None] == cell_codes[None, :, None, None, None]).astype(jnp.float32)

def place_cells(values, slot_onehot):
    spreading = lax.optimization_barrier(jnp.sum(values[:, :, None] * slot_onehot[None], axis=1))
    channels = spreading.shape[0]
    bins_x, bins_y, bins_z = (spreading.shape[2], spreading.shape[3], spreading.shape[4])
    spreading = spreading.reshape(channels, 2, 2, 2, bins_x, bins_y, bins_z).transpose(0, 4, 1, 5, 2, 6, 3)
    return spreading.reshape(channels, 2 * bins_x, 2 * bins_y, 2 * bins_z)

def pick_slots(values, slot_onehot):
    channels = values.shape[0]
    bins_x, bins_y, bins_z = (values.shape[1] // 2, values.shape[2] // 2, values.shape[3] // 2)
    grouped = values.reshape(channels, bins_x, 2, bins_y, 2, bins_z, 2).transpose(0, 2, 4, 6, 1, 3, 5)
    grouped = grouped.reshape(channels, 8, bins_x, bins_y, bins_z)
    return lax.optimization_barrier(jnp.sum(grouped[:, None] * slot_onehot[None], axis=2))

def cross_product(first_vector, second_vector):
    return jnp.stack([first_vector[1] * second_vector[2] - first_vector[2] * second_vector[1], first_vector[2] * second_vector[0] - first_vector[0] * second_vector[2], first_vector[0] * second_vector[1] - first_vector[1] * second_vector[0]])

def grain_payload(grain_cell, grain_offset, grain_radius, grain_velocity, grain_spin):
    corner = jnp.stack([grain_cell // 4, grain_cell // 2 % 2, grain_cell % 2]).astype(jnp.float32)
    return jnp.concatenate([corner + grain_offset, grain_radius[None], grain_velocity, grain_spin])

def contact_loads(local_state, neighbour):
    own_state = local_state[:, :, None]
    running = jnp.zeros((6,) + local_state.shape[1:], jnp.float32)
    for offset in NEIGHBOURS:
        other_state = neighbour(offset)[:, None]
        separation = jnp.stack([2.0 * offset[component] + other_state[component] - own_state[component] for component in range(3)])
        distance = jnp.sqrt(lax.optimization_barrier(jnp.sum(separation * separation, axis=0)))
        normal = separation / jnp.maximum(distance, distance_floor)
        intersection_depth = jnp.maximum(own_state[3] + other_state[3] - distance, 0.0)
        strength = own_state[3] * other_state[3] * intersection_depth
        turning = own_state[3] * own_state[7:10] + other_state[3] * other_state[7:10]
        relative = own_state[4:7] - other_state[4:7] + cross_product(turning, normal)
        normal_speed = lax.optimization_barrier(jnp.sum(relative * normal, axis=0))
        contact_force = strength * (-normal - damp_normal * normal_speed * normal - damp_tangent * (relative - normal_speed * normal))
        contact_torque = cross_product(own_state[3] * normal, contact_force)
        running = running + lax.optimization_barrier(jnp.sum(jnp.concatenate([contact_force, contact_torque]), axis=2))
    return running

def deposit_term(weight_cells, motion_cells, offset):
    lever = jnp.stack([offset[component] + 0.5 - motion_cells[6 + component] for component in range(3)])
    moving = motion_cells[0:3] + cross_product(motion_cells[3:6], lever)
    return jnp.concatenate([weight_cells, weight_cells * moving])

def solid_fields(solid_sums):
    fraction = 1.0 - jnp.exp(-solid_sums[0])
    excess = relax_time - 0.5
    weight = fraction * excess / (1.0 - fraction + excess)
    divisor = jnp.maximum(solid_sums[0], fraction_floor)
    return (weight, solid_sums[1:4] / divisor, divisor)

def equilibrium(member, density, velocity):
    vector = VELOCITIES[member]
    projected = vector[0] * velocity[0] + vector[1] * velocity[1] + vector[2] * velocity[2]
    squared = velocity[0] * velocity[0] + velocity[1] * velocity[1] + velocity[2] * velocity[2]
    return WEIGHTS[member] * density * (1.0 + 3.0 * projected + 4.5 * projected * projected - 1.5 * squared)

def collide(populations, weight, solid_velocity):
    density = sum(populations)
    momentum = [sum((VELOCITIES[member][component] * populations[member] for member in range(19))) for component in range(3)]
    fluid_velocity = [momentum[component] / density for component in range(3)]
    fluid_state = [equilibrium(member, density, fluid_velocity) for member in range(19)]
    solid_state = [equilibrium(member, density, solid_velocity) for member in range(19)]
    collided = []
    transfer = [0.0, 0.0, 0.0]
    for member in range(19):
        reverse = OPPOSITE[member]
        exchange_term = populations[reverse] - fluid_state[reverse] - (populations[member] - solid_state[member])
        relaxed = populations[member] - (1.0 - weight) * (populations[member] - fluid_state[member]) / relax_time
        collided.append(relaxed + weight * exchange_term)
        for component in range(3):
            transfer[component] = transfer[component] + VELOCITIES[member][component] * exchange_term
    cell_force = jnp.stack([-weight * transfer[component] for component in range(3)])
    return (collided, cell_force)

def hydro_loads(shifted, weight_list, motion_cells, slot_onehot):
    force_sum = jnp.zeros_like(motion_cells[0:3])
    moment_sum = jnp.zeros_like(motion_cells[0:3])
    for member, offset in enumerate(NEIGHBOURS):
        weighted = weight_list[member] * shifted(offset)
        force_sum = force_sum + weighted
        moment_sum = moment_sum + cross_product((offset[0] + 0.5, offset[1] + 0.5, offset[2] + 0.5), weighted)
    torque_sum = moment_sum - cross_product(motion_cells[6:9], force_sum)
    return pick_slots(jnp.concatenate([force_sum, torque_sum]), slot_onehot)

def reference(populations, grain_cell, grain_offset, grain_radius, grain_velocity, grain_spin, intersection):
    slot_onehot = slot_table(grain_cell)
    payload = grain_payload(grain_cell, grain_offset, grain_radius, grain_velocity, grain_spin)

    def neighbour(offset):
        return jnp.roll(payload, (-offset[0], -offset[1], -offset[2]), axis=(2, 3, 4))
    contact = contact_loads(payload, neighbour)
    motion_cells = place_cells(jnp.concatenate([grain_velocity, grain_spin, grain_offset]), slot_onehot)
    weight_list = [place_cells(intersection[member:member + 1], slot_onehot) for member in range(27)]
    solid_sums = jnp.zeros((4,) + populations.shape[1:], jnp.float32)
    for member, offset in enumerate(NEIGHBOURS):
        deposit = deposit_term(weight_list[member], motion_cells, offset)
        solid_sums = solid_sums + jnp.roll(deposit, offset, axis=(1, 2, 3))
    weight, solid_velocity, divisor = solid_fields(solid_sums)
    collided, cell_force = collide([populations[member] for member in range(19)], weight, solid_velocity)
    force_share = cell_force / divisor
    passed = [jnp.roll(collided[member], VELOCITIES[member], axis=(0, 1, 2)) for member in range(19)]

    def shifted(offset):
        return jnp.roll(force_share, (-offset[0], -offset[1], -offset[2]), axis=(1, 2, 3))
    hydro_part = hydro_loads(shifted, weight_list, motion_cells, slot_onehot)
    return (jnp.stack(passed), hydro_part + contact)
```

```python
import functools

import jax
import jax.numpy as jnp
from jax import lax
from jax.experimental import pallas as pl
from jax.experimental.pallas import tpu as pltpu
from jax.sharding import PartitionSpec as P

VELOCITIES = [
    (0, 0, 0),
    (1, 0, 0),
    (-1, 0, 0),
    (0, 1, 0),
    (0, -1, 0),
    (0, 0, 1),
    (0, 0, -1),
    (1, 1, 0),
    (-1, -1, 0),
    (1, -1, 0),
    (-1, 1, 0),
    (1, 0, 1),
    (-1, 0, -1),
    (1, 0, -1),
    (-1, 0, 1),
    (0, 1, 1),
    (0, -1, -1),
    (0, 1, -1),
    (0, -1, 1),
]
WEIGHTS = [1.0 / 3.0] + [1.0 / 18.0] * 6 + [1.0 / 36.0] * 12
relax_time = 0.8
fraction_floor = 0.1
distance_floor = 0.5

E0, RADIUS, CODE, PLACE = 9, 36, 37, 38
POPS_LANE, SLOT_LANE = 41, 64
Y_FIELDS = list(range(9)) + [RADIUS, CODE]
Y_GRAIN, Y_CORNER, Y_BLOCKS = 19, 34, 36
F32 = jnp.float32


def iota(shape, dim):
    return lax.broadcasted_iota(jnp.int32, shape, dim)


def pick_lanes(values, index):
    return jnp.take_along_axis(values, index, axis=1, mode="promise_in_bounds")


def roll(values, shift, axis):
    size = values.shape[axis]
    return pltpu.roll(values, shift % size, axis) if shift % size else values


def cross(a, b):
    return [
        a[1] * b[2] - a[2] * b[1],
        a[2] * b[0] - a[0] * b[2],
        a[0] * b[1] - a[1] * b[0],
    ]


class Group:
    def __init__(self, refs):
        self.pops, self.cell, self.off, self.rad, self.vel, self.spin, self.inter = refs

    def slot(self, s, field):
        if field < 3:
            return self.vel[field, s, 0]
        if field < 6:
            return self.spin[field - 3, s, 0]
        if field < 9:
            return self.off[field - 6, s, 0]
        if field < RADIUS:
            return self.inter[field - E0, s, 0]
        if field == RADIUS:
            return self.rad[s, 0]
        return self.cell[s, 0].astype(F32)

    def place(self, s):
        code = self.cell[s, 0]
        corner = [code >> 2, (code >> 1) & 1, code & 1]
        return [corner[c].astype(F32) + self.off[c, s, 0] for c in range(3)]


def split_groups(refs, groups):
    return [Group(refs[7 * g : 7 * g + 7]) for g in range(groups)]


def z_pack_kernel(groups, flags, *refs):
    out = refs[-1]
    high = flags[1] == 1
    lane = iota((4, 128), 1)
    index4 = jnp.where(high, jnp.full((4, 128), 127, jnp.int32), jnp.zeros((4, 128), jnp.int32))
    index2 = jnp.where(high, jnp.full((2, 128), 127, jnp.int32), jnp.zeros((2, 128), jnp.int32))
    lane2 = iota((2, 128), 1)
    for g, group in enumerate(split_groups(refs, groups)):
        grain = jnp.zeros((2, 128), F32)
        for s in range(2):
            values = [group.slot(s, field) for field in range(38)] + group.place(s)
            for field, value in enumerate(values):
                grain = jnp.where(lane2 == SLOT_LANE * s + field, pick_lanes(value, index2), grain)
        both = jnp.concatenate([grain[0:1], grain[0:1], grain[1:2], grain[1:2]], axis=0)
        for i in range(2):
            rows = both
            for member in range(19):
                value = group.pops[member, i]
                last = value.shape[1] - 128
                tile = jnp.where(high, value[:, last:], value[:, :128])
                rows = jnp.where(lane == POPS_LANE + member, pick_lanes(tile, index4), rows)
            out[g, 4 * i : 4 * i + 4, :] = rows


def y_pack_kernel(groups, flags, *refs):
    out = refs[-1]
    high = flags[0] == 1
    for g, group in enumerate(split_groups(refs, groups)):
        for member in range(19):
            for i in range(2):
                row = jnp.where(high, group.pops[member, i, 3:4], group.pops[member, i, 0:1])
                for t in range(2):
                    at = 4 * g + 2 * i + t
                    out[member, at : at + 1, :] = row[:, 128 * t : 128 * t + 128]
        for s in range(2):
            for f in range(29):
                if f < 11:
                    value = group.slot(s, Y_FIELDS[f])
                else:
                    kx, q, kz = (f - 11) // 6, (f - 11) // 3 % 2, (f - 11) % 3
                    value = group.inter[9 * kx + 3 * (q + flags[0]) + kz, s, 0]
                q = 2 * f + s
                at = 4 * g + q % 4
                out[Y_GRAIN + q // 4, at : at + 1, :] = jnp.where(high, value[1:2], value[0:1])
    out[Y_GRAIN + 14, :, :] = jnp.where(
        iota((4 * groups, 128), 0) % 4 >= 2, 0.0, out[Y_GRAIN + 14, :, :]
    )
    out[Y_CORNER:Y_BLOCKS, :, :] = jnp.zeros((2, 4 * groups, 128), F32)


def store_z(groups, paired, flags, first, second, held):
    side = flags[1]
    for g in range(groups):
        held[side, g] = first[g]
        held[1 - side, g] = second[(g + 1) % 2 if paired else g]


def corner_kernel(groups, paired, flags, first, second, rows, out, held):
    store_z(groups, paired, flags, first, second, held)
    high = flags[0] == 1
    for side in range(2):
        for g in range(groups):
            for i in range(2):
                value = held[side, g, 4 * i : 4 * i + 4, :]
                at = 4 * g + 2 * i
                out[side, at : at + 2, :] = jnp.where(high, value[2:4], value[0:2])


def equilibrium_parts(velocity):
    squared = 1.0 - 1.5 * (
        velocity[0] * velocity[0] + velocity[1] * velocity[1] + velocity[2] * velocity[2]
    )
    return squared


def dot_lattice(vector, velocity):
    total = None
    for c in range(3):
        if vector[c]:
            if total is None:
                total = velocity[c] if vector[c] > 0 else -velocity[c]
            else:
                total = total + velocity[c] if vector[c] > 0 else total - velocity[c]
    return total


def main_kernel(groups, paired, flags, *refs):
    layers = 2 * groups
    block = split_groups(refs, groups)
    z_first, z_second, y_first, y_second = refs[7 * groups : 7 * groups + 4]
    out_pops, out_loads = refs[7 * groups + 4 : 7 * groups + 6]
    held_z, held_y, edge, placed, solid, passed, share = refs[7 * groups + 6 :]
    targets = [0, 1, 2, layers - 1]

    store_z(groups, paired, flags, z_first, z_second, held_z)
    side = flags[0]
    held_y[side] = y_first[...]
    for b in range(Y_BLOCKS):
        value = y_second[b]
        held_y[1 - side, b] = roll(value, 4, 0) if paired else value
    for s in range(2):
        for layer in range(layers):
            g, i = layer // 2, layer % 2
            at = 4 * g + 2 * i
            edge[s, layer, 2:6, :] = held_z[s, g, 4 * i : 4 * i + 4, :]
            edge[s, layer, 0:2, :] = held_y[0, Y_CORNER + s, at : at + 2, :]
            edge[s, layer, 6:8, :] = held_y[1, Y_CORNER + s, at : at + 2, :]

    row8 = iota((8, 128), 0)
    lane8 = iota((8, 128), 1)
    half = lane8 // 2

    def y_row(end, g, s, field):
        if field in Y_FIELDS:
            f = Y_FIELDS.index(field)
        else:
            k = field - E0
            q = k // 3 % 3 - (1 - end)
            if q not in (0, 1):
                return jnp.zeros((1, 128), F32)
            f = 11 + 6 * (k // 9) + 3 * q + k % 3
        q = 2 * f + s
        at = 4 * g + q % 4
        return held_y[end, Y_GRAIN + q // 4, at : at + 1, :]

    def column(matrix, at):
        return jnp.broadcast_to(matrix[:, at : at + 1], (8, 128))

    def spread(g, s, field):
        own = block[g].slot(s, field)
        low, high = y_row(0, g, s, field), y_row(1, g, s, field)
        rows = jnp.where(
            row8 < 4,
            jnp.where(row8 < 2, low, own[0:1]),
            jnp.where(row8 < 6, own[1:2], high),
        )
        at = SLOT_LANE * s + field
        return jnp.concatenate(
            [
                pick_lanes(rows, half),
                pick_lanes(rows, half + 64),
                jnp.where(
                    lane8 < 64, column(edge[1, 2 * g], at), column(edge[0, 2 * g], at)
                ),
            ],
            axis=1,
        )

    cell_code = (
        2 * (iota((8, 384), 0) % 2) + iota((8, 384), 1) % 2
    ).astype(F32)
    masks = []
    for g in range(groups):
        codes = [spread(g, s, CODE) for s in range(2)]
        for i in range(2):
            masks.append([codes[s] == cell_code + 4.0 * i for s in range(2)])
    for g in range(groups):
        for field in range(36):
            value0, value1 = spread(g, 0, field), spread(g, 1, field)
            for i in range(2):
                mask0, mask1 = masks[2 * g + i]
                placed[field, 2 * g + i] = jnp.where(
                    mask0, value0, jnp.where(mask1, value1, 0.0)
                )
    motion = []
    for layer in range(layers):
        spin = [placed[3 + c, layer] for c in range(3)]
        arm = [0.5 - placed[6 + c, layer] for c in range(3)]
        turn = cross(spin, arm)
        for c in range(3):
            placed[c, layer] = placed[c, layer] + turn[c]

    for n, target in enumerate(targets):
        total = [None] * 4
        for kz in (-1, 0, 1):
            along_z = [None] * 4
            for ky in (-1, 0, 1):
                along_y = [None] * 4
                for kx in (-1, 0, 1):
                    source = (target - kx) % layers
                    weight = placed[E0 + 9 * (kx + 1) + 3 * (ky + 1) + kz + 1, source]
                    spin = [placed[3 + c, source] for c in range(3)]
                    base = [placed[c, source] for c in range(3)]
                    k = (kx, ky, kz)
                    terms = [weight]
                    for c in range(3):
                        u, v = (c + 1) % 3, (c + 2) % 3
                        speed = base[c]
                        if k[v]:
                            speed = speed + spin[u] if k[v] > 0 else speed - spin[u]
                        if k[u]:
                            speed = speed - spin[v] if k[u] > 0 else speed + spin[v]
                        terms.append(weight * speed)
                    along_y = [t if a is None else a + t for a, t in zip(along_y, terms)]
                moved = [roll(a, ky, 0) for a in along_y]
                along_z = [t if a is None else a + t for a, t in zip(along_z, moved)]
            moved = [roll(a, kz, 1) for a in along_z]
            total = [t if a is None else a + t for a, t in zip(total, moved)]
        for f in range(4):
            solid[f, n] = total[f]

    for n, target in enumerate(targets):
        g, i = target // 2, target % 2
        for t in range(3):
            tile = slice(128 * t, 128 * t + 128)
            f = []
            for member in range(19):
                if t < 2:
                    own = block[g].pops[member, i, :, tile]
                    at = 4 * g + 2 * i + t
                    low = held_y[0, member, at : at + 1, :]
                    high = held_y[1, member, at : at + 1, :]
                    f.append(jnp.concatenate([low, low, own, high, high], axis=0))
                else:
                    at = POPS_LANE + member
                    f.append(
                        jnp.where(
                            lane8 < 64, column(edge[1, target], at), column(edge[0, target], at)
                        )
                    )
            sums = [solid[c, n, :, tile] for c in range(4)]
            fraction = 1.0 - jnp.exp(-sums[0])
            excess = relax_time - 0.5
            weight = fraction * excess / (1.0 - fraction + excess)
            inverse = 1.0 / jnp.maximum(sums[0], fraction_floor)
            solid_velocity = [sums[1 + c] * inverse for c in range(3)]
            density = sum(f[1:], f[0])
            momentum = []
            for c in range(3):
                plus = [f[m] for m in range(19) if VELOCITIES[m][c] > 0]
                minus = [f[m] for m in range(19) if VELOCITIES[m][c] < 0]
                momentum.append(sum(plus[1:], plus[0]) - sum(minus[1:], minus[0]))
            per_density = 1.0 / density
            fluid_velocity = [momentum[c] * per_density for c in range(3)]
            for c in range(3):
                share[c, n, :, tile] = (
                    weight * inverse * (momentum[c] - density * solid_velocity[c])
                )
            relax = (1.0 - weight) * (1.0 / relax_time)
            keep = 1.0 - relax
            fluid_base = equilibrium_parts(fluid_velocity)
            solid_base = equilibrium_parts(solid_velocity)
            if n < 2:
                members = list(range(19))
            else:
                sign = -1 if n == 2 else 1
                members = [m for m in range(19) if VELOCITIES[m][0] == sign]
            done = {}
            for member in [0] + list(range(1, 19, 2)):
                reverse = member + 1 if member else 0
                if member not in members and reverse not in members:
                    continue
                part = WEIGHTS[member] * density
                if member == 0:
                    fluid = [part * fluid_base] * 2
                    settled = [part * solid_base] * 2
                else:
                    vector = VELOCITIES[member]
                    ends = []
                    for base, velocity in (
                        (fluid_base, fluid_velocity),
                        (solid_base, solid_velocity),
                    ):
                        along = dot_lattice(vector, velocity)
                        even = base + 4.5 * along * along
                        odd = 3.0 * along
                        ends.append([part * (even + odd), part * (even - odd)])
                    fluid, settled = ends
                pair = [f[member], f[reverse]]
                for way, m in enumerate((member, reverse)[: 2 if member else 1]):
                    if m not in members:
                        continue
                    exchange = (pair[1 - way] - fluid[1 - way]) - (pair[way] - settled[way])
                    value = keep * pair[way] + relax * fluid[way] + weight * exchange
                    passed[m, n, :, tile] = value

    at_layer = {0: 0, 1: 1, 2: 2, -1: 3}
    for member in range(19):
        vector = VELOCITIES[member]
        for i in range(2):
            value = passed[member, at_layer[i - vector[0]]]
            value = roll(value, vector[2], 1)[:, :256]
            out_pops[member, i] = roll(value, vector[1] - 2, 0)[0:4]

    force = [[None] * 3 for _ in range(2)]
    moment = [[None] * 3 for _ in range(2)]

    def add(store, c, value, sign=1):
        if store[c] is None:
            store[c] = value if sign > 0 else -value
        else:
            store[c] = store[c] + value if sign > 0 else store[c] - value

    for kz in (-1, 0, 1):
        across = [[roll(share[c, n], -kz, 1)[:, :256] for c in range(3)] for n in range(4)]
        for ky in (-1, 0, 1):
            near = [[roll(across[n][c], -ky, 0) for c in range(3)] for n in range(4)]
            for i in range(2):
                together = [None] * 3
                for kx in (-1, 0, 1):
                    weight = placed[E0 + 9 * (kx + 1) + 3 * (ky + 1) + kz + 1, i, :, :256]
                    for c in range(3):
                        value = weight * near[at_layer[i + kx]][c]
                        add(together, c, value)
                        if kx and c == 2:
                            add(moment[i], 1, value, -kx)
                        if kx and c == 1:
                            add(moment[i], 2, value, kx)
                for c in range(3):
                    add(force[i], c, together[c])
                if ky:
                    add(moment[i], 0, together[2], ky)
                    add(moment[i], 2, together[0], -ky)
                if kz:
                    add(moment[i], 0, together[1], -kz)
                    add(moment[i], 1, together[0], kz)
    hydro = []
    for i in range(2):
        arm = [0.5 - placed[6 + c, i, :, :256] for c in range(3)]
        turn = cross(arm, force[i])
        hydro.append(force[i] + [moment[i][c] + turn[c] for c in range(3)])

    own = block[0]

    def rows_own(values):
        return jnp.concatenate([values[0], values[0], values[1], values[1]], axis=0)

    def position(code, offset):
        first = jnp.floor(code * 0.25)
        rest = code - 4.0 * first
        second = jnp.floor(rest * 0.5)
        corner = [first, second, rest - 2.0 * second]
        return [corner[c] + offset[c] for c in range(3)]

    def own_field(field):
        return rows_own([own.slot(s, field) for s in range(2)])

    a_place = position(own_field(CODE), [own_field(6 + c) for c in range(3)])
    a_radius = own_field(RADIUS)
    a_speed = [own_field(c) for c in range(3)]
    a_turn = [a_radius * own_field(3 + c) for c in range(3)]
    push = [jnp.zeros((8, 128), F32)] * 3
    twist = [jnp.zeros((8, 128), F32)] * 3
    fields = [CODE, 6, 7, 8, RADIUS, 0, 1, 2, 3, 4, 5]
    lanes = [PLACE, PLACE + 1, PLACE + 2, RADIUS, 0, 1, 2, 3, 4, 5]
    for oy in (-1, 0, 1):
        for g in range(groups):
            steps = [0] if g == 0 else []
            if g == 1:
                steps = steps + [1]
            if g == groups - 1:
                steps = steps + [-1]
            state = []
            for field in fields:
                values = []
                for s in range(2):
                    value = block[g].slot(s, field)
                    if oy < 0:
                        value = jnp.concatenate([y_row(0, g, s, field), value[0:1]], axis=0)
                    if oy > 0:
                        value = jnp.concatenate([value[1:2], y_row(1, g, s, field)], axis=0)
                    values.append(value)
                state.append(jnp.concatenate(values + values, axis=0))
            state = position(state[0], state[1:4]) + state[4:]
            for oz in (-1, 0, 1):
                other = state
                if oz:
                    matrix = edge[(oz + 1) // 2, 2 * g]
                    at = 2 * (oy + 1)
                    rows = jnp.concatenate([matrix[at : at + 1], matrix[at + 2 : at + 3]], axis=0)
                    turned = roll(rows, -SLOT_LANE, 1)
                    matrix = jnp.concatenate([rows, turned, rows, turned], axis=0)
                    end = lane8 == (0 if oz < 0 else 127)
                    other = [
                        jnp.where(end, column(matrix, lanes[q]), roll(state[q], -oz, 1))
                        for q in range(10)
                    ]
                b_radius = other[3]
                turning = [a_turn[c] + b_radius * other[7 + c] for c in range(3)]
                slip = [a_speed[c] - other[4 + c] for c in range(3)]
                gap = [other[c] - a_place[c] for c in range(3)]
                if oy:
                    gap[1] = gap[1] + 2.0 * oy
                if oz:
                    gap[2] = gap[2] + 2.0 * oz
                for ox in steps:
                    first = gap[0] + 2.0 * ox if ox else gap[0]
                    apart = [first, gap[1], gap[2]]
                    distance = jnp.sqrt(
                        apart[0] * apart[0] + apart[1] * apart[1] + apart[2] * apart[2]
                    )
                    scale = 1.0 / jnp.maximum(distance, distance_floor)
                    normal = [apart[c] * scale for c in range(3)]
                    depth = jnp.maximum(a_radius + b_radius - distance, 0.0)
                    strength = a_radius * b_radius * depth
                    swing = cross(turning, normal)
                    relative = [slip[c] + swing[c] for c in range(3)]
                    along = (
                        relative[0] * normal[0]
                        + relative[1] * normal[1]
                        + relative[2] * normal[2]
                    )
                    factor = 1.0 + along
                    pushed = [strength * (factor * normal[c] + relative[c]) for c in range(3)]
                    twisted = cross(normal, pushed)
                    push = [push[c] - pushed[c] for c in range(3)]
                    twist = [twist[c] - twisted[c] for c in range(3)]
    contact = push + [a_radius * twist[c] for c in range(3)]
    contact = [value + roll(value, -2, 0) for value in contact]

    even = (2 * lane8) % 128
    for f in range(6):
        for s in range(2):
            value = jnp.where(masks[0][s][:, :256], hydro[0][f], 0.0) + jnp.where(
                masks[1][s][:, :256], hydro[1][f], 0.0
            )
            value = value + roll(value, -1, 0)
            value = value + roll(value, -1, 1)
            value = jnp.where(
                lane8 < 64, pick_lanes(value[:, :128], even), pick_lanes(value[:, 128:], even)
            )
            both = jnp.concatenate([value[2:3], value[4:5]], axis=0)
            out_loads[f, s, 0] = both + contact[f][4 * s : 4 * s + 2]


VMEM = pl.BlockSpec(memory_space=pltpu.VMEM)
SMEM = pl.BlockSpec(memory_space=pltpu.SMEM)
PARAMS = pltpu.CompilerParams(vmem_limit_bytes=32 * 2**20)


def call(kernel, flags, operands, shapes, scratch=(), aliases=None):
    return pl.pallas_call(
        kernel,
        out_shape=[jax.ShapeDtypeStruct(shape, F32) for shape in shapes],
        in_specs=[SMEM] + [VMEM] * len(operands),
        out_specs=[VMEM] * len(shapes),
        scratch_shapes=[pltpu.VMEM(shape, F32) for shape in scratch],
        compiler_params=PARAMS,
        input_output_aliases=aliases or {},
    )(flags, *operands)


def step(paired, sizes, *blocks):
    nx, ny, nz = sizes
    axes = ("gx", "gy", "gz")

    def permute(value, target):
        pairs = []
        for x in range(nx):
            for y in range(ny):
                for z in range(nz):
                    tx, ty, tz = target(x, y, z)
                    there = ((tx % nx) * ny + ty % ny) * nz + tz % nz
                    pairs.append(((x * ny + y) * nz + z, there))
        return lax.ppermute(value, axes, pairs)

    def swap(value):
        return permute(value, lambda x, y, z: (1 - x, y, z))

    one, zero = jnp.int32(1), jnp.int32(0)
    if paired:
        groups = 2
        ix, iy, iz = [lax.axis_index(axis) for axis in axes]
        flags = jnp.stack([1 - (ix + iy) % 2, 1 - (ix + iz) % 2]).astype(jnp.int32)
        operands = list(blocks) + [swap(block) for block in blocks]
    else:
        groups = 3
        operands = list(blocks)
        operands += [permute(block, lambda x, y, z: (x - 1, y, z)) for block in blocks]
        operands += [permute(block, lambda x, y, z: (x + 1, y, z)) for block in blocks]
    z_shape = (groups, 8, 128)
    y_shape = (Y_BLOCKS, 4 * groups, 128)
    corner_shape = (2, 4 * groups, 128)

    def pack_z(flags):
        return call(functools.partial(z_pack_kernel, groups), flags, operands, [z_shape])[0]

    def pack_y(flags):
        return call(functools.partial(y_pack_kernel, groups), flags, operands, [y_shape])[0]

    def corners(flags, side, ends, rows):
        return pl.pallas_call(
            functools.partial(corner_kernel, groups, paired),
            out_shape=jax.ShapeDtypeStruct(y_shape, F32),
            in_specs=[SMEM, VMEM, VMEM, pl.BlockSpec(memory_space=pl.ANY)],
            out_specs=pl.BlockSpec(
                corner_shape, lambda i: (Y_CORNER // 2, 0, 0), memory_space=pltpu.VMEM
            ),
            grid=(1,),
            scratch_shapes=[pltpu.VMEM((2,) + z_shape, F32)],
            compiler_params=PARAMS,
            input_output_aliases={3: 0},
        )(flags, ends[0], ends[1], rows)

    if paired:
        first = permute(
            pack_z(flags), lambda x, y, z: (x, y, z + (1 if (x + z) % 2 == 0 else -1))
        )
        ends = [first, swap(first)]
        rows = corners(flags, None, ends, pack_y(flags))
        first = permute(rows, lambda x, y, z: (x, y + (1 if (x + y) % 2 == 0 else -1), z))
        halos = [first, swap(first)]
    else:
        flags = jnp.ones((2,), jnp.int32)
        low = jnp.zeros((2,), jnp.int32)
        ends = [
            permute(pack_z(low), lambda x, y, z: (x, y, z - 1)),
            permute(pack_z(flags), lambda x, y, z: (x, y, z + 1)),
        ]
        down = corners(jnp.array([0, 1], jnp.int32), None, ends, pack_y(low))
        up = corners(flags, None, ends, pack_y(flags))
        halos = [
            permute(down, lambda x, y, z: (x, y - 1, z)),
            permute(up, lambda x, y, z: (x, y + 1, z)),
        ]
    scratch = [
        (2,) + z_shape,
        (2,) + y_shape,
        (2, 2 * groups, 8, 128),
        (36, 2 * groups, 8, 384),
        (4, 4, 8, 384),
        (19, 4, 8, 384),
        (3, 4, 8, 384),
    ]
    populations, offset = blocks[0], blocks[2]
    shapes = [populations.shape, (6,) + offset.shape[1:]]
    return tuple(
        call(
            functools.partial(main_kernel, groups, paired),
            flags,
            operands + ends + halos,
            shapes,
            scratch,
        )
    )


def solution(mesh, paired=None):
    sizes = tuple(mesh.shape[axis] for axis in ("gx", "gy", "gz"))
    if paired is None:
        paired = sizes[0] == 2 and sizes[1] % 2 == 0 and sizes[2] % 2 == 0
    cells, bins = P(None, "gx", "gy", "gz"), P(None, None, "gx", "gy", "gz")
    return jax.shard_map(
        functools.partial(step, paired, sizes),
        mesh=mesh,
        in_specs=(cells, cells, bins, cells, bins, bins, bins),
        out_specs=(cells, bins),
        check_vma=False,
    )
```

```python
import functools

import jax
import jax.numpy as jnp
from jax import lax
from jax.experimental import pallas as pl
from jax.experimental.pallas import tpu as pltpu
from jax.sharding import PartitionSpec as P

VELOCITIES = [
    (0, 0, 0),
    (1, 0, 0),
    (-1, 0, 0),
    (0, 1, 0),
    (0, -1, 0),
    (0, 0, 1),
    (0, 0, -1),
    (1, 1, 0),
    (-1, -1, 0),
    (1, -1, 0),
    (-1, 1, 0),
    (1, 0, 1),
    (-1, 0, -1),
    (1, 0, -1),
    (-1, 0, 1),
    (0, 1, 1),
    (0, -1, -1),
    (0, 1, -1),
    (0, -1, 1),
]
WEIGHTS = [1.0 / 3.0] + [1.0 / 18.0] * 6 + [1.0 / 36.0] * 12
relax_time = 0.8
fraction_floor = 0.1
distance_floor = 0.5

E0, RADIUS, CODE, PLACE = 9, 36, 37, 38
POPS_LANE, SLOT_LANE = 41, 64
Y_FIELDS = list(range(9)) + [RADIUS, CODE]
Y_GRAIN, Y_BLOCKS = 76, 17
W_GRAIN, W_BLOCKS = 38, 57
F32 = jnp.float32


def iota(shape, dim):
    return lax.broadcasted_iota(jnp.int32, shape, dim)


def pick_lanes(values, index):
    return jnp.take_along_axis(values, index, axis=1, mode="promise_in_bounds")


def roll(values, shift, axis):
    size = values.shape[axis]
    return pltpu.roll(values, shift % size, axis) if shift % size else values


def cross(a, b):
    return [
        a[1] * b[2] - a[2] * b[1],
        a[2] * b[0] - a[0] * b[2],
        a[0] * b[1] - a[1] * b[0],
    ]


def pack_kernel(flags, *refs):
    sources, (whole, mine, theirs), held, sems = refs[:7], refs[7:10], refs[10:17], refs[17]
    copies = [
        pltpu.make_async_copy(source, target, sems.at[n])
        for n, (source, target) in enumerate(zip(sources, held))
    ]
    for copy in copies[1:] + copies[:1]:
        copy.start()
    pops, cell, off, rad, vel, spin, inter = held
    for copy in copies[1:]:
        copy.wait()

    def slot(s, field):
        if field < 3:
            return vel[field, s, 0]
        if field < 6:
            return spin[field - 3, s, 0]
        if field < 9:
            return off[field - 6, s, 0]
        if field < RADIUS:
            return inter[field - E0, s, 0]
        if field == RADIUS:
            return rad[s, 0]
        return cell[s, 0].astype(F32)

    for field in range(38):
        for s in range(2):
            at = 4 * (field % 2) + 2 * s
            whole[W_GRAIN + field // 2, at : at + 2, :] = slot(s, field)
    for out, end in ((mine.at[0], flags[0]), (theirs, 1 - flags[0])):
        high = end == 1
        for s in range(2):
            for f in range(29):
                if f < 11:
                    value = slot(s, Y_FIELDS[f])
                else:
                    kx, q, kz = (f - 11) // 6, (f - 11) // 3 % 2, (f - 11) % 3
                    value = inter[9 * kx + 3 * (q + end) + kz, s, 0]
                r = Y_GRAIN + 2 * f + s
                out[r // 8, r % 8 : r % 8 + 1, :] = jnp.where(high, value[1:2], value[0:1])
        out[16, 6:8, :] = jnp.zeros((2, 128), F32)
    copies[0].wait()
    for member in range(19):
        for i in range(2):
            value = pops[member, i]
            for t in range(2):
                tile = value[:, 128 * t : 128 * t + 128]
                whole[2 * member + i, 4 * t : 4 * t + 4, :] = tile
                r = 4 * member + 2 * i + t
                first, last = tile[0:1], tile[3:4]
                high = flags[0] == 1
                mine[0, r // 8, r % 8 : r % 8 + 1, :] = jnp.where(high, last, first)
                theirs[r // 8, r % 8 : r % 8 + 1, :] = jnp.where(high, first, last)


class Block:
    def __init__(self, whole, halos, group):
        self.whole, self.halos, self.group = whole, halos, group

    def slot(self, s, field):
        at = 4 * (field % 2) + 2 * s
        return self.whole[W_GRAIN + field // 2, at : at + 2, :]

    def pops(self, member, i, t):
        return self.whole[2 * member + i, 4 * t : 4 * t + 4, :]

    def halo_pops(self, end, member, i, t):
        r = 4 * member + 2 * i + t
        return self.halos[end, self.group, r // 8, r % 8 : r % 8 + 1, :]

    def halo_slot(self, end, s, field):
        if field in Y_FIELDS:
            f = Y_FIELDS.index(field)
        else:
            k = field - E0
            q = k // 3 % 3 - (1 - end)
            if q not in (0, 1):
                return jnp.zeros((1, 128), F32)
            f = 11 + 6 * (k // 9) + 3 * q + k % 3
        r = Y_GRAIN + 2 * f + s
        return self.halos[end, self.group, r // 8, r % 8 : r % 8 + 1, :]

    def bins(self, s, field):
        own = self.slot(s, field)
        row = iota((8, 128), 0)
        low, high = self.halo_slot(0, s, field), self.halo_slot(1, s, field)
        return jnp.where(
            row < 4,
            jnp.where(row < 2, low, own[0:1]),
            jnp.where(row < 6, own[1:2], high),
        )

    def cells(self, member, i, t):
        own = self.pops(member, i, t)
        low, high = self.halo_pops(0, member, i, t), self.halo_pops(1, member, i, t)
        return jnp.concatenate([low, low, own, high, high], axis=0)


def position(code, offset):
    first = jnp.floor(code * 0.25)
    rest = code - 4.0 * first
    second = jnp.floor(rest * 0.5)
    corner = [first, second, rest - 2.0 * second]
    return [corner[c] + offset[c] for c in range(3)]


def store_ends(groups, paired, side, first, second, held):
    for g in range(groups):
        held[side, g] = first[g]
        held[1 - side, g] = second[(g + 1) % 2 if paired else g]


def z_pack_kernel(groups, paired, flags, *refs):
    wholes, (first, second, out, held) = refs[:groups], refs[groups:]
    store_ends(groups, paired, flags[0], first, second, held)
    high = flags[1] == 1
    lane = iota((8, 128), 1)
    index = jnp.where(high, jnp.full((8, 128), 127, jnp.int32), jnp.zeros((8, 128), jnp.int32))
    for g in range(groups):
        block = Block(wholes[g], held, g)
        grain = jnp.zeros((8, 128), F32)
        for s in range(2):
            values = [block.bins(s, field) for field in range(38)]
            values += position(values[CODE], values[6:9])
            for field, value in enumerate(values):
                grain = jnp.where(lane == SLOT_LANE * s + field, pick_lanes(value, index), grain)
        for i in range(2):
            rows = grain
            for member in range(19):
                tile = jnp.where(high, block.cells(member, i, 1), block.cells(member, i, 0))
                rows = jnp.where(lane == POPS_LANE + member, pick_lanes(tile, index), rows)
            out[g, i] = rows


def equilibrium_parts(velocity):
    squared = 1.0 - 1.5 * (
        velocity[0] * velocity[0] + velocity[1] * velocity[1] + velocity[2] * velocity[2]
    )
    return squared


def dot_lattice(vector, velocity):
    total = None
    for c in range(3):
        if vector[c]:
            if total is None:
                total = velocity[c] if vector[c] > 0 else -velocity[c]
            else:
                total = total + velocity[c] if vector[c] > 0 else total - velocity[c]
    return total


def main_kernel(groups, paired, flags, *refs):
    layers = 2 * groups
    wholes = refs[:groups]
    y_first, y_second, z_first, z_second = refs[groups : groups + 4]
    out_pops, out_loads = refs[groups + 4 : groups + 6]
    held_z, held_y, placed, solid, passed, share = refs[groups + 6 :]
    targets = [0, 1, 2, layers - 1]

    store_ends(groups, paired, flags[0], y_first, y_second, held_y)
    store_ends(groups, paired, flags[1], z_first, z_second, held_z)
    block = [Block(wholes[g], held_y, g) for g in range(groups)]

    def edge(end, layer):
        return held_z[end, layer // 2, layer % 2]

    row8 = iota((8, 128), 0)
    lane8 = iota((8, 128), 1)
    half = lane8 // 2

    def column(matrix, at):
        return jnp.broadcast_to(matrix[:, at : at + 1], (8, 128))

    def spread(g, s, field):
        rows = block[g].bins(s, field)
        at = SLOT_LANE * s + field
        return jnp.concatenate(
            [
                pick_lanes(rows, half),
                pick_lanes(rows, half + 64),
                jnp.where(
                    lane8 < 64, column(edge(1, 2 * g), at), column(edge(0, 2 * g), at)
                ),
            ],
            axis=1,
        )

    cell_code = (
        2 * (iota((8, 384), 0) % 2) + iota((8, 384), 1) % 2
    ).astype(F32)
    masks = []
    for g in range(groups):
        codes = [spread(g, s, CODE) for s in range(2)]
        for i in range(2):
            masks.append([codes[s] == cell_code + 4.0 * i for s in range(2)])
    for g in range(groups):
        for field in range(36):
            value0, value1 = spread(g, 0, field), spread(g, 1, field)
            for i in range(2):
                mask0, mask1 = masks[2 * g + i]
                placed[field, 2 * g + i] = jnp.where(
                    mask0, value0, jnp.where(mask1, value1, 0.0)
                )
    motion = []
    for layer in range(layers):
        spin = [placed[3 + c, layer] for c in range(3)]
        arm = [0.5 - placed[6 + c, layer] for c in range(3)]
        turn = cross(spin, arm)
        for c in range(3):
            placed[c, layer] = placed[c, layer] + turn[c]

    for n, target in enumerate(targets):
        total = [None] * 4
        for kz in (-1, 0, 1):
            along_z = [None] * 4
            for ky in (-1, 0, 1):
                along_y = [None] * 4
                for kx in (-1, 0, 1):
                    source = (target - kx) % layers
                    weight = placed[E0 + 9 * (kx + 1) + 3 * (ky + 1) + kz + 1, source]
                    spin = [placed[3 + c, source] for c in range(3)]
                    base = [placed[c, source] for c in range(3)]
                    k = (kx, ky, kz)
                    terms = [weight]
                    for c in range(3):
                        u, v = (c + 1) % 3, (c + 2) % 3
                        speed = base[c]
                        if k[v]:
                            speed = speed + spin[u] if k[v] > 0 else speed - spin[u]
                        if k[u]:
                            speed = speed - spin[v] if k[u] > 0 else speed + spin[v]
                        terms.append(weight * speed)
                    along_y = [t if a is None else a + t for a, t in zip(along_y, terms)]
                moved = [roll(a, ky, 0) for a in along_y]
                along_z = [t if a is None else a + t for a, t in zip(along_z, moved)]
            moved = [roll(a, kz, 1) for a in along_z]
            total = [t if a is None else a + t for a, t in zip(total, moved)]
        for f in range(4):
            solid[f, n] = total[f]

    for n, target in enumerate(targets):
        g, i = target // 2, target % 2
        for t in range(3):
            tile = slice(128 * t, 128 * t + 128)
            f = []
            for member in range(19):
                if t < 2:
                    f.append(block[g].cells(member, i, t))
                else:
                    at = POPS_LANE + member
                    f.append(
                        jnp.where(
                            lane8 < 64, column(edge(1, target), at), column(edge(0, target), at)
                        )
                    )
            sums = [solid[c, n, :, tile] for c in range(4)]
            fraction = 1.0 - jnp.exp(-sums[0])
            excess = relax_time - 0.5
            weight = fraction * excess / (1.0 - fraction + excess)
            inverse = 1.0 / jnp.maximum(sums[0], fraction_floor)
            solid_velocity = [sums[1 + c] * inverse for c in range(3)]
            density = sum(f[1:], f[0])
            momentum = []
            for c in range(3):
                plus = [f[m] for m in range(19) if VELOCITIES[m][c] > 0]
                minus = [f[m] for m in range(19) if VELOCITIES[m][c] < 0]
                momentum.append(sum(plus[1:], plus[0]) - sum(minus[1:], minus[0]))
            per_density = 1.0 / density
            fluid_velocity = [momentum[c] * per_density for c in range(3)]
            for c in range(3):
                share[c, n, :, tile] = (
                    weight * inverse * (momentum[c] - density * solid_velocity[c])
                )
            relax = (1.0 - weight) * (1.0 / relax_time)
            keep = 1.0 - relax
            fluid_base = equilibrium_parts(fluid_velocity)
            solid_base = equilibrium_parts(solid_velocity)
            if n < 2:
                members = list(range(19))
            else:
                sign = -1 if n == 2 else 1
                members = [m for m in range(19) if VELOCITIES[m][0] == sign]
            done = {}
            for member in [0] + list(range(1, 19, 2)):
                reverse = member + 1 if member else 0
                if member not in members and reverse not in members:
                    continue
                part = WEIGHTS[member] * density
                if member == 0:
                    fluid = [part * fluid_base] * 2
                    settled = [part * solid_base] * 2
                else:
                    vector = VELOCITIES[member]
                    ends = []
                    for base, velocity in (
                        (fluid_base, fluid_velocity),
                        (solid_base, solid_velocity),
                    ):
                        along = dot_lattice(vector, velocity)
                        even = base + 4.5 * along * along
                        odd = 3.0 * along
                        ends.append([part * (even + odd), part * (even - odd)])
                    fluid, settled = ends
                pair = [f[member], f[reverse]]
                for way, m in enumerate((member, reverse)[: 2 if member else 1]):
                    if m not in members:
                        continue
                    exchange = (pair[1 - way] - fluid[1 - way]) - (pair[way] - settled[way])
                    value = keep * pair[way] + relax * fluid[way] + weight * exchange
                    passed[m, n, :, tile] = value

    at_layer = {0: 0, 1: 1, 2: 2, -1: 3}
    for member in range(19):
        vector = VELOCITIES[member]
        for i in range(2):
            value = passed[member, at_layer[i - vector[0]]]
            value = roll(value, vector[2], 1)[:, :256]
            out_pops[member, i] = roll(value, vector[1] - 2, 0)[0:4]

    force = [[None] * 3 for _ in range(2)]
    moment = [[None] * 3 for _ in range(2)]

    def add(store, c, value, sign=1):
        if store[c] is None:
            store[c] = value if sign > 0 else -value
        else:
            store[c] = store[c] + value if sign > 0 else store[c] - value

    for kz in (-1, 0, 1):
        across = [[roll(share[c, n], -kz, 1)[:, :256] for c in range(3)] for n in range(4)]
        for ky in (-1, 0, 1):
            near = [[roll(across[n][c], -ky, 0) for c in range(3)] for n in range(4)]
            for i in range(2):
                together = [None] * 3
                for kx in (-1, 0, 1):
                    weight = placed[E0 + 9 * (kx + 1) + 3 * (ky + 1) + kz + 1, i, :, :256]
                    for c in range(3):
                        value = weight * near[at_layer[i + kx]][c]
                        add(together, c, value)
                        if kx and c == 2:
                            add(moment[i], 1, value, -kx)
                        if kx and c == 1:
                            add(moment[i], 2, value, kx)
                for c in range(3):
                    add(force[i], c, together[c])
                if ky:
                    add(moment[i], 0, together[2], ky)
                    add(moment[i], 2, together[0], -ky)
                if kz:
                    add(moment[i], 0, together[1], -kz)
                    add(moment[i], 1, together[0], kz)
    hydro = []
    for i in range(2):
        arm = [0.5 - placed[6 + c, i, :, :256] for c in range(3)]
        turn = cross(arm, force[i])
        hydro.append(force[i] + [moment[i][c] + turn[c] for c in range(3)])

    own = block[0]

    def rows_own(values):
        return jnp.concatenate([values[0], values[0], values[1], values[1]], axis=0)

    def own_field(field):
        return rows_own([own.slot(s, field) for s in range(2)])

    a_place = position(own_field(CODE), [own_field(6 + c) for c in range(3)])
    a_radius = own_field(RADIUS)
    a_speed = [own_field(c) for c in range(3)]
    a_turn = [a_radius * own_field(3 + c) for c in range(3)]
    push = [jnp.zeros((8, 128), F32)] * 3
    twist = [jnp.zeros((8, 128), F32)] * 3
    fields = [CODE, 6, 7, 8, RADIUS, 0, 1, 2, 3, 4, 5]
    lanes = [PLACE, PLACE + 1, PLACE + 2, RADIUS, 0, 1, 2, 3, 4, 5]
    for oy in (-1, 0, 1):
        for g in range(groups):
            steps = [0] if g == 0 else []
            if g == 1:
                steps = steps + [1]
            if g == groups - 1:
                steps = steps + [-1]
            state = []
            for field in fields:
                values = []
                for s in range(2):
                    value = block[g].slot(s, field)
                    if oy < 0:
                        value = jnp.concatenate([block[g].halo_slot(0, s, field), value[0:1]], axis=0)
                    if oy > 0:
                        value = jnp.concatenate([value[1:2], block[g].halo_slot(1, s, field)], axis=0)
                    values.append(value)
                state.append(jnp.concatenate(values + values, axis=0))
            state = position(state[0], state[1:4]) + state[4:]
            for oz in (-1, 0, 1):
                other = state
                if oz:
                    matrix = edge((oz + 1) // 2, 2 * g)
                    at = 2 * (oy + 1)
                    rows = jnp.concatenate([matrix[at : at + 1], matrix[at + 2 : at + 3]], axis=0)
                    turned = roll(rows, -SLOT_LANE, 1)
                    matrix = jnp.concatenate([rows, turned, rows, turned], axis=0)
                    end = lane8 == (0 if oz < 0 else 127)
                    other = [
                        jnp.where(end, column(matrix, lanes[q]), roll(state[q], -oz, 1))
                        for q in range(10)
                    ]
                b_radius = other[3]
                turning = [a_turn[c] + b_radius * other[7 + c] for c in range(3)]
                slip = [a_speed[c] - other[4 + c] for c in range(3)]
                gap = [other[c] - a_place[c] for c in range(3)]
                if oy:
                    gap[1] = gap[1] + 2.0 * oy
                if oz:
                    gap[2] = gap[2] + 2.0 * oz
                for ox in steps:
                    first = gap[0] + 2.0 * ox if ox else gap[0]
                    apart = [first, gap[1], gap[2]]
                    distance = jnp.sqrt(
                        apart[0] * apart[0] + apart[1] * apart[1] + apart[2] * apart[2]
                    )
                    scale = 1.0 / jnp.maximum(distance, distance_floor)
                    normal = [apart[c] * scale for c in range(3)]
                    depth = jnp.maximum(a_radius + b_radius - distance, 0.0)
                    strength = a_radius * b_radius * depth
                    swing = cross(turning, normal)
                    relative = [slip[c] + swing[c] for c in range(3)]
                    along = (
                        relative[0] * normal[0]
                        + relative[1] * normal[1]
                        + relative[2] * normal[2]
                    )
                    factor = 1.0 + along
                    pushed = [strength * (factor * normal[c] + relative[c]) for c in range(3)]
                    twisted = cross(normal, pushed)
                    push = [push[c] - pushed[c] for c in range(3)]
                    twist = [twist[c] - twisted[c] for c in range(3)]
    contact = push + [a_radius * twist[c] for c in range(3)]
    contact = [value + roll(value, -2, 0) for value in contact]

    even = (2 * lane8) % 128
    for f in range(6):
        for s in range(2):
            value = jnp.where(masks[0][s][:, :256], hydro[0][f], 0.0) + jnp.where(
                masks[1][s][:, :256], hydro[1][f], 0.0
            )
            value = value + roll(value, -1, 0)
            value = value + roll(value, -1, 1)
            value = jnp.where(
                lane8 < 64, pick_lanes(value[:, :128], even), pick_lanes(value[:, 128:], even)
            )
            both = jnp.concatenate([value[2:3], value[4:5]], axis=0)
            out_loads[f, s, 0] = both + contact[f][4 * s : 4 * s + 2]


VMEM = pl.BlockSpec(memory_space=pltpu.VMEM)
SMEM = pl.BlockSpec(memory_space=pltpu.SMEM)
PARAMS = pltpu.CompilerParams(vmem_limit_bytes=32 * 2**20)


def call(kernel, flags, operands, shapes, scratch=(), space=pltpu.VMEM):
    return pl.pallas_call(
        kernel,
        out_shape=[jax.ShapeDtypeStruct(shape, F32) for shape in shapes],
        in_specs=[SMEM] + [pl.BlockSpec(memory_space=space)] * len(operands),
        out_specs=[VMEM] * len(shapes),
        scratch_shapes=[pltpu.VMEM(x, F32) if isinstance(x, tuple) else x for x in scratch],
        compiler_params=PARAMS,
    )(flags, *operands)


def step(paired, sizes, *blocks):
    nx, ny, nz = sizes
    axes = ("gx", "gy", "gz")
    groups = 2 if paired else 3

    def permute(value, target):
        pairs = []
        for x in range(nx):
            for y in range(ny):
                for z in range(nz):
                    tx, ty, tz = target(x, y, z)
                    there = ((tx % nx) * ny + ty % ny) * nz + tz % nz
                    pairs.append(((x * ny + y) * nz + z, there))
        return lax.ppermute(value, axes, pairs)

    def swap(value):
        return permute(value, lambda x, y, z: (1 - x, y, z))

    def to_low(value):
        return permute(value, lambda x, y, z: (x - 1, y, z))

    def to_high(value):
        return permute(value, lambda x, y, z: (x + 1, y, z))

    ends_y = (Y_BLOCKS, 8, 128)
    shape_z = (groups, 2, 8, 128)
    shape_y = (groups,) + ends_y
    if paired:
        ix, iy, iz = [lax.axis_index(axis) for axis in axes]
        flags = jnp.stack([1 - (ix + iy) % 2, 1 - (ix + iz) % 2]).astype(jnp.int32)
    else:
        flags = jnp.ones((2,), jnp.int32)
    held = [pltpu.VMEM(block.shape, block.dtype) for block in blocks]
    blocks = [pltpu.with_memory_space_constraint(block, pltpu.HBM) for block in blocks]
    whole, mine, theirs = call(
        pack_kernel,
        flags,
        blocks,
        [(W_BLOCKS, 8, 128), shape_y, ends_y],
        held + [pltpu.SemaphoreType.DMA((7,))],
        pltpu.HBM,
    )

    def pack_z(flags, wholes, halos):
        kernel = functools.partial(z_pack_kernel, groups, paired)
        return call(kernel, flags, wholes + halos, [shape_z], [(2,) + shape_y])[0]

    if paired:
        rows = mine.at[1].set(swap(theirs))
        wholes = [whole, swap(whole)]
        first = permute(rows, lambda x, y, z: (x, y + (1 if (x + y) % 2 == 0 else -1), z))
        halos = [first, swap(first)]
        first = permute(
            pack_z(flags, wholes, halos),
            lambda x, y, z: (x, y, z + (1 if (x + z) % 2 == 0 else -1)),
        )
        ends = [first, swap(first)]
    else:
        wholes = [whole, to_low(whole), to_high(whole)]
        up, down = [jnp.stack([v, to_low(v), to_high(v)]) for v in (mine[0], theirs)]
        halos = [
            permute(down, lambda x, y, z: (x, y - 1, z)),
            permute(up, lambda x, y, z: (x, y + 1, z)),
        ]
        low = jnp.array([1, 0], jnp.int32)
        ends = [
            permute(pack_z(low, wholes, halos), lambda x, y, z: (x, y, z - 1)),
            permute(pack_z(flags, wholes, halos), lambda x, y, z: (x, y, z + 1)),
        ]
    scratch = [
        (2,) + shape_z,
        (2,) + shape_y,
        (36, 2 * groups, 8, 384),
        (4, 4, 8, 384),
        (19, 4, 8, 384),
        (3, 4, 8, 384),
    ]
    populations, offset = blocks[0], blocks[2]
    shapes = [populations.shape, (6,) + offset.shape[1:]]
    kernel = functools.partial(main_kernel, groups, paired)
    return tuple(call(kernel, flags, wholes + halos + ends, shapes, scratch))


def solution(mesh, paired=None):
    sizes = tuple(mesh.shape[axis] for axis in ("gx", "gy", "gz"))
    if paired is None:
        paired = sizes[0] == 2 and sizes[1] % 2 == 0 and sizes[2] % 2 == 0
    cells, bins = P(None, "gx", "gy", "gz"), P(None, None, "gx", "gy", "gz")
    return jax.shard_map(
        functools.partial(step, paired, sizes),
        mesh=mesh,
        in_specs=(cells, cells, bins, cells, bins, bins, bins),
        out_specs=(cells, bins),
        check_vma=False,
    )
```

```python
import functools

import jax
import jax.numpy as jnp
from jax import lax
from jax.experimental import pallas as pl
from jax.experimental.pallas import tpu as pltpu
from jax.sharding import PartitionSpec as P

VELOCITIES = [
    (0, 0, 0),
    (1, 0, 0),
    (-1, 0, 0),
    (0, 1, 0),
    (0, -1, 0),
    (0, 0, 1),
    (0, 0, -1),
    (1, 1, 0),
    (-1, -1, 0),
    (1, -1, 0),
    (-1, 1, 0),
    (1, 0, 1),
    (-1, 0, -1),
    (1, 0, -1),
    (-1, 0, 1),
    (0, 1, 1),
    (0, -1, -1),
    (0, 1, -1),
    (0, -1, 1),
]
WEIGHTS = [1.0 / 3.0] + [1.0 / 18.0] * 6 + [1.0 / 36.0] * 12
relax_time = 0.8
fraction_floor = 0.1
distance_floor = 0.5

E0, RADIUS, CODE, PLACE = 9, 36, 37, 38
POPS_AT, CODE_AT, EDGE_VALUES = 36, 55, 57
Z_TILES, CONTACT_TILE = 8, 7
Y_FIELDS = list(range(9)) + [RADIUS, CODE]
Y_GRAIN, Y_BLOCKS = 76, 17
W_GRAIN, W_BLOCKS = 38, 57
F32 = jnp.float32


def iota(shape, dim):
    return lax.broadcasted_iota(jnp.int32, shape, dim)


def pick_lanes(values, index):
    return jnp.take_along_axis(values, index, axis=1, mode="promise_in_bounds")


def roll(values, shift, axis):
    size = values.shape[axis]
    return pltpu.roll(values, shift % size, axis) if shift % size else values


def cross(a, b):
    return [
        a[1] * b[2] - a[2] * b[1],
        a[2] * b[0] - a[0] * b[2],
        a[0] * b[1] - a[1] * b[0],
    ]


def pack_kernel(flags, *refs):
    sources, (whole, mine, theirs), held, sems = refs[:7], refs[7:10], refs[10:17], refs[17]
    copies = [
        pltpu.make_async_copy(source, target, sems.at[n])
        for n, (source, target) in enumerate(zip(sources, held))
    ]
    for copy in copies[1:] + copies[:1]:
        copy.start()
    pops, cell, off, rad, vel, spin, inter = held
    for copy in copies[1:]:
        copy.wait()

    def slot(s, field, rows=slice(None)):
        if field < 3:
            return vel[field, s, 0, rows, :]
        if field < 6:
            return spin[field - 3, s, 0, rows, :]
        if field < 9:
            return off[field - 6, s, 0, rows, :]
        if field < RADIUS:
            return inter[field - E0, s, 0, rows, :]
        if field == RADIUS:
            return rad[s, 0, rows, :]
        return cell[s, 0, rows, :].astype(F32)

    for field in range(38):
        for s in range(2):
            at = 4 * (field % 2) + 2 * s
            whole[W_GRAIN + field // 2, at : at + 2, :] = slot(s, field)
    for out, end in ((mine.at[0], flags[0]), (theirs, 1 - flags[0])):
        for s in range(2):
            for f in range(29):
                if f < 11:
                    value = slot(s, Y_FIELDS[f], pl.ds(end, 1))
                else:
                    kx, q, kz = (f - 11) // 6, (f - 11) // 3 % 2, (f - 11) % 3
                    value = inter[9 * kx + 3 * (q + end) + kz, s, 0, pl.ds(end, 1), :]
                r = Y_GRAIN + 2 * f + s
                out[r // 8, r % 8 : r % 8 + 1, :] = value
        out[16, 6:8, :] = jnp.zeros((2, 128), F32)
    copies[0].wait()
    for out, end in ((mine.at[0], flags[0]), (theirs, 1 - flags[0])):
        for member in range(19):
            for i in range(2):
                row = pops[member, i, pl.ds(3 * end, 1), :]
                for t in range(2):
                    r = 4 * member + 2 * i + t
                    out[r // 8, r % 8 : r % 8 + 1, :] = row[:, 128 * t : 128 * t + 128]
    for member in range(19):
        for i in range(2):
            for t in range(2):
                tile = pops[member, i, :, 128 * t : 128 * t + 128]
                whole[2 * member + i, 4 * t : 4 * t + 4, :] = tile


class Block:
    def __init__(self, whole, halos, group):
        self.whole, self.halos, self.group = whole, halos, group

    def slot(self, s, field):
        at = 4 * (field % 2) + 2 * s
        return self.whole[W_GRAIN + field // 2, at : at + 2, :]

    def pops(self, member, i, t):
        return self.whole[2 * member + i, 4 * t : 4 * t + 4, :]

    def halo_pops(self, end, member, i, t):
        r = 4 * member + 2 * i + t
        return self.halos[end, self.group, r // 8, r % 8 : r % 8 + 1, :]

    def halo_slot(self, end, s, field):
        if field in Y_FIELDS:
            f = Y_FIELDS.index(field)
        else:
            k = field - E0
            q = k // 3 % 3 - (1 - end)
            if q not in (0, 1):
                return jnp.zeros((1, 128), F32)
            f = 11 + 6 * (k // 9) + 3 * q + k % 3
        r = Y_GRAIN + 2 * f + s
        return self.halos[end, self.group, r // 8, r % 8 : r % 8 + 1, :]

    def bins(self, s, field):
        row = iota((8, 128), 0)
        n, at = W_GRAIN + field // 2, 4 * (field % 2) + 2 * s
        rows = [
            self.halo_slot(0, s, field),
            self.whole[n, at : at + 1, :],
            self.whole[n, at + 1 : at + 2, :],
            self.halo_slot(1, s, field),
        ]
        rows = [jnp.broadcast_to(value, (8, 128)) for value in rows]
        return jnp.where(
            row < 4,
            jnp.where(row < 2, rows[0], rows[1]),
            jnp.where(row < 6, rows[2], rows[3]),
        )

    def cells(self, member, i, t):
        row = iota((8, 128), 0)
        own = self.whole[2 * member + i]
        if isinstance(t, int):
            own = roll(own, 2 - 4 * t, 0)
            low, high = [self.halo_pops(end, member, i, t) for end in range(2)]
        else:
            own = jnp.where(t, roll(own, -2, 0), roll(own, 2, 0))
            low, high = [
                jnp.where(
                    t, self.halo_pops(end, member, i, 1), self.halo_pops(end, member, i, 0)
                )
                for end in range(2)
            ]
        low, high = jnp.broadcast_to(low, (8, 128)), jnp.broadcast_to(high, (8, 128))
        return jnp.where(row < 2, low, jnp.where(row > 5, high, own))


def position(code, offset):
    first = jnp.floor(code * 0.25)
    rest = code - 4.0 * first
    second = jnp.floor(rest * 0.5)
    corner = [first, second, rest - 2.0 * second]
    return [corner[c] + offset[c] for c in range(3)]


def store_ends(groups, paired, side, first, second, held):
    for g in range(groups):
        held[side, g] = first[g]
        held[1 - side, g] = second[(g + 1) % 2 if paired else g]


def lane_groups(groups):
    return [0, 1, 0, 1] if groups == 2 else [0, 1, 1, 2]


def by_group(groups, values, lane):
    order = lane_groups(groups)
    result = values[order[3]]
    for q in (2, 1, 0):
        if order[q] != order[q + 1] or q < 2:
            result = jnp.where(lane < 32 * (q + 1), values[order[q]], result)
    return result


def by_layer(groups, values, lane):
    odd = lane // 16 % 2 == 1
    pairs = [jnp.where(odd, values[2 * g + 1], values[2 * g]) for g in range(groups)]
    return by_group(groups, pairs, lane)


def cell_codes(lane, row):
    return (4 * (lane // 16 % 2) + 2 * (row % 2) + lane % 2).astype(F32)


def choose(masks, values):
    return jnp.where(masks[0], values[0], jnp.where(masks[1], values[1], 0.0))


def z_pack_kernel(groups, paired, flags, *refs):
    wholes, (first, second, out, held) = refs[:groups], refs[groups:]
    store_ends(groups, paired, flags[0], first, second, held)
    high = flags[1] == 1
    lane, row = iota((8, 128), 1), iota((8, 128), 0)
    block = [Block(wholes[g], held, g) for g in range(groups)]
    start = jnp.where(high, 127, 0)
    index = jnp.full((8, 128), start, jnp.int32)
    pops_index = jnp.full((8, 128), jnp.where(high, 126, 0), jnp.int32) + lane % 2
    inner = lane % 16 // 2

    def picked(s, field):
        values = [pick_lanes(block[g].bins(s, field), index) for g in range(groups)]
        return by_group(groups, values, lane)

    slots = [[picked(s, field) for field in range(38)] for s in range(2)]
    code = cell_codes(lane, row)
    masks = [slots[s][CODE] == code for s in range(2)]
    values = [choose(masks, [slots[0][f], slots[1][f]]) for f in range(36)]
    for member in range(19):
        tiles = []
        for layer in range(2 * groups):
            g, i = layer // 2, layer % 2
            tile = block[g].cells(member, i, high)
            tiles.append(pick_lanes(tile, pops_index))
        values.append(by_layer(groups, tiles, lane))
    for tile in range(CONTACT_TILE):
        packed = values[8 * tile]
        for q in range(1, 8):
            if 8 * tile + q < len(values):
                packed = jnp.where(inner == q, values[8 * tile + q], packed)
        out[tile] = packed
    packed = jnp.zeros((8, 128), F32)
    for s in range(2):
        state = position(slots[s][CODE], slots[s][6:9]) + [slots[s][RADIUS]] + slots[s][0:6]
        for q, value in enumerate(state):
            packed = jnp.where(lane % 32 == 16 * s + q, value, packed)
    out[CONTACT_TILE] = packed


def dot_lattice(vector, velocity):
    total = None
    for c in range(3):
        if vector[c]:
            if total is None:
                total = velocity[c] if vector[c] > 0 else -velocity[c]
            else:
                total = total + velocity[c] if vector[c] > 0 else total - velocity[c]
    return total


def equilibrium_base(velocity):
    return 1.0 - 1.5 * (
        velocity[0] * velocity[0] + velocity[1] * velocity[1] + velocity[2] * velocity[2]
    )


def collide(f, sums, members):
    fraction = 1.0 - jnp.exp(-sums[0])
    excess = relax_time - 0.5
    weight = fraction * excess / (1.0 - fraction + excess)
    inverse = 1.0 / jnp.maximum(sums[0], fraction_floor)
    solid_velocity = [sums[1 + c] * inverse for c in range(3)]
    density = sum(f[1:], f[0])
    momentum = []
    for c in range(3):
        plus = [f[m] for m in range(19) if VELOCITIES[m][c] > 0]
        minus = [f[m] for m in range(19) if VELOCITIES[m][c] < 0]
        momentum.append(sum(plus[1:], plus[0]) - sum(minus[1:], minus[0]))
    per_density = 1.0 / density
    fluid_velocity = [momentum[c] * per_density for c in range(3)]
    share = [weight * inverse * (momentum[c] - density * solid_velocity[c]) for c in range(3)]
    relax = (1.0 - weight) * (1.0 / relax_time)
    keep = 1.0 - relax
    fluid_base = equilibrium_base(fluid_velocity)
    solid_base = equilibrium_base(solid_velocity)
    done = {}
    for member in [0] + list(range(1, 19, 2)):
        reverse = member + 1 if member else 0
        if member not in members and reverse not in members:
            continue
        part = WEIGHTS[member] * density
        if member == 0:
            fluid = [part * fluid_base] * 2
            settled = [part * solid_base] * 2
        else:
            ends = []
            for base, velocity in (
                (fluid_base, fluid_velocity),
                (solid_base, solid_velocity),
            ):
                along = dot_lattice(VELOCITIES[member], velocity)
                even = base + 4.5 * along * along
                odd = 3.0 * along
                ends.append([part * (even + odd), part * (even - odd)])
            fluid, settled = ends
        pair = [f[member], f[reverse]]
        for way, m in enumerate((member, reverse)[: 2 if member else 1]):
            if m in members:
                exchange = (pair[1 - way] - fluid[1 - way]) - (pair[way] - settled[way])
                done[m] = keep * pair[way] + relax * fluid[way] + weight * exchange
    return done, share


def deposit_terms(weight, base, spin, k):
    terms = [weight]
    for c in range(3):
        u, v = (c + 1) % 3, (c + 2) % 3
        speed = base[c]
        if k[v]:
            speed = speed + spin[u] if k[v] > 0 else speed - spin[u]
        if k[u]:
            speed = speed - spin[v] if k[u] > 0 else speed + spin[v]
        terms.append(weight * speed)
    return terms


def plus(totals, terms):
    return list(terms) if totals is None else [a + b for a, b in zip(totals, terms)]


class Moments:
    def __init__(self):
        self.force, self.moment = [None] * 3, [None] * 3

    def add(self, store, c, value, sign):
        if store[c] is None:
            store[c] = value if sign > 0 else -value
        else:
            store[c] = store[c] + value if sign > 0 else store[c] - value

    def turn(self, axis, forces, sign):
        u, v = (axis + 1) % 3, (axis + 2) % 3
        self.add(self.moment, v, forces[u], sign)
        self.add(self.moment, u, forces[v], -sign)

    def push(self, forces):
        for c in range(3):
            self.add(self.force, c, forces[c], 1)

    def loads(self, offset):
        turned = cross([0.5 - value for value in offset], self.force)
        return self.force + [self.moment[c] + turned[c] for c in range(3)]


def pair_force(gap, a_radius, a_speed, a_turn, other, keep=None):
    b_radius = other[0]
    distance = jnp.sqrt(gap[0] * gap[0] + gap[1] * gap[1] + gap[2] * gap[2])
    scale = 1.0 / jnp.maximum(distance, distance_floor)
    normal = [gap[c] * scale for c in range(3)]
    depth = jnp.maximum(a_radius + b_radius - distance, 0.0)
    strength = a_radius * b_radius * depth
    if keep is not None:
        strength = jnp.where(keep, strength, 0.0)
    turning = [a_turn[c] + b_radius * other[4 + c] for c in range(3)]
    swing = cross(turning, normal)
    relative = [a_speed[c] - other[1 + c] + swing[c] for c in range(3)]
    along = relative[0] * normal[0] + relative[1] * normal[1] + relative[2] * normal[2]
    factor = 1.0 + along
    pushed = [strength * (factor * normal[c] + relative[c]) for c in range(3)]
    return pushed, cross(normal, pushed)


def own_state(block):
    def rows(field):
        values = [block.slot(s, field) for s in range(2)]
        return jnp.concatenate([values[0], values[0], values[1], values[1]], axis=0)

    place = position(rows(CODE), [rows(6 + c) for c in range(3)])
    return place, [rows(RADIUS)] + [rows(c) for c in range(6)]


PARTS = [4, 9, 14, 18]
AT_LAYER = {0: 0, 1: 1, 2: 2, -1: 3}


def bulk_kernel(groups, paired, flags, *refs):
    layers = 2 * groups
    wholes, (y_first, y_second) = refs[:groups], refs[groups : groups + 2]
    out_pops, out_loads = refs[groups + 2 : groups + 4]
    held, placed, solid, passed, share = refs[groups + 4 :]
    targets = [0, 1, 2, layers - 1]
    store_ends(groups, paired, flags[0], y_first, y_second, held)
    block = [Block(wholes[g], held, g) for g in range(groups)]
    lane8 = iota((8, 128), 1)
    half = lane8 // 2

    def spread(rows):
        return jnp.concatenate([pick_lanes(rows, half), pick_lanes(rows, half + 64)], axis=1)

    cell_code = (2 * (iota((8, 256), 0) % 2) + iota((8, 256), 1) % 2).astype(F32)
    masks = []
    codes = [[block[g].bins(s, CODE) for g in range(groups)] for s in range(2)]
    for g in range(groups):
        wide = [spread(codes[s][g]) for s in range(2)]
        for i in range(2):
            masks.append([wide[s] == cell_code + 4.0 * i for s in range(2)])
    for field in range(36):
        rows = [[block[g].bins(s, field) for g in range(groups)] for s in range(2)]
        for g in range(groups):
            values = [spread(rows[s][g]) for s in range(2)]
            for i in range(2):
                placed[field, 2 * g + i] = choose(masks[2 * g + i], values)
    for layer in range(layers):
        spin = [placed[3 + c, layer] for c in range(3)]
        turned = cross(spin, [0.5 - placed[6 + c, layer] for c in range(3)])
        for c in range(3):
            placed[c, layer] = placed[c, layer] + turned[c]

    for n, target in enumerate(targets):
        total = None
        for kz in (-1, 0, 1):
            along_z = None
            for ky in (-1, 0, 1):
                along_y = None
                for kx in (-1, 0, 1):
                    source = (target - kx) % layers
                    weight = placed[E0 + 9 * (kx + 1) + 3 * (ky + 1) + kz + 1, source]
                    spin = [placed[3 + c, source] for c in range(3)]
                    base = [placed[c, source] for c in range(3)]
                    along_y = plus(along_y, deposit_terms(weight, base, spin, (kx, ky, kz)))
                along_z = plus(along_z, [roll(a, ky, 0) for a in along_y])
            total = plus(total, [roll(a, kz, 1) for a in along_z])
        for f in range(4):
            solid[f, n] = total[f]

    for n, target in enumerate(targets):
        g, i = target // 2, target % 2
        if n < 2:
            members = list(range(19))
        else:
            members = [m for m in range(19) if VELOCITIES[m][0] == (-1 if n == 2 else 1)]
        for t in range(2):
            tile = slice(128 * t, 128 * t + 128)
            f = [block[g].cells(member, i, t) for member in range(19)]
            done, forces = collide(f, [solid[c, n, :, tile] for c in range(4)], members)
            for c in range(3):
                share[c, n, :, tile] = forces[c]
            for m, value in done.items():
                passed[m, n, :, tile] = value
    for member in range(19):
        vector = VELOCITIES[member]
        for i in range(2):
            value = roll(passed[member, AT_LAYER[i - vector[0]]], vector[2], 1)
            value = roll(value, vector[1] - 2, 0)
            for t in range(2):
                out_pops[2 * member + i, 4 * t : 4 * t + 4, :] = value[
                    0:4, 128 * t : 128 * t + 128
                ]

    moments = [Moments() for _ in range(2)]
    for kz in (-1, 0, 1):
        across = [[roll(share[c, n], -kz, 1) for c in range(3)] for n in range(4)]
        for ky in (-1, 0, 1):
            near = [[roll(across[n][c], -ky, 0) for c in range(3)] for n in range(4)]
            for i in range(2):
                together = None
                for kx in (-1, 0, 1):
                    weight = placed[E0 + 9 * (kx + 1) + 3 * (ky + 1) + kz + 1, i]
                    forces = [weight * near[AT_LAYER[i + kx]][c] for c in range(3)]
                    together = plus(together, forces)
                    if kx:
                        moments[i].turn(0, forces, kx)
                moments[i].push(together)
                if ky:
                    moments[i].turn(1, together, ky)
                if kz:
                    moments[i].turn(2, together, kz)
    hydro = [moments[i].loads([placed[6 + c, i] for c in range(3)]) for i in range(2)]

    even = (2 * lane8) % 128
    inside = (lane8 > 0) & (lane8 < 127)
    for f in range(6):
        for s in range(2):
            value = jnp.where(masks[0][s], hydro[0][f], 0.0) + jnp.where(
                masks[1][s], hydro[1][f], 0.0
            )
            value = value + roll(value, -1, 0)
            value = value + roll(value, -1, 1)
            value = jnp.where(
                lane8 < 64, pick_lanes(value[:, :128], even), pick_lanes(value[:, 128:], even)
            )
            value = jnp.where(inside, value, 0.0)
            both = jnp.concatenate([value[2:3], value[4:5]], axis=0)
            out_loads[f, 2 * s : 2 * s + 2, :] = both


def side_kernel(groups, paired, flags, *refs):
    layers = 2 * groups
    wholes, (y_first, y_second) = refs[:groups], refs[groups : groups + 2]
    out_contact, out_edge, held = refs[groups + 2 :]
    store_ends(groups, paired, flags[0], y_first, y_second, held)
    block = [Block(wholes[g], held, g) for g in range(groups)]
    lane8, row8 = iota((8, 128), 1), iota((8, 128), 0)
    inner = lane8 % 16
    z_near = jnp.where(inner < 8, jnp.maximum(inner - 4, 0), jnp.minimum(inner + 116, 127))
    z_bin = jnp.where(inner < 8, z_near // 2, jnp.minimum(inner + 244, 255) // 2)

    def at_edge(s, field):
        rows = [pick_lanes(block[g].bins(s, field), z_bin) for g in range(groups)]
        return by_group(groups, rows, lane8)

    edge_code = cell_codes(lane8, row8)
    codes = [at_edge(s, CODE) for s in range(2)]
    for s in range(2):
        out_edge[CODE_AT + s] = codes[s]
    edge_masks = [value == edge_code for value in codes]
    for field in range(36):
        out_edge[field] = choose(edge_masks, [at_edge(s, field) for s in range(2)])
    for member in range(19):
        tiles = []
        for layer in range(layers):
            near = [block[layer // 2].cells(member, layer % 2, t) for t in range(2)]
            tiles.append(
                jnp.where(inner < 8, pick_lanes(near[0], z_near), pick_lanes(near[1], z_near))
            )
        out_edge[POPS_AT + member] = by_layer(groups, tiles, lane8)

    place, state = own_state(block[0])
    a_radius, a_speed = state[0], state[1:4]
    a_turn = [a_radius * value for value in state[4:7]]
    push, twist = None, None
    for oy in (-1, 0, 1):
        for g in range(groups):
            steps = [0] if g == 0 else []
            if g == 1:
                steps = steps + [1]
            if g == groups - 1:
                steps = steps + [-1]
            states = []
            for field in [CODE, 6, 7, 8, RADIUS, 0, 1, 2, 3, 4, 5]:
                values = []
                for s in range(2):
                    value = block[g].slot(s, field)
                    if oy < 0:
                        value = jnp.concatenate(
                            [block[g].halo_slot(0, s, field), value[0:1]], axis=0
                        )
                    if oy > 0:
                        value = jnp.concatenate(
                            [value[1:2], block[g].halo_slot(1, s, field)], axis=0
                        )
                    values.append(value)
                states.append(jnp.concatenate(values + values, axis=0))
            states = position(states[0], states[1:4]) + states[4:]
            for oz in (-1, 0, 1):
                other = [roll(value, -oz, 1) for value in states]
                keep = lane8 != (0 if oz < 0 else 127) if oz else None
                gap = [other[c] - place[c] for c in range(3)]
                gap[1], gap[2] = gap[1] + 2.0 * oy, gap[2] + 2.0 * oz
                for ox in steps:
                    apart = [gap[0] + 2.0 * ox, gap[1], gap[2]]
                    pushed, twisted = pair_force(
                        apart, a_radius, a_speed, a_turn, other[3:], keep
                    )
                    push, twist = plus(push, pushed), plus(twist, twisted)
    contact = [-value for value in push] + [-a_radius * value for value in twist]
    contact = [value + roll(value, -2, 0) for value in contact]

    for f in range(6):
        out_contact[f] = contact[f]


def edge_kernel(
    groups, paired, flags, whole, bulk_pops, bulk_loads, bulk_contact, edge, first, second, *refs
):
    final_pops, final_loads, held, out_pops, out_loads, sems = refs
    side = flags[1]
    for tile in range(Z_TILES):
        held[side, tile] = first[tile]
        value = second[tile]
        held[1 - side, tile] = roll(value, 32, 1) if paired else value
    lane, row = iota((8, 128), 1), iota((8, 128), 0)
    inner = lane % 16
    at_low = (inner == 2) | (inner == 3)
    at_high = (inner == 12) | (inner == 13)

    def value_of(field):
        q = 2 * (field % 8)
        low = roll(held[0, field // 8], 2 - q, 1)
        high = roll(held[1, field // 8], 12 - q, 1)
        return jnp.where(at_low, low, jnp.where(at_high, high, edge[field]))

    speed, spin, offset = [[value_of(3 * n + c) for c in range(3)] for n in range(3)]
    weights = [value_of(E0 + k) for k in range(27)]
    turned = cross(spin, [0.5 - value for value in offset])
    base = [speed[c] + turned[c] for c in range(3)]
    sums = None
    for kx in (-1, 0, 1):
        for kz in (-1, 0, 1):
            along = None
            for ky in (-1, 0, 1):
                weight = weights[9 * (kx + 1) + 3 * (ky + 1) + kz + 1]
                terms = deposit_terms(weight, base, spin, (kx, ky, kz))
                along = plus(along, [roll(a, ky, 0) for a in terms])
            sums = plus(sums, [roll(a, 16 * kx + kz, 1) for a in along])
    f = [value_of(POPS_AT + member) for member in range(19)]
    done, share = collide(f, sums, list(range(19)))

    lane4 = iota((4, 128), 1)
    copies = []
    for member in range(19):
        vector = VELOCITIES[member]
        value = roll(done[member], vector[1] - 2, 0)
        shift = 16 * vector[0] + vector[2]
        for i in range(2):
            for t in range(2):
                home = shift - 16 * i + (116 if t else -4)
                moved = roll(value, home, 1)[0:4]
                bulk = bulk_pops[2 * member + i, 4 * t : 4 * t + 4, :]
                mask = lane4 >= 126 if t else lane4 < 2
                out_pops[member, i, :, 128 * t : 128 * t + 128] = jnp.where(mask, moved, bulk)
        if member in PARTS:
            n = PARTS.index(member)
            part = pl.ds(PARTS[n - 1] + 1 if n else 0, member - (PARTS[n - 1] if n else -1))
            copy = pltpu.make_async_copy(out_pops.at[part], final_pops.at[part], sems.at[n])
            copy.start()
            copies.append(copy)

    moments = Moments()
    for kx in (-1, 0, 1):
        for kz in (-1, 0, 1):
            near = [roll(share[c], -16 * kx - kz, 1) for c in range(3)]
            together = None
            for ky in (-1, 0, 1):
                weight = weights[9 * (kx + 1) + 3 * (ky + 1) + kz + 1]
                forces = [weight * roll(near[c], -ky, 0) for c in range(3)]
                together = plus(together, forces)
                if ky:
                    moments.turn(1, forces, ky)
            moments.push(together)
            if kx:
                moments.turn(0, together, kx)
            if kz:
                moments.turn(2, together, kz)
    hydro = moments.loads(offset)

    place, state = own_state(Block(whole, None, 0))
    own_index = jnp.where(lane < 64, 0, 127)
    place = [pick_lanes(value, own_index) for value in place]
    state = [pick_lanes(value, own_index) for value in state]
    a_radius, a_speed = state[0], state[1:4]
    a_turn = [a_radius * value for value in state[4:7]]
    step_x, step_y = inner - 1, lane % 64 // 16 - 1
    order = lane_groups(groups)
    runs = [order.index(groups - 1), 0, 1]
    run = 32 * jnp.where(step_x < 0, runs[0], jnp.where(step_x == 0, 0, runs[2]))
    other = [None] * 10
    for end in range(2):
        tile = held[end, CONTACT_TILE]
        for oy in (-1, 0, 1):
            at = 2 * (oy + 1)
            rows = jnp.concatenate([tile[at : at + 1], tile[at + 2 : at + 3]], axis=0)
            moved = roll(rows, -16, 1)
            rows = jnp.concatenate([rows, moved, rows, moved], axis=0)
            mask = (lane // 64 == end) & (step_y == oy)
            for q in range(10):
                value = pick_lanes(rows, run + q)
                other[q] = value if other[q] is None else jnp.where(mask, value, other[q])
    keep = (step_x < 2) & (step_y < 2)
    gap = [
        other[0] - place[0] + (2 * step_x).astype(F32),
        other[1] - place[1] + (2 * step_y).astype(F32),
        other[2] - place[2] + jnp.where(lane < 64, -2.0, 2.0),
    ]
    pushed, twisted = pair_force(gap, a_radius, a_speed, a_turn, other[3:], keep)
    contact = [-value for value in pushed] + [-a_radius * value for value in twisted]
    ends = lane == 0, lane == 127
    masks = [edge[CODE_AT + s] == cell_codes(lane, row) for s in range(2)]
    for f in range(6):
        value = contact[f] + roll(contact[f], -2, 0)
        value = value + roll(value, -1, 1) + roll(value, -2, 1)
        value = value + roll(value, -16, 1) + roll(value, -32, 1)
        touch = jnp.where(ends[0], value, jnp.where(ends[1], roll(value, 63, 1), 0.0))
        for s in range(2):
            value = jnp.where(masks[s], hydro[f], 0.0)
            value = value + roll(value, -16, 1)
            value = value + roll(value, -1, 0)
            value = value + roll(value, -1, 1)
            value = jnp.where(
                ends[0], roll(value, -4, 1), jnp.where(ends[1], roll(value, 117, 1), 0.0)
            )
            both = jnp.concatenate([value[2:3], value[4:5]], axis=0)
            both = both + touch[4 * s : 4 * s + 2]
            both = both + bulk_contact[f, 4 * s : 4 * s + 2, :]
            out_loads[f, s, 0] = bulk_loads[f, 2 * s : 2 * s + 2, :] + both
    copy = pltpu.make_async_copy(out_loads, final_loads, sems.at[len(PARTS)])
    copy.start()
    for copy in copies + [copy]:
        copy.wait()


SMEM = pl.BlockSpec(memory_space=pltpu.SMEM)
PARAMS = pltpu.CompilerParams(vmem_limit_bytes=32 * 2**20)


def call(kernel, flags, operands, shapes, scratch=(), spaces=(pltpu.VMEM, pltpu.VMEM)):
    return pl.pallas_call(
        kernel,
        out_shape=[jax.ShapeDtypeStruct(shape, F32) for shape in shapes],
        in_specs=[SMEM] + [pl.BlockSpec(memory_space=spaces[0])] * len(operands),
        out_specs=[pl.BlockSpec(memory_space=spaces[1])] * len(shapes),
        scratch_shapes=[pltpu.VMEM(x, F32) if isinstance(x, tuple) else x for x in scratch],
        compiler_params=PARAMS,
    )(flags, *operands)


def step(paired, sizes, *blocks):
    nx, ny, nz = sizes
    axes = ("gx", "gy", "gz")
    groups = 2 if paired else 3

    def permute(value, target):
        pairs = []
        for x in range(nx):
            for y in range(ny):
                for z in range(nz):
                    tx, ty, tz = target(x, y, z)
                    there = ((tx % nx) * ny + ty % ny) * nz + tz % nz
                    pairs.append(((x * ny + y) * nz + z, there))
        return lax.ppermute(value, axes, pairs)

    def swap(value):
        return permute(value, lambda x, y, z: (1 - x, y, z))

    def to_low(value):
        return permute(value, lambda x, y, z: (x - 1, y, z))

    def to_high(value):
        return permute(value, lambda x, y, z: (x + 1, y, z))

    ends_y = (Y_BLOCKS, 8, 128)
    shape_z = (Z_TILES, 8, 128)
    shape_y = (groups,) + ends_y
    if paired:
        ix, iy, iz = [lax.axis_index(axis) for axis in axes]
        flags = jnp.stack([1 - (ix + iy) % 2, 1 - (ix + iz) % 2]).astype(jnp.int32)
    else:
        flags = jnp.ones((2,), jnp.int32)
    held = [pltpu.VMEM(block.shape, block.dtype) for block in blocks]
    blocks = [pltpu.with_memory_space_constraint(block, pltpu.HBM) for block in blocks]
    whole, mine, theirs = call(
        pack_kernel,
        flags,
        blocks,
        [(W_BLOCKS, 8, 128), shape_y, ends_y],
        held + [pltpu.SemaphoreType.DMA((7,))],
        (pltpu.HBM, pltpu.VMEM),
    )

    def pack_z(flags, wholes, halos):
        kernel = functools.partial(z_pack_kernel, groups, paired)
        return call(kernel, flags, wholes + halos, [shape_z], [(2,) + shape_y])[0]

    def pack_bulk(wholes, halos):
        scratch = [
            (2,) + shape_y,
            (36, 2 * groups, 8, 256),
            (4, 4, 8, 256),
            (19, 4, 8, 256),
            (3, 4, 8, 256),
        ]
        return call(
            functools.partial(bulk_kernel, groups, paired),
            flags,
            wholes + halos,
            [(W_GRAIN, 8, 128), (6, 4, 128)],
            scratch,
        )

    if paired:
        rows = mine.at[1].set(swap(theirs))
        wholes = [whole, swap(whole)]
        first = permute(rows, lambda x, y, z: (x, y + (1 if (x + y) % 2 == 0 else -1), z))
        halos = [first, swap(first)]
        first = permute(
            pack_z(flags, wholes, halos),
            lambda x, y, z: (x, y, z + (1 if (x + z) % 2 == 0 else -1)),
        )
        bulk = pack_bulk(wholes, halos)
        first, bulk = lax.optimization_barrier((first, bulk))
        ends = [first, swap(first)]
    else:
        wholes = [whole, to_low(whole), to_high(whole)]
        up, down = [jnp.stack([v, to_low(v), to_high(v)]) for v in (mine[0], theirs)]
        halos = [
            permute(down, lambda x, y, z: (x, y - 1, z)),
            permute(up, lambda x, y, z: (x, y + 1, z)),
        ]
        low = jnp.array([1, 0], jnp.int32)
        ends = [
            permute(pack_z(low, wholes, halos), lambda x, y, z: (x, y, z - 1)),
            permute(pack_z(flags, wholes, halos), lambda x, y, z: (x, y, z + 1)),
        ]
        bulk = pack_bulk(wholes, halos)
    side = call(
        functools.partial(side_kernel, groups, paired),
        flags,
        wholes + halos,
        [(6, 8, 128), (EDGE_VALUES, 8, 128)],
        [(2,) + shape_y],
    )
    populations, offset = blocks[0], blocks[2]
    shapes = [populations.shape, (6,) + offset.shape[1:]]
    return tuple(
        call(
            functools.partial(edge_kernel, groups, paired),
            flags,
            [whole] + list(bulk) + list(side) + ends,
            shapes,
            [(2,) + shape_z] + shapes + [pltpu.SemaphoreType.DMA((len(PARTS) + 1,))],
            (pltpu.VMEM, pltpu.HBM),
        )
    )


def solution(mesh, paired=None):
    sizes = tuple(mesh.shape[axis] for axis in ("gx", "gy", "gz"))
    if paired is None:
        paired = sizes[0] == 2 and sizes[1] % 2 == 0 and sizes[2] % 2 == 0
    cells, bins = P(None, "gx", "gy", "gz"), P(None, None, "gx", "gy", "gz")
    return jax.shard_map(
        functools.partial(step, paired, sizes),
        mesh=mesh,
        in_specs=(cells, cells, bins, cells, bins, bins, bins),
        out_specs=(cells, bins),
        check_vma=False,
    )
```

```python
import functools

import jax
import jax.numpy as jnp
from jax import lax
from jax.experimental import pallas as pl
from jax.experimental.pallas import tpu as pltpu
from jax.sharding import PartitionSpec as P

VELOCITIES = [
    (0, 0, 0),
    (1, 0, 0),
    (-1, 0, 0),
    (0, 1, 0),
    (0, -1, 0),
    (0, 0, 1),
    (0, 0, -1),
    (1, 1, 0),
    (-1, -1, 0),
    (1, -1, 0),
    (-1, 1, 0),
    (1, 0, 1),
    (-1, 0, -1),
    (1, 0, -1),
    (-1, 0, 1),
    (0, 1, 1),
    (0, -1, -1),
    (0, 1, -1),
    (0, -1, 1),
]
WEIGHTS = [1.0 / 3.0] + [1.0 / 18.0] * 6 + [1.0 / 36.0] * 12
relax_time = 0.8
fraction_floor = 0.1
distance_floor = 0.5

E0, RADIUS, CODE, PLACE = 9, 36, 37, 38
POPS_AT, CODE_AT, EDGE_VALUES = 36, 55, 57
Z_TILES, CONTACT_TILE = 8, 7
Y_FIELDS = list(range(9)) + [RADIUS, CODE]
Y_GRAIN, Y_BLOCKS = 76, 17
W_GRAIN, W_BLOCKS = 38, 57
F32 = jnp.float32


def end_flags(sides):
    if sides is not None:
        return sides
    ix, iy, iz = [lax.axis_index(axis) for axis in ("gx", "gy", "gz")]
    return 1 - lax.rem(ix + iy, 2), 1 - lax.rem(ix + iz, 2)


def iota(shape, dim):
    return lax.broadcasted_iota(jnp.int32, shape, dim)


def pick_lanes(values, index):
    return jnp.take_along_axis(values, index, axis=1, mode="promise_in_bounds")


def roll(values, shift, axis):
    size = values.shape[axis]
    return pltpu.roll(values, shift % size, axis) if shift % size else values


def cross(a, b):
    return [
        a[1] * b[2] - a[2] * b[1],
        a[2] * b[0] - a[0] * b[2],
        a[0] * b[1] - a[1] * b[0],
    ]


def pack_kernel(sides, *refs):
    flags = end_flags(sides)
    sources, (whole, mine, theirs), held, sems = refs[:7], refs[7:10], refs[10:17], refs[17]
    copies = [
        pltpu.make_async_copy(source, target, sems.at[n])
        for n, (source, target) in enumerate(zip(sources, held))
    ]
    for copy in copies[1:] + copies[:1]:
        copy.start()
    pops, cell, off, rad, vel, spin, inter = held
    for copy in copies[1:]:
        copy.wait()

    def slot(s, field, rows=slice(None)):
        if field < 3:
            return vel[field, s, 0, rows, :]
        if field < 6:
            return spin[field - 3, s, 0, rows, :]
        if field < 9:
            return off[field - 6, s, 0, rows, :]
        if field < RADIUS:
            return inter[field - E0, s, 0, rows, :]
        if field == RADIUS:
            return rad[s, 0, rows, :]
        return cell[s, 0, rows, :].astype(F32)

    for field in range(38):
        for s in range(2):
            at = 4 * (field % 2) + 2 * s
            whole[W_GRAIN + field // 2, at : at + 2, :] = slot(s, field)
    for out, end in ((mine.at[0], flags[0]), (theirs, 1 - flags[0])):
        for s in range(2):
            for f in range(29):
                if f < 11:
                    value = slot(s, Y_FIELDS[f], pl.ds(end, 1))
                else:
                    kx, q, kz = (f - 11) // 6, (f - 11) // 3 % 2, (f - 11) % 3
                    value = inter[9 * kx + 3 * (q + end) + kz, s, 0, pl.ds(end, 1), :]
                r = Y_GRAIN + 2 * f + s
                out[r // 8, r % 8 : r % 8 + 1, :] = value
        out[16, 6:8, :] = jnp.zeros((2, 128), F32)
    copies[0].wait()
    for out, end in ((mine.at[0], flags[0]), (theirs, 1 - flags[0])):
        for member in range(19):
            for i in range(2):
                row = pops[member, i, pl.ds(3 * end, 1), :]
                for t in range(2):
                    r = 4 * member + 2 * i + t
                    out[r // 8, r % 8 : r % 8 + 1, :] = row[:, 128 * t : 128 * t + 128]
    for member in range(19):
        for i in range(2):
            for t in range(2):
                tile = pops[member, i, :, 128 * t : 128 * t + 128]
                whole[2 * member + i, 4 * t : 4 * t + 4, :] = tile


class Block:
    def __init__(self, whole, halos, group):
        self.whole, self.halos, self.group = whole, halos, group

    def slot(self, s, field):
        at = 4 * (field % 2) + 2 * s
        return self.whole[W_GRAIN + field // 2, at : at + 2, :]

    def pops(self, member, i, t):
        return self.whole[2 * member + i, 4 * t : 4 * t + 4, :]

    def halo_pops(self, end, member, i, t):
        r = 4 * member + 2 * i + t
        return self.halos[end, self.group, r // 8, r % 8 : r % 8 + 1, :]

    def halo_slot(self, end, s, field):
        if field in Y_FIELDS:
            f = Y_FIELDS.index(field)
        else:
            k = field - E0
            q = k // 3 % 3 - (1 - end)
            if q not in (0, 1):
                return jnp.zeros((1, 128), F32)
            f = 11 + 6 * (k // 9) + 3 * q + k % 3
        r = Y_GRAIN + 2 * f + s
        return self.halos[end, self.group, r // 8, r % 8 : r % 8 + 1, :]

    def bins(self, s, field):
        row = iota((8, 128), 0)
        n, at = W_GRAIN + field // 2, 4 * (field % 2) + 2 * s
        rows = [
            self.halo_slot(0, s, field),
            self.whole[n, at : at + 1, :],
            self.whole[n, at + 1 : at + 2, :],
            self.halo_slot(1, s, field),
        ]
        rows = [jnp.broadcast_to(value, (8, 128)) for value in rows]
        return jnp.where(
            row < 4,
            jnp.where(row < 2, rows[0], rows[1]),
            jnp.where(row < 6, rows[2], rows[3]),
        )

    def cells(self, member, i, t):
        row = iota((8, 128), 0)
        own = self.whole[2 * member + i]
        if isinstance(t, int):
            own = roll(own, 2 - 4 * t, 0)
            low, high = [self.halo_pops(end, member, i, t) for end in range(2)]
        else:
            own = jnp.where(t, roll(own, -2, 0), roll(own, 2, 0))
            low, high = [
                jnp.where(
                    t, self.halo_pops(end, member, i, 1), self.halo_pops(end, member, i, 0)
                )
                for end in range(2)
            ]
        low, high = jnp.broadcast_to(low, (8, 128)), jnp.broadcast_to(high, (8, 128))
        return jnp.where(row < 2, low, jnp.where(row > 5, high, own))


def position(code, offset):
    first = jnp.floor(code * 0.25)
    rest = code - 4.0 * first
    second = jnp.floor(rest * 0.5)
    corner = [first, second, rest - 2.0 * second]
    return [corner[c] + offset[c] for c in range(3)]


def store_ends(groups, paired, side, first, second, held):
    for g in range(groups):
        held[side, g] = first[g]
        held[1 - side, g] = second[(g + 1) % 2 if paired else g]


def lane_groups(groups):
    return [0, 1, 0, 1] if groups == 2 else [0, 1, 1, 2]


def by_group(groups, values, lane):
    order = lane_groups(groups)
    result = values[order[3]]
    for q in (2, 1, 0):
        if order[q] != order[q + 1] or q < 2:
            result = jnp.where(lane < 32 * (q + 1), values[order[q]], result)
    return result


def by_layer(groups, values, lane):
    odd = lane // 16 % 2 == 1
    pairs = [jnp.where(odd, values[2 * g + 1], values[2 * g]) for g in range(groups)]
    return by_group(groups, pairs, lane)


def cell_codes(lane, row):
    return (4 * (lane // 16 % 2) + 2 * (row % 2) + lane % 2).astype(F32)


def choose(masks, values):
    return jnp.where(masks[0], values[0], jnp.where(masks[1], values[1], 0.0))


def z_pack_kernel(groups, paired, sides, *refs):
    flags = end_flags(sides)
    wholes, (first, second, out, held) = refs[:groups], refs[groups:]
    store_ends(groups, paired, flags[0], first, second, held)
    high = flags[1] == 1
    lane, row = iota((8, 128), 1), iota((8, 128), 0)
    block = [Block(wholes[g], held, g) for g in range(groups)]
    start = jnp.where(high, 127, 0)
    index = jnp.full((8, 128), start, jnp.int32)
    pops_index = jnp.full((8, 128), jnp.where(high, 126, 0), jnp.int32) + lane % 2
    inner = lane % 16 // 2

    def picked(s, field):
        values = [pick_lanes(block[g].bins(s, field), index) for g in range(groups)]
        return by_group(groups, values, lane)

    slots = [[picked(s, field) for field in range(38)] for s in range(2)]
    code = cell_codes(lane, row)
    masks = [slots[s][CODE] == code for s in range(2)]
    values = [choose(masks, [slots[0][f], slots[1][f]]) for f in range(36)]
    for member in range(19):
        tiles = []
        for layer in range(2 * groups):
            g, i = layer // 2, layer % 2
            tile = block[g].cells(member, i, high)
            tiles.append(pick_lanes(tile, pops_index))
        values.append(by_layer(groups, tiles, lane))
    for tile in range(CONTACT_TILE):
        packed = values[8 * tile]
        for q in range(1, 8):
            if 8 * tile + q < len(values):
                packed = jnp.where(inner == q, values[8 * tile + q], packed)
        out[tile] = packed
    packed = jnp.zeros((8, 128), F32)
    for s in range(2):
        state = position(slots[s][CODE], slots[s][6:9]) + [slots[s][RADIUS]] + slots[s][0:6]
        for q, value in enumerate(state):
            packed = jnp.where(lane % 32 == 16 * s + q, value, packed)
    out[CONTACT_TILE] = packed


def dot_lattice(vector, velocity):
    total = None
    for c in range(3):
        if vector[c]:
            if total is None:
                total = velocity[c] if vector[c] > 0 else -velocity[c]
            else:
                total = total + velocity[c] if vector[c] > 0 else total - velocity[c]
    return total


def equilibrium_base(velocity):
    return 1.0 - 1.5 * (
        velocity[0] * velocity[0] + velocity[1] * velocity[1] + velocity[2] * velocity[2]
    )


def collide(f, sums, members):
    fraction = 1.0 - jnp.exp(-sums[0])
    excess = relax_time - 0.5
    weight = fraction * excess / (1.0 - fraction + excess)
    inverse = 1.0 / jnp.maximum(sums[0], fraction_floor)
    solid_velocity = [sums[1 + c] * inverse for c in range(3)]
    density = sum(f[1:], f[0])
    momentum = []
    for c in range(3):
        plus = [f[m] for m in range(19) if VELOCITIES[m][c] > 0]
        minus = [f[m] for m in range(19) if VELOCITIES[m][c] < 0]
        momentum.append(sum(plus[1:], plus[0]) - sum(minus[1:], minus[0]))
    per_density = 1.0 / density
    fluid_velocity = [momentum[c] * per_density for c in range(3)]
    share = [weight * inverse * (momentum[c] - density * solid_velocity[c]) for c in range(3)]
    relax = (1.0 - weight) * (1.0 / relax_time)
    keep = 1.0 - relax
    fluid_base = equilibrium_base(fluid_velocity)
    solid_base = equilibrium_base(solid_velocity)
    done = {}
    for member in [0] + list(range(1, 19, 2)):
        reverse = member + 1 if member else 0
        if member not in members and reverse not in members:
            continue
        part = WEIGHTS[member] * density
        if member == 0:
            fluid = [part * fluid_base] * 2
            settled = [part * solid_base] * 2
        else:
            ends = []
            for base, velocity in (
                (fluid_base, fluid_velocity),
                (solid_base, solid_velocity),
            ):
                along = dot_lattice(VELOCITIES[member], velocity)
                even = base + 4.5 * along * along
                odd = 3.0 * along
                ends.append([part * (even + odd), part * (even - odd)])
            fluid, settled = ends
        pair = [f[member], f[reverse]]
        for way, m in enumerate((member, reverse)[: 2 if member else 1]):
            if m in members:
                exchange = (pair[1 - way] - fluid[1 - way]) - (pair[way] - settled[way])
                done[m] = keep * pair[way] + relax * fluid[way] + weight * exchange
    return done, share


def deposit_terms(weight, base, spin, k):
    terms = [weight]
    for c in range(3):
        u, v = (c + 1) % 3, (c + 2) % 3
        speed = base[c]
        if k[v]:
            speed = speed + spin[u] if k[v] > 0 else speed - spin[u]
        if k[u]:
            speed = speed - spin[v] if k[u] > 0 else speed + spin[v]
        terms.append(weight * speed)
    return terms


def plus(totals, terms):
    return list(terms) if totals is None else [a + b for a, b in zip(totals, terms)]


class Moments:
    def __init__(self):
        self.force, self.moment = [None] * 3, [None] * 3

    def add(self, store, c, value, sign):
        if store[c] is None:
            store[c] = value if sign > 0 else -value
        else:
            store[c] = store[c] + value if sign > 0 else store[c] - value

    def turn(self, axis, forces, sign):
        u, v = (axis + 1) % 3, (axis + 2) % 3
        self.add(self.moment, v, forces[u], sign)
        self.add(self.moment, u, forces[v], -sign)

    def push(self, forces):
        for c in range(3):
            self.add(self.force, c, forces[c], 1)

    def loads(self, offset):
        turned = cross([0.5 - value for value in offset], self.force)
        return self.force + [self.moment[c] + turned[c] for c in range(3)]


def pair_force(gap, a_radius, a_speed, a_turn, other, keep=None):
    b_radius = other[0]
    distance = jnp.sqrt(gap[0] * gap[0] + gap[1] * gap[1] + gap[2] * gap[2])
    scale = 1.0 / jnp.maximum(distance, distance_floor)
    normal = [gap[c] * scale for c in range(3)]
    depth = jnp.maximum(a_radius + b_radius - distance, 0.0)
    strength = a_radius * b_radius * depth
    if keep is not None:
        strength = jnp.where(keep, strength, 0.0)
    turning = [a_turn[c] + b_radius * other[4 + c] for c in range(3)]
    swing = cross(turning, normal)
    relative = [a_speed[c] - other[1 + c] + swing[c] for c in range(3)]
    along = relative[0] * normal[0] + relative[1] * normal[1] + relative[2] * normal[2]
    factor = 1.0 + along
    pushed = [strength * (factor * normal[c] + relative[c]) for c in range(3)]
    return pushed, cross(normal, pushed)


def own_state(block):
    def rows(field):
        values = [block.slot(s, field) for s in range(2)]
        return jnp.concatenate([values[0], values[0], values[1], values[1]], axis=0)

    place = position(rows(CODE), [rows(6 + c) for c in range(3)])
    return place, [rows(RADIUS)] + [rows(c) for c in range(6)]


PARTS = [4, 9, 14, 18]
AT_LAYER = {0: 0, 1: 1, 2: 2, -1: 3}


def bulk_kernel(groups, paired, sides, *refs):
    flags = end_flags(sides)
    layers = 2 * groups
    wholes, (y_first, y_second) = refs[:groups], refs[groups : groups + 2]
    out_pops, out_loads = refs[groups + 2 : groups + 4]
    held, placed, solid, passed, share = refs[groups + 4 :]
    targets = [0, 1, 2, layers - 1]
    store_ends(groups, paired, flags[0], y_first, y_second, held)
    block = [Block(wholes[g], held, g) for g in range(groups)]
    lane8 = iota((8, 128), 1)
    half = lane8 // 2

    def spread(rows):
        return jnp.concatenate([pick_lanes(rows, half), pick_lanes(rows, half + 64)], axis=1)

    cell_code = (2 * (iota((8, 256), 0) % 2) + iota((8, 256), 1) % 2).astype(F32)
    masks = []
    codes = [[block[g].bins(s, CODE) for g in range(groups)] for s in range(2)]
    for g in range(groups):
        wide = [spread(codes[s][g]) for s in range(2)]
        for i in range(2):
            masks.append([wide[s] == cell_code + 4.0 * i for s in range(2)])
    for field in range(36):
        rows = [[block[g].bins(s, field) for g in range(groups)] for s in range(2)]
        for g in range(groups):
            values = [spread(rows[s][g]) for s in range(2)]
            for i in range(2):
                placed[field, 2 * g + i] = choose(masks[2 * g + i], values)
    for layer in range(layers):
        spin = [placed[3 + c, layer] for c in range(3)]
        turned = cross(spin, [0.5 - placed[6 + c, layer] for c in range(3)])
        for c in range(3):
            placed[c, layer] = placed[c, layer] + turned[c]

    for n, target in enumerate(targets):
        total = None
        for kz in (-1, 0, 1):
            along_z = None
            for ky in (-1, 0, 1):
                along_y = None
                for kx in (-1, 0, 1):
                    source = (target - kx) % layers
                    weight = placed[E0 + 9 * (kx + 1) + 3 * (ky + 1) + kz + 1, source]
                    spin = [placed[3 + c, source] for c in range(3)]
                    base = [placed[c, source] for c in range(3)]
                    along_y = plus(along_y, deposit_terms(weight, base, spin, (kx, ky, kz)))
                along_z = plus(along_z, [roll(a, ky, 0) for a in along_y])
            total = plus(total, [roll(a, kz, 1) for a in along_z])
        for f in range(4):
            solid[f, n] = total[f]

    for n, target in enumerate(targets):
        g, i = target // 2, target % 2
        if n < 2:
            members = list(range(19))
        else:
            members = [m for m in range(19) if VELOCITIES[m][0] == (-1 if n == 2 else 1)]
        for t in range(2):
            tile = slice(128 * t, 128 * t + 128)
            f = [block[g].cells(member, i, t) for member in range(19)]
            done, forces = collide(f, [solid[c, n, :, tile] for c in range(4)], members)
            for c in range(3):
                share[c, n, :, tile] = forces[c]
            for m, value in done.items():
                passed[m, n, :, tile] = value
    for member in range(19):
        vector = VELOCITIES[member]
        for i in range(2):
            value = roll(passed[member, AT_LAYER[i - vector[0]]], vector[2], 1)
            value = roll(value, vector[1] - 2, 0)
            for t in range(2):
                out_pops[2 * member + i, 4 * t : 4 * t + 4, :] = value[
                    0:4, 128 * t : 128 * t + 128
                ]

    moments = [Moments() for _ in range(2)]
    for kz in (-1, 0, 1):
        across = [[roll(share[c, n], -kz, 1) for c in range(3)] for n in range(4)]
        for ky in (-1, 0, 1):
            near = [[roll(across[n][c], -ky, 0) for c in range(3)] for n in range(4)]
            for i in range(2):
                together = None
                for kx in (-1, 0, 1):
                    weight = placed[E0 + 9 * (kx + 1) + 3 * (ky + 1) + kz + 1, i]
                    forces = [weight * near[AT_LAYER[i + kx]][c] for c in range(3)]
                    together = plus(together, forces)
                    if kx:
                        moments[i].turn(0, forces, kx)
                moments[i].push(together)
                if ky:
                    moments[i].turn(1, together, ky)
                if kz:
                    moments[i].turn(2, together, kz)
    hydro = [moments[i].loads([placed[6 + c, i] for c in range(3)]) for i in range(2)]

    even = (2 * lane8) % 128
    inside = (lane8 > 0) & (lane8 < 127)
    for f in range(6):
        for s in range(2):
            value = jnp.where(masks[0][s], hydro[0][f], 0.0) + jnp.where(
                masks[1][s], hydro[1][f], 0.0
            )
            value = value + roll(value, -1, 0)
            value = value + roll(value, -1, 1)
            value = jnp.where(
                lane8 < 64, pick_lanes(value[:, :128], even), pick_lanes(value[:, 128:], even)
            )
            value = jnp.where(inside, value, 0.0)
            both = jnp.concatenate([value[2:3], value[4:5]], axis=0)
            out_loads[f, 2 * s : 2 * s + 2, :] = both


def side_kernel(groups, paired, sides, *refs):
    flags = end_flags(sides)
    layers = 2 * groups
    wholes, (y_first, y_second) = refs[:groups], refs[groups : groups + 2]
    out_contact, out_edge, held = refs[groups + 2 :]
    store_ends(groups, paired, flags[0], y_first, y_second, held)
    block = [Block(wholes[g], held, g) for g in range(groups)]
    lane8, row8 = iota((8, 128), 1), iota((8, 128), 0)
    inner = lane8 % 16
    z_near = jnp.where(inner < 8, jnp.maximum(inner - 4, 0), jnp.minimum(inner + 116, 127))
    z_bin = jnp.where(inner < 8, z_near // 2, jnp.minimum(inner + 244, 255) // 2)

    def at_edge(s, field):
        rows = [pick_lanes(block[g].bins(s, field), z_bin) for g in range(groups)]
        return by_group(groups, rows, lane8)

    edge_code = cell_codes(lane8, row8)
    codes = [at_edge(s, CODE) for s in range(2)]
    for s in range(2):
        out_edge[CODE_AT + s] = codes[s]
    edge_masks = [value == edge_code for value in codes]
    for field in range(36):
        out_edge[field] = choose(edge_masks, [at_edge(s, field) for s in range(2)])
    for member in range(19):
        tiles = []
        for layer in range(layers):
            near = [block[layer // 2].cells(member, layer % 2, t) for t in range(2)]
            tiles.append(
                jnp.where(inner < 8, pick_lanes(near[0], z_near), pick_lanes(near[1], z_near))
            )
        out_edge[POPS_AT + member] = by_layer(groups, tiles, lane8)

    place, state = own_state(block[0])
    a_radius, a_speed = state[0], state[1:4]
    a_turn = [a_radius * value for value in state[4:7]]
    push, twist = None, None
    for oy in (-1, 0, 1):
        for g in range(groups):
            steps = [0] if g == 0 else []
            if g == 1:
                steps = steps + [1]
            if g == groups - 1:
                steps = steps + [-1]
            states = []
            for field in [CODE, 6, 7, 8, RADIUS, 0, 1, 2, 3, 4, 5]:
                values = []
                for s in range(2):
                    value = block[g].slot(s, field)
                    if oy < 0:
                        value = jnp.concatenate(
                            [block[g].halo_slot(0, s, field), value[0:1]], axis=0
                        )
                    if oy > 0:
                        value = jnp.concatenate(
                            [value[1:2], block[g].halo_slot(1, s, field)], axis=0
                        )
                    values.append(value)
                states.append(jnp.concatenate(values + values, axis=0))
            states = position(states[0], states[1:4]) + states[4:]
            for oz in (-1, 0, 1):
                other = [roll(value, -oz, 1) for value in states]
                keep = lane8 != (0 if oz < 0 else 127) if oz else None
                gap = [other[c] - place[c] for c in range(3)]
                gap[1], gap[2] = gap[1] + 2.0 * oy, gap[2] + 2.0 * oz
                for ox in steps:
                    apart = [gap[0] + 2.0 * ox, gap[1], gap[2]]
                    pushed, twisted = pair_force(
                        apart, a_radius, a_speed, a_turn, other[3:], keep
                    )
                    push, twist = plus(push, pushed), plus(twist, twisted)
    contact = [-value for value in push] + [-a_radius * value for value in twist]
    contact = [value + roll(value, -2, 0) for value in contact]

    for f in range(6):
        out_contact[f] = contact[f]


def edge_kernel(
    groups, paired, sides, whole, bulk_pops, bulk_loads, bulk_contact, edge, first, second, *refs
):
    final_pops, final_loads, held, out_pops, out_loads, sems = refs
    side = end_flags(sides)[1]
    for tile in range(Z_TILES):
        held[side, tile] = first[tile]
        value = second[tile]
        held[1 - side, tile] = roll(value, 32, 1) if paired else value
    lane, row = iota((8, 128), 1), iota((8, 128), 0)
    inner = lane % 16
    at_low = (inner == 2) | (inner == 3)
    at_high = (inner == 12) | (inner == 13)

    def value_of(field):
        q = 2 * (field % 8)
        low = roll(held[0, field // 8], 2 - q, 1)
        high = roll(held[1, field // 8], 12 - q, 1)
        return jnp.where(at_low, low, jnp.where(at_high, high, edge[field]))

    speed, spin, offset = [[value_of(3 * n + c) for c in range(3)] for n in range(3)]
    weights = [value_of(E0 + k) for k in range(27)]
    turned = cross(spin, [0.5 - value for value in offset])
    base = [speed[c] + turned[c] for c in range(3)]
    sums = None
    for kx in (-1, 0, 1):
        for kz in (-1, 0, 1):
            along = None
            for ky in (-1, 0, 1):
                weight = weights[9 * (kx + 1) + 3 * (ky + 1) + kz + 1]
                terms = deposit_terms(weight, base, spin, (kx, ky, kz))
                along = plus(along, [roll(a, ky, 0) for a in terms])
            sums = plus(sums, [roll(a, 16 * kx + kz, 1) for a in along])
    f = [value_of(POPS_AT + member) for member in range(19)]
    done, share = collide(f, sums, list(range(19)))

    lane4 = iota((4, 128), 1)
    copies = []
    for member in range(19):
        vector = VELOCITIES[member]
        value = roll(done[member], vector[1] - 2, 0)
        shift = 16 * vector[0] + vector[2]
        for i in range(2):
            for t in range(2):
                home = shift - 16 * i + (116 if t else -4)
                moved = roll(value, home, 1)[0:4]
                bulk = bulk_pops[2 * member + i, 4 * t : 4 * t + 4, :]
                mask = lane4 >= 126 if t else lane4 < 2
                out_pops[member, i, :, 128 * t : 128 * t + 128] = jnp.where(mask, moved, bulk)
        if member in PARTS:
            n = PARTS.index(member)
            part = pl.ds(PARTS[n - 1] + 1 if n else 0, member - (PARTS[n - 1] if n else -1))
            copy = pltpu.make_async_copy(out_pops.at[part], final_pops.at[part], sems.at[n])
            copy.start()
            copies.append(copy)

    moments = Moments()
    for kx in (-1, 0, 1):
        for kz in (-1, 0, 1):
            near = [roll(share[c], -16 * kx - kz, 1) for c in range(3)]
            together = None
            for ky in (-1, 0, 1):
                weight = weights[9 * (kx + 1) + 3 * (ky + 1) + kz + 1]
                forces = [weight * roll(near[c], -ky, 0) for c in range(3)]
                together = plus(together, forces)
                if ky:
                    moments.turn(1, forces, ky)
            moments.push(together)
            if kx:
                moments.turn(0, together, kx)
            if kz:
                moments.turn(2, together, kz)
    hydro = moments.loads(offset)

    place, state = own_state(Block(whole, None, 0))
    own_index = jnp.where(lane < 64, 0, 127)
    place = [pick_lanes(value, own_index) for value in place]
    state = [pick_lanes(value, own_index) for value in state]
    a_radius, a_speed = state[0], state[1:4]
    a_turn = [a_radius * value for value in state[4:7]]
    step_x, step_y = inner - 1, lane % 64 // 16 - 1
    order = lane_groups(groups)
    runs = [order.index(groups - 1), 0, 1]
    run = 32 * jnp.where(step_x < 0, runs[0], jnp.where(step_x == 0, 0, runs[2]))
    other = [None] * 10
    for end in range(2):
        tile = held[end, CONTACT_TILE]
        for oy in (-1, 0, 1):
            at = 2 * (oy + 1)
            rows = jnp.concatenate([tile[at : at + 1], tile[at + 2 : at + 3]], axis=0)
            moved = roll(rows, -16, 1)
            rows = jnp.concatenate([rows, moved, rows, moved], axis=0)
            mask = (lane // 64 == end) & (step_y == oy)
            for q in range(10):
                value = pick_lanes(rows, run + q)
                other[q] = value if other[q] is None else jnp.where(mask, value, other[q])
    keep = (step_x < 2) & (step_y < 2)
    gap = [
        other[0] - place[0] + (2 * step_x).astype(F32),
        other[1] - place[1] + (2 * step_y).astype(F32),
        other[2] - place[2] + jnp.where(lane < 64, -2.0, 2.0),
    ]
    pushed, twisted = pair_force(gap, a_radius, a_speed, a_turn, other[3:], keep)
    contact = [-value for value in pushed] + [-a_radius * value for value in twisted]
    ends = lane == 0, lane == 127
    masks = [edge[CODE_AT + s] == cell_codes(lane, row) for s in range(2)]
    for f in range(6):
        value = contact[f] + roll(contact[f], -2, 0)
        value = value + roll(value, -1, 1) + roll(value, -2, 1)
        value = value + roll(value, -16, 1) + roll(value, -32, 1)
        touch = jnp.where(ends[0], value, jnp.where(ends[1], roll(value, 63, 1), 0.0))
        for s in range(2):
            value = jnp.where(masks[s], hydro[f], 0.0)
            value = value + roll(value, -16, 1)
            value = value + roll(value, -1, 0)
            value = value + roll(value, -1, 1)
            value = jnp.where(
                ends[0], roll(value, -4, 1), jnp.where(ends[1], roll(value, 117, 1), 0.0)
            )
            both = jnp.concatenate([value[2:3], value[4:5]], axis=0)
            both = both + touch[4 * s : 4 * s + 2]
            both = both + bulk_contact[f, 4 * s : 4 * s + 2, :]
            out_loads[f, s, 0] = bulk_loads[f, 2 * s : 2 * s + 2, :] + both
    copy = pltpu.make_async_copy(out_loads, final_loads, sems.at[len(PARTS)])
    copy.start()
    for copy in copies + [copy]:
        copy.wait()


PARAMS = pltpu.CompilerParams(vmem_limit_bytes=32 * 2**20)


def call(kernel, operands, shapes, scratch=(), spaces=(pltpu.VMEM, pltpu.VMEM)):
    return pl.pallas_call(
        kernel,
        out_shape=[jax.ShapeDtypeStruct(shape, F32) for shape in shapes],
        in_specs=[pl.BlockSpec(memory_space=spaces[0])] * len(operands),
        out_specs=[pl.BlockSpec(memory_space=spaces[1])] * len(shapes),
        scratch_shapes=[pltpu.VMEM(x, F32) if isinstance(x, tuple) else x for x in scratch],
        compiler_params=PARAMS,
    )(*operands)


def step(paired, sizes, *blocks):
    nx, ny, nz = sizes
    axes = ("gx", "gy", "gz")
    groups = 2 if paired else 3

    def permute(value, target):
        pairs = []
        for x in range(nx):
            for y in range(ny):
                for z in range(nz):
                    tx, ty, tz = target(x, y, z)
                    there = ((tx % nx) * ny + ty % ny) * nz + tz % nz
                    pairs.append(((x * ny + y) * nz + z, there))
        return lax.ppermute(value, axes, pairs)

    def swap(value):
        return permute(value, lambda x, y, z: (1 - x, y, z))

    def to_low(value):
        return permute(value, lambda x, y, z: (x - 1, y, z))

    def to_high(value):
        return permute(value, lambda x, y, z: (x + 1, y, z))

    ends_y = (Y_BLOCKS, 8, 128)
    shape_z = (Z_TILES, 8, 128)
    shape_y = (groups,) + ends_y
    sides = None if paired else (1, 1)
    held = [pltpu.VMEM(block.shape, block.dtype) for block in blocks]
    blocks = [pltpu.with_memory_space_constraint(block, pltpu.HBM) for block in blocks]
    whole, mine, theirs = call(
        functools.partial(pack_kernel, sides),
        blocks,
        [(W_BLOCKS, 8, 128), shape_y, ends_y],
        held + [pltpu.SemaphoreType.DMA((7,))],
        (pltpu.HBM, pltpu.VMEM),
    )

    def pack_z(sides, wholes, halos):
        kernel = functools.partial(z_pack_kernel, groups, paired, sides)
        return call(kernel, wholes + halos, [shape_z], [(2,) + shape_y])[0]

    def pack_bulk(wholes, halos):
        scratch = [
            (2,) + shape_y,
            (36, 2 * groups, 8, 256),
            (4, 4, 8, 256),
            (19, 4, 8, 256),
            (3, 4, 8, 256),
        ]
        return call(
            functools.partial(bulk_kernel, groups, paired, sides),
            wholes + halos,
            [(W_GRAIN, 8, 128), (6, 4, 128)],
            scratch,
        )

    if paired:
        rows = mine.at[1].set(swap(theirs))
        wholes = [whole, swap(whole)]
        first = permute(rows, lambda x, y, z: (x, y + (1 if (x + y) % 2 == 0 else -1), z))
        halos = [first, swap(first)]
        first = permute(
            pack_z(sides, wholes, halos),
            lambda x, y, z: (x, y, z + (1 if (x + z) % 2 == 0 else -1)),
        )
        bulk = pack_bulk(wholes, halos)
        first, bulk = lax.optimization_barrier((first, bulk))
        ends = [first, swap(first)]
    else:
        wholes = [whole, to_low(whole), to_high(whole)]
        up, down = [jnp.stack([v, to_low(v), to_high(v)]) for v in (mine[0], theirs)]
        halos = [
            permute(down, lambda x, y, z: (x, y - 1, z)),
            permute(up, lambda x, y, z: (x, y + 1, z)),
        ]
        low = (1, 0)
        ends = [
            permute(pack_z(low, wholes, halos), lambda x, y, z: (x, y, z - 1)),
            permute(pack_z(sides, wholes, halos), lambda x, y, z: (x, y, z + 1)),
        ]
        bulk = pack_bulk(wholes, halos)
    side = call(
        functools.partial(side_kernel, groups, paired, sides),
        wholes + halos,
        [(6, 8, 128), (EDGE_VALUES, 8, 128)],
        [(2,) + shape_y],
    )
    populations, offset = blocks[0], blocks[2]
    shapes = [populations.shape, (6,) + offset.shape[1:]]
    return tuple(
        call(
            functools.partial(edge_kernel, groups, paired, sides),
            [whole] + list(bulk) + list(side) + ends,
            shapes,
            [(2,) + shape_z] + shapes + [pltpu.SemaphoreType.DMA((len(PARTS) + 1,))],
            (pltpu.VMEM, pltpu.HBM),
        )
    )


def solution(mesh, paired=None):
    sizes = tuple(mesh.shape[axis] for axis in ("gx", "gy", "gz"))
    if paired is None:
        paired = sizes[0] == 2 and sizes[1] % 2 == 0 and sizes[2] % 2 == 0
    cells, bins = P(None, "gx", "gy", "gz"), P(None, None, "gx", "gy", "gz")
    return jax.shard_map(
        functools.partial(step, paired, sizes),
        mesh=mesh,
        in_specs=(cells, cells, bins, cells, bins, bins, bins),
        out_specs=(cells, bins),
        check_vma=False,
    )
```

```python
import functools

import jax
import jax.numpy as jnp
from jax import lax
from jax.experimental import pallas as pl
from jax.experimental.pallas import tpu as pltpu
from jax.sharding import PartitionSpec as P

VELOCITIES = [
    (0, 0, 0),
    (1, 0, 0),
    (-1, 0, 0),
    (0, 1, 0),
    (0, -1, 0),
    (0, 0, 1),
    (0, 0, -1),
    (1, 1, 0),
    (-1, -1, 0),
    (1, -1, 0),
    (-1, 1, 0),
    (1, 0, 1),
    (-1, 0, -1),
    (1, 0, -1),
    (-1, 0, 1),
    (0, 1, 1),
    (0, -1, -1),
    (0, 1, -1),
    (0, -1, 1),
]
WEIGHTS = [1.0 / 3.0] + [1.0 / 18.0] * 6 + [1.0 / 36.0] * 12
relax_time = 0.8
fraction_floor = 0.1
distance_floor = 0.5

E0, RADIUS, CODE, PLACE = 9, 36, 37, 38
POPS_AT, CODE_AT, EDGE_VALUES = 36, 55, 57
Z_TILES, CONTACT_TILE = 8, 7
Y_FIELDS = list(range(9)) + [RADIUS, CODE]
Y_MEMBERS = [m for m in range(19) if VELOCITIES[m][1]] + [19, 20, 21]
Y_STANDS = {0: 10, 1: 11, 5: 12}
Y_GRAIN, Y_BLOCKS = 52, 14
W_GRAIN, W_BLOCKS = 38, 57
F32 = jnp.float32


def end_flags(sides):
    if sides is not None:
        return sides
    ix, iy, iz = [lax.axis_index(axis) for axis in ("gx", "gy", "gz")]
    return 1 - lax.rem(ix + iy, 2), 1 - lax.rem(ix + iz, 2)


def iota(shape, dim):
    return lax.broadcasted_iota(jnp.int32, shape, dim)


def pick_lanes(values, index):
    return jnp.take_along_axis(values, index, axis=1, mode="promise_in_bounds")


def roll(values, shift, axis):
    size = values.shape[axis]
    return pltpu.roll(values, shift % size, axis) if shift % size else values


def cross(a, b):
    return [
        a[1] * b[2] - a[2] * b[1],
        a[2] * b[0] - a[0] * b[2],
        a[0] * b[1] - a[1] * b[0],
    ]


def pack_kernel(sides, *refs):
    flags = end_flags(sides)
    sources, (whole, mine, theirs), held, sems = refs[:7], refs[7:10], refs[10:17], refs[17]
    copies = [
        pltpu.make_async_copy(source, target, sems.at[n])
        for n, (source, target) in enumerate(zip(sources[1:], held[1:]))
    ]
    for n, part in enumerate(POPS_PARTS):
        part = pl.ds(*part)
        copies.append(pltpu.make_async_copy(sources[0].at[part], held[0].at[part], sems.at[6 + n]))
    for copy in copies:
        copy.start()
    pops, cell, off, rad, vel, spin, inter = held
    for copy in copies[:6]:
        copy.wait()

    def slot(s, field, rows=slice(None)):
        if field < 3:
            return vel[field, s, 0, rows, :]
        if field < 6:
            return spin[field - 3, s, 0, rows, :]
        if field < 9:
            return off[field - 6, s, 0, rows, :]
        if field < RADIUS:
            return inter[field - E0, s, 0, rows, :]
        if field == RADIUS:
            return rad[s, 0, rows, :]
        return cell[s, 0, rows, :].astype(F32)

    for field in range(38):
        for s in range(2):
            at = 4 * (field % 2) + 2 * s
            whole[W_GRAIN + field // 2, at : at + 2, :] = slot(s, field)
    for out, end in ((mine.at[0], flags[0]), (theirs, 1 - flags[0])):
        for s in range(2):
            for f in range(29):
                if f < 11:
                    value = slot(s, Y_FIELDS[f], pl.ds(end, 1))
                else:
                    kx, q, kz = (f - 11) // 6, (f - 11) // 3 % 2, (f - 11) % 3
                    value = inter[9 * kx + 3 * (q + end) + kz, s, 0, pl.ds(end, 1), :]
                r = Y_GRAIN + 2 * f + s
                out[r // 8, r % 8 : r % 8 + 1, :] = value
        out[Y_BLOCKS - 1, 6:8, :] = jnp.zeros((2, 128), F32)
    for copy in copies[6:]:
        copy.wait()
    still = [m for m in range(19) if not VELOCITIES[m][1]]
    for i in range(2):
        sums = []
        for c in (0, 2):
            rising = [pops[m, i] for m in still if VELOCITIES[m][c] > 0]
            falling = [pops[m, i] for m in still if VELOCITIES[m][c] < 0]
            sums.append(sum(rising[1:], rising[0]) - sum(falling[1:], falling[0]))
        total = sum([pops[m, i] for m in still[1:]], pops[0, i])
        pops[19, i] = total - sums[0] - sums[1]
        pops[20, i] = sums[0]
        pops[21, i] = sums[1]
    for out, end in ((mine.at[0], flags[0]), (theirs, 1 - flags[0])):
        for n, member in enumerate(Y_MEMBERS):
            for i in range(2):
                row = pops[member, i, pl.ds(3 * end, 1), :]
                for t in range(2):
                    r = 4 * n + 2 * i + t
                    out[r // 8, r % 8 : r % 8 + 1, :] = row[:, 128 * t : 128 * t + 128]
    for member in range(19):
        for i in range(2):
            for t in range(2):
                tile = pops[member, i, :, 128 * t : 128 * t + 128]
                whole[2 * member + i, 4 * t : 4 * t + 4, :] = tile


class Block:
    def __init__(self, whole, halos, group):
        self.whole, self.halos, self.group = whole, halos, group

    def slot(self, s, field):
        at = 4 * (field % 2) + 2 * s
        return self.whole[W_GRAIN + field // 2, at : at + 2, :]

    def pops(self, member, i, t):
        return self.whole[2 * member + i, 4 * t : 4 * t + 4, :]

    def halo_pops(self, end, member, i, t):
        if VELOCITIES[member][1]:
            n = Y_MEMBERS.index(member)
        elif member in Y_STANDS:
            n = Y_STANDS[member]
        else:
            return jnp.zeros((1, 128), F32)
        r = 4 * n + 2 * i + t
        return self.halos[end, self.group, r // 8, r % 8 : r % 8 + 1, :]

    def halo_slot(self, end, s, field):
        if field in Y_FIELDS:
            f = Y_FIELDS.index(field)
        else:
            k = field - E0
            q = k // 3 % 3 - (1 - end)
            if q not in (0, 1):
                return jnp.zeros((1, 128), F32)
            f = 11 + 6 * (k // 9) + 3 * q + k % 3
        r = Y_GRAIN + 2 * f + s
        return self.halos[end, self.group, r // 8, r % 8 : r % 8 + 1, :]

    def bins(self, s, field):
        row = iota((8, 128), 0)
        n, at = W_GRAIN + field // 2, 4 * (field % 2) + 2 * s
        rows = [
            self.halo_slot(0, s, field),
            self.whole[n, at : at + 1, :],
            self.whole[n, at + 1 : at + 2, :],
            self.halo_slot(1, s, field),
        ]
        rows = [jnp.broadcast_to(value, (8, 128)) for value in rows]
        return jnp.where(
            row < 4,
            jnp.where(row < 2, rows[0], rows[1]),
            jnp.where(row < 6, rows[2], rows[3]),
        )

    def cells(self, member, i, t):
        row = iota((8, 128), 0)
        own = self.whole[2 * member + i]
        if isinstance(t, int):
            own = roll(own, 2 - 4 * t, 0)
            low, high = [self.halo_pops(end, member, i, t) for end in range(2)]
        else:
            own = jnp.where(t, roll(own, -2, 0), roll(own, 2, 0))
            low, high = [
                jnp.where(
                    t, self.halo_pops(end, member, i, 1), self.halo_pops(end, member, i, 0)
                )
                for end in range(2)
            ]
        low, high = jnp.broadcast_to(low, (8, 128)), jnp.broadcast_to(high, (8, 128))
        return jnp.where(row < 2, low, jnp.where(row > 5, high, own))


def position(code, offset):
    first = jnp.floor(code * 0.25)
    rest = code - 4.0 * first
    second = jnp.floor(rest * 0.5)
    corner = [first, second, rest - 2.0 * second]
    return [corner[c] + offset[c] for c in range(3)]


def store_ends(groups, paired, side, first, second, held):
    for g in range(groups):
        held[side, g] = first[g]
        held[1 - side, g] = second[(g + 1) % 2 if paired else g]


def lane_groups(groups):
    return [0, 1, 0, 1] if groups == 2 else [0, 1, 1, 2]


def by_group(groups, values, lane):
    order = lane_groups(groups)
    result = values[order[3]]
    for q in (2, 1, 0):
        if order[q] != order[q + 1] or q < 2:
            result = jnp.where(lane < 32 * (q + 1), values[order[q]], result)
    return result


def by_layer(groups, values, lane):
    odd = lane // 16 % 2 == 1
    pairs = [jnp.where(odd, values[2 * g + 1], values[2 * g]) for g in range(groups)]
    return by_group(groups, pairs, lane)


def cell_codes(lane, row):
    return (4 * (lane // 16 % 2) + 2 * (row % 2) + lane % 2).astype(F32)


def choose(masks, values):
    return jnp.where(masks[0], values[0], jnp.where(masks[1], values[1], 0.0))


def z_pack_kernel(groups, paired, sides, *refs):
    flags = end_flags(sides)
    wholes, (first, second, out, held) = refs[:groups], refs[groups:]
    store_ends(groups, paired, flags[0], first, second, held)
    high = flags[1] == 1
    lane, row = iota((8, 128), 1), iota((8, 128), 0)
    block = [Block(wholes[g], held, g) for g in range(groups)]
    start = jnp.where(high, 127, 0)
    index = jnp.full((8, 128), start, jnp.int32)
    pops_index = jnp.full((8, 128), jnp.where(high, 126, 0), jnp.int32) + lane % 2
    inner = lane % 16 // 2

    def picked(s, field):
        values = [pick_lanes(block[g].bins(s, field), index) for g in range(groups)]
        return by_group(groups, values, lane)

    slots = [[picked(s, field) for field in range(38)] for s in range(2)]
    code = cell_codes(lane, row)
    masks = [slots[s][CODE] == code for s in range(2)]
    values = [choose(masks, [slots[0][f], slots[1][f]]) for f in range(36)]
    for member in range(19):
        tiles = []
        for layer in range(2 * groups):
            g, i = layer // 2, layer % 2
            tile = block[g].cells(member, i, high)
            tiles.append(pick_lanes(tile, pops_index))
        values.append(by_layer(groups, tiles, lane))
    for tile in range(CONTACT_TILE):
        packed = values[8 * tile]
        for q in range(1, 8):
            if 8 * tile + q < len(values):
                packed = jnp.where(inner == q, values[8 * tile + q], packed)
        out[tile] = packed
    packed = jnp.zeros((8, 128), F32)
    for s in range(2):
        state = position(slots[s][CODE], slots[s][6:9]) + [slots[s][RADIUS]] + slots[s][0:6]
        for q, value in enumerate(state):
            packed = jnp.where(lane % 32 == 16 * s + q, value, packed)
    out[CONTACT_TILE] = packed


def dot_lattice(vector, velocity):
    total = None
    for c in range(3):
        if vector[c]:
            if total is None:
                total = velocity[c] if vector[c] > 0 else -velocity[c]
            else:
                total = total + velocity[c] if vector[c] > 0 else total - velocity[c]
    return total


def equilibrium_base(velocity):
    return 1.0 - 1.5 * (
        velocity[0] * velocity[0] + velocity[1] * velocity[1] + velocity[2] * velocity[2]
    )


def collide(f, sums, members):
    fraction = 1.0 - jnp.exp(-sums[0])
    excess = relax_time - 0.5
    weight = fraction * excess / (1.0 - fraction + excess)
    inverse = 1.0 / jnp.maximum(sums[0], fraction_floor)
    solid_velocity = [sums[1 + c] * inverse for c in range(3)]
    density = sum(f[1:], f[0])
    momentum = []
    for c in range(3):
        plus = [f[m] for m in range(19) if VELOCITIES[m][c] > 0]
        minus = [f[m] for m in range(19) if VELOCITIES[m][c] < 0]
        momentum.append(sum(plus[1:], plus[0]) - sum(minus[1:], minus[0]))
    per_density = 1.0 / density
    fluid_velocity = [momentum[c] * per_density for c in range(3)]
    share = [weight * inverse * (momentum[c] - density * solid_velocity[c]) for c in range(3)]
    relax = (1.0 - weight) * (1.0 / relax_time)
    keep = 1.0 - relax
    fluid_base = equilibrium_base(fluid_velocity)
    solid_base = equilibrium_base(solid_velocity)
    done = {}
    for member in [0] + list(range(1, 19, 2)):
        reverse = member + 1 if member else 0
        if member not in members and reverse not in members:
            continue
        part = WEIGHTS[member] * density
        if member == 0:
            fluid = [part * fluid_base] * 2
            settled = [part * solid_base] * 2
        else:
            ends = []
            for base, velocity in (
                (fluid_base, fluid_velocity),
                (solid_base, solid_velocity),
            ):
                along = dot_lattice(VELOCITIES[member], velocity)
                even = base + 4.5 * along * along
                odd = 3.0 * along
                ends.append([part * (even + odd), part * (even - odd)])
            fluid, settled = ends
        pair = [f[member], f[reverse]]
        for way, m in enumerate((member, reverse)[: 2 if member else 1]):
            if m in members:
                exchange = (pair[1 - way] - fluid[1 - way]) - (pair[way] - settled[way])
                done[m] = keep * pair[way] + relax * fluid[way] + weight * exchange
    return done, share


def deposit_terms(weight, base, spin, k):
    terms = [weight]
    for c in range(3):
        u, v = (c + 1) % 3, (c + 2) % 3
        speed = base[c]
        if k[v]:
            speed = speed + spin[u] if k[v] > 0 else speed - spin[u]
        if k[u]:
            speed = speed - spin[v] if k[u] > 0 else speed + spin[v]
        terms.append(weight * speed)
    return terms


def plus(totals, terms):
    return list(terms) if totals is None else [a + b for a, b in zip(totals, terms)]


class Moments:
    def __init__(self):
        self.force, self.moment = [None] * 3, [None] * 3

    def add(self, store, c, value, sign):
        if store[c] is None:
            store[c] = value if sign > 0 else -value
        else:
            store[c] = store[c] + value if sign > 0 else store[c] - value

    def turn(self, axis, forces, sign):
        u, v = (axis + 1) % 3, (axis + 2) % 3
        self.add(self.moment, v, forces[u], sign)
        self.add(self.moment, u, forces[v], -sign)

    def push(self, forces):
        for c in range(3):
            self.add(self.force, c, forces[c], 1)

    def loads(self, offset):
        turned = cross([0.5 - value for value in offset], self.force)
        return self.force + [self.moment[c] + turned[c] for c in range(3)]


def pair_force(gap, a_radius, a_speed, a_turn, other, keep=None):
    b_radius = other[0]
    distance = jnp.sqrt(gap[0] * gap[0] + gap[1] * gap[1] + gap[2] * gap[2])
    scale = 1.0 / jnp.maximum(distance, distance_floor)
    normal = [gap[c] * scale for c in range(3)]
    depth = jnp.maximum(a_radius + b_radius - distance, 0.0)
    strength = a_radius * b_radius * depth
    if keep is not None:
        strength = jnp.where(keep, strength, 0.0)
    turning = [a_turn[c] + b_radius * other[4 + c] for c in range(3)]
    swing = cross(turning, normal)
    relative = [a_speed[c] - other[1 + c] + swing[c] for c in range(3)]
    along = relative[0] * normal[0] + relative[1] * normal[1] + relative[2] * normal[2]
    factor = 1.0 + along
    pushed = [strength * (factor * normal[c] + relative[c]) for c in range(3)]
    return pushed, cross(normal, pushed)


def own_state(block):
    def rows(field):
        values = [block.slot(s, field) for s in range(2)]
        return jnp.concatenate([values[0], values[0], values[1], values[1]], axis=0)

    place = position(rows(CODE), [rows(6 + c) for c in range(3)])
    return place, [rows(RADIUS)] + [rows(c) for c in range(6)]


POPS_PARTS = [(0, 5), (5, 5), (10, 5), (15, 4)]
PARTS = [4, 9, 14, 18]
AT_LAYER = {0: 0, 1: 1, 2: 2, -1: 3}


def bulk_kernel(groups, paired, sides, *refs):
    flags = end_flags(sides)
    layers = 2 * groups
    wholes, (y_first, y_second) = refs[:groups], refs[groups : groups + 2]
    out_pops, out_loads = refs[groups + 2 : groups + 4]
    held, placed, solid, passed, share = refs[groups + 4 :]
    targets = [0, 1, 2, layers - 1]
    store_ends(groups, paired, flags[0], y_first, y_second, held)
    block = [Block(wholes[g], held, g) for g in range(groups)]
    lane8 = iota((8, 128), 1)
    half = lane8 // 2

    def spread(rows):
        return jnp.concatenate([pick_lanes(rows, half), pick_lanes(rows, half + 64)], axis=1)

    cell_code = (2 * (iota((8, 256), 0) % 2) + iota((8, 256), 1) % 2).astype(F32)
    masks = []
    codes = [[block[g].bins(s, CODE) for g in range(groups)] for s in range(2)]
    for g in range(groups):
        wide = [spread(codes[s][g]) for s in range(2)]
        for i in range(2):
            masks.append([wide[s] == cell_code + 4.0 * i for s in range(2)])
    for field in range(36):
        rows = [[block[g].bins(s, field) for g in range(groups)] for s in range(2)]
        for g in range(groups):
            values = [spread(rows[s][g]) for s in range(2)]
            for i in range(2):
                placed[field, 2 * g + i] = choose(masks[2 * g + i], values)
    for layer in range(layers):
        spin = [placed[3 + c, layer] for c in range(3)]
        turned = cross(spin, [0.5 - placed[6 + c, layer] for c in range(3)])
        for c in range(3):
            placed[c, layer] = placed[c, layer] + turned[c]

    for n, target in enumerate(targets):
        total = None
        for kz in (-1, 0, 1):
            along_z = None
            for ky in (-1, 0, 1):
                along_y = None
                for kx in (-1, 0, 1):
                    source = (target - kx) % layers
                    weight = placed[E0 + 9 * (kx + 1) + 3 * (ky + 1) + kz + 1, source]
                    spin = [placed[3 + c, source] for c in range(3)]
                    base = [placed[c, source] for c in range(3)]
                    along_y = plus(along_y, deposit_terms(weight, base, spin, (kx, ky, kz)))
                along_z = plus(along_z, [roll(a, ky, 0) for a in along_y])
            total = plus(total, [roll(a, kz, 1) for a in along_z])
        for f in range(4):
            solid[f, n] = total[f]

    for n, target in enumerate(targets):
        g, i = target // 2, target % 2
        if n < 2:
            members = list(range(19))
        else:
            members = [m for m in range(19) if VELOCITIES[m][0] == (-1 if n == 2 else 1)]
        for t in range(2):
            tile = slice(128 * t, 128 * t + 128)
            f = [block[g].cells(member, i, t) for member in range(19)]
            done, forces = collide(f, [solid[c, n, :, tile] for c in range(4)], members)
            for c in range(3):
                share[c, n, :, tile] = forces[c]
            for m, value in done.items():
                passed[m, n, :, tile] = value
    for member in range(19):
        vector = VELOCITIES[member]
        for i in range(2):
            value = roll(passed[member, AT_LAYER[i - vector[0]]], vector[2], 1)
            value = roll(value, vector[1] - 2, 0)
            for t in range(2):
                out_pops[2 * member + i, 4 * t : 4 * t + 4, :] = value[
                    0:4, 128 * t : 128 * t + 128
                ]

    moments = [Moments() for _ in range(2)]
    for kz in (-1, 0, 1):
        across = [[roll(share[c, n], -kz, 1) for c in range(3)] for n in range(4)]
        for ky in (-1, 0, 1):
            near = [[roll(across[n][c], -ky, 0) for c in range(3)] for n in range(4)]
            for i in range(2):
                together = None
                for kx in (-1, 0, 1):
                    weight = placed[E0 + 9 * (kx + 1) + 3 * (ky + 1) + kz + 1, i]
                    forces = [weight * near[AT_LAYER[i + kx]][c] for c in range(3)]
                    together = plus(together, forces)
                    if kx:
                        moments[i].turn(0, forces, kx)
                moments[i].push(together)
                if ky:
                    moments[i].turn(1, together, ky)
                if kz:
                    moments[i].turn(2, together, kz)
    hydro = [moments[i].loads([placed[6 + c, i] for c in range(3)]) for i in range(2)]

    even = (2 * lane8) % 128
    inside = (lane8 > 0) & (lane8 < 127)
    for f in range(6):
        for s in range(2):
            value = jnp.where(masks[0][s], hydro[0][f], 0.0) + jnp.where(
                masks[1][s], hydro[1][f], 0.0
            )
            value = value + roll(value, -1, 0)
            value = value + roll(value, -1, 1)
            value = jnp.where(
                lane8 < 64, pick_lanes(value[:, :128], even), pick_lanes(value[:, 128:], even)
            )
            value = jnp.where(inside, value, 0.0)
            both = jnp.concatenate([value[2:3], value[4:5]], axis=0)
            out_loads[f, 2 * s : 2 * s + 2, :] = both


def side_kernel(groups, paired, sides, *refs):
    flags = end_flags(sides)
    layers = 2 * groups
    wholes, (y_first, y_second) = refs[:groups], refs[groups : groups + 2]
    out_contact, out_edge, held = refs[groups + 2 :]
    store_ends(groups, paired, flags[0], y_first, y_second, held)
    block = [Block(wholes[g], held, g) for g in range(groups)]
    lane8, row8 = iota((8, 128), 1), iota((8, 128), 0)
    inner = lane8 % 16
    z_near = jnp.where(inner < 8, jnp.maximum(inner - 4, 0), jnp.minimum(inner + 116, 127))
    z_bin = jnp.where(inner < 8, z_near // 2, jnp.minimum(inner + 244, 255) // 2)

    def at_edge(s, field):
        rows = [pick_lanes(block[g].bins(s, field), z_bin) for g in range(groups)]
        return by_group(groups, rows, lane8)

    edge_code = cell_codes(lane8, row8)
    codes = [at_edge(s, CODE) for s in range(2)]
    for s in range(2):
        out_edge[CODE_AT + s] = codes[s]
    edge_masks = [value == edge_code for value in codes]
    for field in range(36):
        out_edge[field] = choose(edge_masks, [at_edge(s, field) for s in range(2)])
    for member in range(19):
        tiles = []
        for layer in range(layers):
            near = [block[layer // 2].cells(member, layer % 2, t) for t in range(2)]
            tiles.append(
                jnp.where(inner < 8, pick_lanes(near[0], z_near), pick_lanes(near[1], z_near))
            )
        out_edge[POPS_AT + member] = by_layer(groups, tiles, lane8)

    place, state = own_state(block[0])
    a_radius, a_speed = state[0], state[1:4]
    a_turn = [a_radius * value for value in state[4:7]]
    push, twist = None, None
    for oy in (-1, 0, 1):
        for g in range(groups):
            steps = [0] if g == 0 else []
            if g == 1:
                steps = steps + [1]
            if g == groups - 1:
                steps = steps + [-1]
            states = []
            for field in [CODE, 6, 7, 8, RADIUS, 0, 1, 2, 3, 4, 5]:
                values = []
                for s in range(2):
                    value = block[g].slot(s, field)
                    if oy < 0:
                        value = jnp.concatenate(
                            [block[g].halo_slot(0, s, field), value[0:1]], axis=0
                        )
                    if oy > 0:
                        value = jnp.concatenate(
                            [value[1:2], block[g].halo_slot(1, s, field)], axis=0
                        )
                    values.append(value)
                states.append(jnp.concatenate(values + values, axis=0))
            states = position(states[0], states[1:4]) + states[4:]
            for oz in (-1, 0, 1):
                other = [roll(value, -oz, 1) for value in states]
                keep = lane8 != (0 if oz < 0 else 127) if oz else None
                gap = [other[c] - place[c] for c in range(3)]
                gap[1], gap[2] = gap[1] + 2.0 * oy, gap[2] + 2.0 * oz
                for ox in steps:
                    apart = [gap[0] + 2.0 * ox, gap[1], gap[2]]
                    pushed, twisted = pair_force(
                        apart, a_radius, a_speed, a_turn, other[3:], keep
                    )
                    push, twist = plus(push, pushed), plus(twist, twisted)
    contact = [-value for value in push] + [-a_radius * value for value in twist]
    contact = [value + roll(value, -2, 0) for value in contact]

    for f in range(6):
        out_contact[f] = contact[f]


def edge_kernel(
    groups, paired, sides, whole, bulk_pops, bulk_loads, bulk_contact, edge, first, second, *refs
):
    final_pops, final_loads, held, out_pops, out_loads, sems = refs
    side = end_flags(sides)[1]
    for tile in range(Z_TILES):
        held[side, tile] = first[tile]
        value = second[tile]
        held[1 - side, tile] = roll(value, 32, 1) if paired else value
    lane, row = iota((8, 128), 1), iota((8, 128), 0)
    inner = lane % 16
    at_low = (inner == 2) | (inner == 3)
    at_high = (inner == 12) | (inner == 13)

    def value_of(field):
        q = 2 * (field % 8)
        low = roll(held[0, field // 8], 2 - q, 1)
        high = roll(held[1, field // 8], 12 - q, 1)
        return jnp.where(at_low, low, jnp.where(at_high, high, edge[field]))

    speed, spin, offset = [[value_of(3 * n + c) for c in range(3)] for n in range(3)]
    weights = [value_of(E0 + k) for k in range(27)]
    turned = cross(spin, [0.5 - value for value in offset])
    base = [speed[c] + turned[c] for c in range(3)]
    sums = None
    for kx in (-1, 0, 1):
        for kz in (-1, 0, 1):
            along = None
            for ky in (-1, 0, 1):
                weight = weights[9 * (kx + 1) + 3 * (ky + 1) + kz + 1]
                terms = deposit_terms(weight, base, spin, (kx, ky, kz))
                along = plus(along, [roll(a, ky, 0) for a in terms])
            sums = plus(sums, [roll(a, 16 * kx + kz, 1) for a in along])
    f = [value_of(POPS_AT + member) for member in range(19)]
    done, share = collide(f, sums, list(range(19)))

    lane4 = iota((4, 128), 1)
    copies = []
    for member in range(19):
        vector = VELOCITIES[member]
        value = roll(done[member], vector[1] - 2, 0)
        shift = 16 * vector[0] + vector[2]
        for i in range(2):
            for t in range(2):
                home = shift - 16 * i + (116 if t else -4)
                moved = roll(value, home, 1)[0:4]
                bulk = bulk_pops[2 * member + i, 4 * t : 4 * t + 4, :]
                mask = lane4 >= 126 if t else lane4 < 2
                out_pops[member, i, :, 128 * t : 128 * t + 128] = jnp.where(mask, moved, bulk)
        if member in PARTS:
            n = PARTS.index(member)
            part = pl.ds(PARTS[n - 1] + 1 if n else 0, member - (PARTS[n - 1] if n else -1))
            copy = pltpu.make_async_copy(out_pops.at[part], final_pops.at[part], sems.at[n])
            copy.start()
            copies.append(copy)

    moments = Moments()
    for kx in (-1, 0, 1):
        for kz in (-1, 0, 1):
            near = [roll(share[c], -16 * kx - kz, 1) for c in range(3)]
            together = None
            for ky in (-1, 0, 1):
                weight = weights[9 * (kx + 1) + 3 * (ky + 1) + kz + 1]
                forces = [weight * roll(near[c], -ky, 0) for c in range(3)]
                together = plus(together, forces)
                if ky:
                    moments.turn(1, forces, ky)
            moments.push(together)
            if kx:
                moments.turn(0, together, kx)
            if kz:
                moments.turn(2, together, kz)
    hydro = moments.loads(offset)

    place, state = own_state(Block(whole, None, 0))
    own_index = jnp.where(lane < 64, 0, 127)
    place = [pick_lanes(value, own_index) for value in place]
    state = [pick_lanes(value, own_index) for value in state]
    a_radius, a_speed = state[0], state[1:4]
    a_turn = [a_radius * value for value in state[4:7]]
    step_x, step_y = inner - 1, lane % 64 // 16 - 1
    order = lane_groups(groups)
    runs = [order.index(groups - 1), 0, 1]
    run = 32 * jnp.where(step_x < 0, runs[0], jnp.where(step_x == 0, 0, runs[2]))
    other = [None] * 10
    for end in range(2):
        tile = held[end, CONTACT_TILE]
        for oy in (-1, 0, 1):
            at = 2 * (oy + 1)
            rows = jnp.concatenate([tile[at : at + 1], tile[at + 2 : at + 3]], axis=0)
            moved = roll(rows, -16, 1)
            rows = jnp.concatenate([rows, moved, rows, moved], axis=0)
            mask = (lane // 64 == end) & (step_y == oy)
            for q in range(10):
                value = pick_lanes(rows, run + q)
                other[q] = value if other[q] is None else jnp.where(mask, value, other[q])
    keep = (step_x < 2) & (step_y < 2)
    gap = [
        other[0] - place[0] + (2 * step_x).astype(F32),
        other[1] - place[1] + (2 * step_y).astype(F32),
        other[2] - place[2] + jnp.where(lane < 64, -2.0, 2.0),
    ]
    pushed, twisted = pair_force(gap, a_radius, a_speed, a_turn, other[3:], keep)
    contact = [-value for value in pushed] + [-a_radius * value for value in twisted]
    ends = lane == 0, lane == 127
    masks = [edge[CODE_AT + s] == cell_codes(lane, row) for s in range(2)]
    for f in range(6):
        value = contact[f] + roll(contact[f], -2, 0)
        value = value + roll(value, -1, 1) + roll(value, -2, 1)
        value = value + roll(value, -16, 1) + roll(value, -32, 1)
        touch = jnp.where(ends[0], value, jnp.where(ends[1], roll(value, 63, 1), 0.0))
        for s in range(2):
            value = jnp.where(masks[s], hydro[f], 0.0)
            value = value + roll(value, -16, 1)
            value = value + roll(value, -1, 0)
            value = value + roll(value, -1, 1)
            value = jnp.where(
                ends[0], roll(value, -4, 1), jnp.where(ends[1], roll(value, 117, 1), 0.0)
            )
            both = jnp.concatenate([value[2:3], value[4:5]], axis=0)
            both = both + touch[4 * s : 4 * s + 2]
            both = both + bulk_contact[f, 4 * s : 4 * s + 2, :]
            out_loads[f, s, 0] = bulk_loads[f, 2 * s : 2 * s + 2, :] + both
    copy = pltpu.make_async_copy(out_loads, final_loads, sems.at[len(PARTS)])
    copy.start()
    for copy in copies + [copy]:
        copy.wait()


PARAMS = pltpu.CompilerParams(vmem_limit_bytes=32 * 2**20)


def call(kernel, operands, shapes, scratch=(), spaces=(pltpu.VMEM, pltpu.VMEM)):
    return pl.pallas_call(
        kernel,
        out_shape=[jax.ShapeDtypeStruct(shape, F32) for shape in shapes],
        in_specs=[pl.BlockSpec(memory_space=spaces[0])] * len(operands),
        out_specs=[pl.BlockSpec(memory_space=spaces[1])] * len(shapes),
        scratch_shapes=[pltpu.VMEM(x, F32) if isinstance(x, tuple) else x for x in scratch],
        compiler_params=PARAMS,
    )(*operands)


def step(paired, sizes, *blocks):
    nx, ny, nz = sizes
    axes = ("gx", "gy", "gz")
    groups = 2 if paired else 3

    def permute(value, target):
        pairs = []
        for x in range(nx):
            for y in range(ny):
                for z in range(nz):
                    tx, ty, tz = target(x, y, z)
                    there = ((tx % nx) * ny + ty % ny) * nz + tz % nz
                    pairs.append(((x * ny + y) * nz + z, there))
        return lax.ppermute(value, axes, pairs)

    def swap(value):
        return permute(value, lambda x, y, z: (1 - x, y, z))

    def to_low(value):
        return permute(value, lambda x, y, z: (x - 1, y, z))

    def to_high(value):
        return permute(value, lambda x, y, z: (x + 1, y, z))

    ends_y = (Y_BLOCKS, 8, 128)
    shape_z = (Z_TILES, 8, 128)
    shape_y = (groups,) + ends_y
    sides = None if paired else (1, 1)
    held = [pltpu.VMEM(block.shape, block.dtype) for block in blocks]
    held[0] = pltpu.VMEM((22,) + blocks[0].shape[1:], F32)
    blocks = [pltpu.with_memory_space_constraint(block, pltpu.HBM) for block in blocks]
    whole, mine, theirs = call(
        functools.partial(pack_kernel, sides),
        blocks,
        [(W_BLOCKS, 8, 128), shape_y, ends_y],
        held + [pltpu.SemaphoreType.DMA((6 + len(POPS_PARTS),))],
        (pltpu.HBM, pltpu.VMEM),
    )

    def pack_z(sides, wholes, halos):
        kernel = functools.partial(z_pack_kernel, groups, paired, sides)
        return call(kernel, wholes + halos, [shape_z], [(2,) + shape_y])[0]

    def pack_bulk(wholes, halos):
        scratch = [
            (2,) + shape_y,
            (36, 2 * groups, 8, 256),
            (4, 4, 8, 256),
            (19, 4, 8, 256),
            (3, 4, 8, 256),
        ]
        return call(
            functools.partial(bulk_kernel, groups, paired, sides),
            wholes + halos,
            [(W_GRAIN, 8, 128), (6, 4, 128)],
            scratch,
        )

    if paired:
        rows = mine.at[1].set(swap(theirs))
        wholes = [whole, swap(whole)]
        first = permute(rows, lambda x, y, z: (x, y + (1 if (x + y) % 2 == 0 else -1), z))
        halos = [first, swap(first)]
        first = permute(
            pack_z(sides, wholes, halos),
            lambda x, y, z: (x, y, z + (1 if (x + z) % 2 == 0 else -1)),
        )
        bulk = pack_bulk(wholes, halos)
        first, bulk = lax.optimization_barrier((first, bulk))
        ends = [first, swap(first)]
    else:
        wholes = [whole, to_low(whole), to_high(whole)]
        up, down = [jnp.stack([v, to_low(v), to_high(v)]) for v in (mine[0], theirs)]
        halos = [
            permute(down, lambda x, y, z: (x, y - 1, z)),
            permute(up, lambda x, y, z: (x, y + 1, z)),
        ]
        low = (1, 0)
        ends = [
            permute(pack_z(low, wholes, halos), lambda x, y, z: (x, y, z - 1)),
            permute(pack_z(sides, wholes, halos), lambda x, y, z: (x, y, z + 1)),
        ]
        bulk = pack_bulk(wholes, halos)
    side = call(
        functools.partial(side_kernel, groups, paired, sides),
        wholes + halos,
        [(6, 8, 128), (EDGE_VALUES, 8, 128)],
        [(2,) + shape_y],
    )
    populations, offset = blocks[0], blocks[2]
    shapes = [populations.shape, (6,) + offset.shape[1:]]
    return tuple(
        call(
            functools.partial(edge_kernel, groups, paired, sides),
            [whole] + list(bulk) + list(side) + ends,
            shapes,
            [(2,) + shape_z] + shapes + [pltpu.SemaphoreType.DMA((len(PARTS) + 1,))],
            (pltpu.VMEM, pltpu.HBM),
        )
    )


def solution(mesh, paired=None):
    sizes = tuple(mesh.shape[axis] for axis in ("gx", "gy", "gz"))
    if paired is None:
        paired = sizes[0] == 2 and sizes[1] % 2 == 0 and sizes[2] % 2 == 0
    cells, bins = P(None, "gx", "gy", "gz"), P(None, None, "gx", "gy", "gz")
    return jax.shard_map(
        functools.partial(step, paired, sizes),
        mesh=mesh,
        in_specs=(cells, cells, bins, cells, bins, bins, bins),
        out_specs=(cells, bins),
        check_vma=False,
    )
```

```python
import functools

import jax
import jax.numpy as jnp
from jax import lax
from jax.experimental import pallas as pl
from jax.experimental.pallas import tpu as pltpu
from jax.sharding import PartitionSpec as P

VELOCITIES = [
    (0, 0, 0),
    (1, 0, 0),
    (-1, 0, 0),
    (0, 1, 0),
    (0, -1, 0),
    (0, 0, 1),
    (0, 0, -1),
    (1, 1, 0),
    (-1, -1, 0),
    (1, -1, 0),
    (-1, 1, 0),
    (1, 0, 1),
    (-1, 0, -1),
    (1, 0, -1),
    (-1, 0, 1),
    (0, 1, 1),
    (0, -1, -1),
    (0, 1, -1),
    (0, -1, 1),
]
WEIGHTS = [1.0 / 3.0] + [1.0 / 18.0] * 6 + [1.0 / 36.0] * 12
relax_time = 0.8
fraction_floor = 0.1
distance_floor = 0.5

E0, RADIUS, CODE, PLACE = 9, 36, 37, 38
POPS_AT, CODE_AT, EDGE_VALUES = 36, 55, 57
Z_TILES, CONTACT_TILE = 8, 7
Y_FIELDS = list(range(9)) + [RADIUS, CODE]
Y_MEMBERS = [m for m in range(19) if VELOCITIES[m][1]] + [19, 20, 21]
Y_STANDS = {0: 10, 1: 11, 5: 12}
Y_GRAIN, Y_BLOCKS = 52, 14
W_GRAIN, W_BLOCKS = 38, 57
F32 = jnp.float32


def end_flags(sides):
    if sides is not None:
        return sides
    ix, iy, iz = [lax.axis_index(axis) for axis in ("gx", "gy", "gz")]
    return 1 - lax.rem(ix + iy, 2), 1 - lax.rem(ix + iz, 2)


def iota(shape, dim):
    return lax.broadcasted_iota(jnp.int32, shape, dim)


def pick_lanes(values, index):
    return jnp.take_along_axis(values, index, axis=1, mode="promise_in_bounds")


def roll(values, shift, axis):
    size = values.shape[axis]
    return pltpu.roll(values, shift % size, axis) if shift % size else values


def cross(a, b):
    return [
        a[1] * b[2] - a[2] * b[1],
        a[2] * b[0] - a[0] * b[2],
        a[0] * b[1] - a[1] * b[0],
    ]


def pack_kernel(sides, *refs):
    flags = end_flags(sides)
    sources, (whole, mine, theirs), held, sems = refs[:7], refs[7:10], refs[10:17], refs[17]
    copies = [
        pltpu.make_async_copy(source, target, sems.at[n])
        for n, (source, target) in enumerate(zip(sources[1:], held[1:]))
    ]
    for n, part in enumerate(POPS_PARTS):
        part = pl.ds(*part)
        copies.append(pltpu.make_async_copy(sources[0].at[part], held[0].at[part], sems.at[6 + n]))
    for copy in copies:
        copy.start()
    pops, cell, off, rad, vel, spin, inter = held
    for copy in copies[:6]:
        copy.wait()

    def slot(s, field, rows=slice(None)):
        if field < 3:
            return vel[field, s, 0, rows, :]
        if field < 6:
            return spin[field - 3, s, 0, rows, :]
        if field < 9:
            return off[field - 6, s, 0, rows, :]
        if field < RADIUS:
            return inter[field - E0, s, 0, rows, :]
        if field == RADIUS:
            return rad[s, 0, rows, :]
        return cell[s, 0, rows, :].astype(F32)

    for field in range(38):
        for s in range(2):
            at = 4 * (field % 2) + 2 * s
            whole[W_GRAIN + field // 2, at : at + 2, :] = slot(s, field)
    for out, end in ((mine.at[0], flags[0]), (theirs, 1 - flags[0])):
        for s in range(2):
            for f in range(29):
                if f < 11:
                    value = slot(s, Y_FIELDS[f], pl.ds(end, 1))
                else:
                    kx, q, kz = (f - 11) // 6, (f - 11) // 3 % 2, (f - 11) % 3
                    value = inter[9 * kx + 3 * (q + end) + kz, s, 0, pl.ds(end, 1), :]
                r = Y_GRAIN + 2 * f + s
                out[r // 8, r % 8 : r % 8 + 1, :] = value
        out[Y_BLOCKS - 1, 6:8, :] = jnp.zeros((2, 128), F32)
    for copy in copies[6:]:
        copy.wait()
    still = [m for m in range(19) if not VELOCITIES[m][1]]
    for i in range(2):
        sums = []
        for c in (0, 2):
            rising = [pops[m, i] for m in still if VELOCITIES[m][c] > 0]
            falling = [pops[m, i] for m in still if VELOCITIES[m][c] < 0]
            sums.append(sum(rising[1:], rising[0]) - sum(falling[1:], falling[0]))
        total = sum([pops[m, i] for m in still[1:]], pops[0, i])
        pops[19, i] = total - sums[0] - sums[1]
        pops[20, i] = sums[0]
        pops[21, i] = sums[1]
    for out, end in ((mine.at[0], flags[0]), (theirs, 1 - flags[0])):
        for n, member in enumerate(Y_MEMBERS):
            for i in range(2):
                row = pops[member, i, pl.ds(3 * end, 1), :]
                for t in range(2):
                    r = 4 * n + 2 * i + t
                    out[r // 8, r % 8 : r % 8 + 1, :] = row[:, 128 * t : 128 * t + 128]
    for member in range(19):
        for i in range(2):
            for t in range(2):
                tile = pops[member, i, :, 128 * t : 128 * t + 128]
                whole[2 * member + i, 4 * t : 4 * t + 4, :] = tile


class Block:
    def __init__(self, whole, halos, group):
        self.whole, self.halos, self.group = whole, halos, group

    def slot(self, s, field):
        at = 4 * (field % 2) + 2 * s
        return self.whole[W_GRAIN + field // 2, at : at + 2, :]

    def pops(self, member, i, t):
        return self.whole[2 * member + i, 4 * t : 4 * t + 4, :]

    def halo_pops(self, end, member, i, t):
        if VELOCITIES[member][1]:
            n = Y_MEMBERS.index(member)
        elif member in Y_STANDS:
            n = Y_STANDS[member]
        else:
            return jnp.zeros((1, 128), F32)
        r = 4 * n + 2 * i + t
        return self.halos[end, self.group, r // 8, r % 8 : r % 8 + 1, :]

    def halo_slot(self, end, s, field):
        if field in Y_FIELDS:
            f = Y_FIELDS.index(field)
        else:
            k = field - E0
            q = k // 3 % 3 - (1 - end)
            if q not in (0, 1):
                return jnp.zeros((1, 128), F32)
            f = 11 + 6 * (k // 9) + 3 * q + k % 3
        r = Y_GRAIN + 2 * f + s
        return self.halos[end, self.group, r // 8, r % 8 : r % 8 + 1, :]

    def bins(self, s, field):
        row = iota((8, 128), 0)
        n, at = W_GRAIN + field // 2, 4 * (field % 2) + 2 * s
        rows = [
            self.halo_slot(0, s, field),
            self.whole[n, at : at + 1, :],
            self.whole[n, at + 1 : at + 2, :],
            self.halo_slot(1, s, field),
        ]
        rows = [jnp.broadcast_to(value, (8, 128)) for value in rows]
        return jnp.where(
            row < 4,
            jnp.where(row < 2, rows[0], rows[1]),
            jnp.where(row < 6, rows[2], rows[3]),
        )

    def cells(self, member, i, t):
        row = iota((8, 128), 0)
        own = self.whole[2 * member + i]
        if isinstance(t, int):
            own = roll(own, 2 - 4 * t, 0)
            low, high = [self.halo_pops(end, member, i, t) for end in range(2)]
        else:
            own = jnp.where(t, roll(own, -2, 0), roll(own, 2, 0))
            low, high = [
                jnp.where(
                    t, self.halo_pops(end, member, i, 1), self.halo_pops(end, member, i, 0)
                )
                for end in range(2)
            ]
        low, high = jnp.broadcast_to(low, (8, 128)), jnp.broadcast_to(high, (8, 128))
        return jnp.where(row < 2, low, jnp.where(row > 5, high, own))


def position(code, offset):
    first = jnp.floor(code * 0.25)
    rest = code - 4.0 * first
    second = jnp.floor(rest * 0.5)
    corner = [first, second, rest - 2.0 * second]
    return [corner[c] + offset[c] for c in range(3)]


def store_ends(groups, paired, side, first, second, held):
    for g in range(groups):
        held[side, g] = first[g]
        held[1 - side, g] = second[(g + 1) % 2 if paired else g]


def lane_groups(groups):
    return [0, 1, 0, 1] if groups == 2 else [0, 1, 1, 2]


def by_group(groups, values, lane):
    order = lane_groups(groups)
    result = values[order[3]]
    for q in (2, 1, 0):
        if order[q] != order[q + 1] or q < 2:
            result = jnp.where(lane < 32 * (q + 1), values[order[q]], result)
    return result


def by_layer(groups, values, lane):
    odd = lane // 16 % 2 == 1
    pairs = [jnp.where(odd, values[2 * g + 1], values[2 * g]) for g in range(groups)]
    return by_group(groups, pairs, lane)


def cell_codes(lane, row):
    return (4 * (lane // 16 % 2) + 2 * (row % 2) + lane % 2).astype(F32)


def choose(masks, values):
    return jnp.where(masks[0], values[0], jnp.where(masks[1], values[1], 0.0))


def z_pack_kernel(groups, paired, sides, *refs):
    flags = end_flags(sides)
    wholes, (first, second, out, held) = refs[:groups], refs[groups:]
    store_ends(groups, paired, flags[0], first, second, held)
    high = flags[1] == 1
    lane, row = iota((8, 128), 1), iota((8, 128), 0)
    block = [Block(wholes[g], held, g) for g in range(groups)]
    start = jnp.where(high, 127, 0)
    index = jnp.full((8, 128), start, jnp.int32)
    pops_index = jnp.full((8, 128), jnp.where(high, 126, 0), jnp.int32) + lane % 2
    inner = lane % 16 // 2

    def picked(s, field):
        values = [pick_lanes(block[g].bins(s, field), index) for g in range(groups)]
        return by_group(groups, values, lane)

    slots = [[picked(s, field) for field in range(38)] for s in range(2)]
    code = cell_codes(lane, row)
    masks = [slots[s][CODE] == code for s in range(2)]
    values = [choose(masks, [slots[0][f], slots[1][f]]) for f in range(36)]
    for member in range(19):
        tiles = []
        for layer in range(2 * groups):
            g, i = layer // 2, layer % 2
            tile = block[g].cells(member, i, high)
            tiles.append(pick_lanes(tile, pops_index))
        values.append(by_layer(groups, tiles, lane))
    for tile in range(CONTACT_TILE):
        packed = values[8 * tile]
        for q in range(1, 8):
            if 8 * tile + q < len(values):
                packed = jnp.where(inner == q, values[8 * tile + q], packed)
        out[tile] = packed
    packed = jnp.zeros((8, 128), F32)
    for s in range(2):
        state = position(slots[s][CODE], slots[s][6:9]) + [slots[s][RADIUS]] + slots[s][0:6]
        for q, value in enumerate(state):
            packed = jnp.where(lane % 32 == 16 * s + q, value, packed)
    out[CONTACT_TILE] = packed


def dot_lattice(vector, velocity):
    total = None
    for c in range(3):
        if vector[c]:
            if total is None:
                total = velocity[c] if vector[c] > 0 else -velocity[c]
            else:
                total = total + velocity[c] if vector[c] > 0 else total - velocity[c]
    return total


def equilibrium_base(velocity):
    return 1.0 - 1.5 * (
        velocity[0] * velocity[0] + velocity[1] * velocity[1] + velocity[2] * velocity[2]
    )


def collide(f, sums, members):
    fraction = 1.0 - jnp.exp(-sums[0])
    excess = relax_time - 0.5
    weight = fraction * excess / (1.0 - fraction + excess)
    inverse = 1.0 / jnp.maximum(sums[0], fraction_floor)
    solid_velocity = [sums[1 + c] * inverse for c in range(3)]
    density = sum(f[1:], f[0])
    momentum = []
    for c in range(3):
        plus = [f[m] for m in range(19) if VELOCITIES[m][c] > 0]
        minus = [f[m] for m in range(19) if VELOCITIES[m][c] < 0]
        momentum.append(sum(plus[1:], plus[0]) - sum(minus[1:], minus[0]))
    per_density = 1.0 / density
    fluid_velocity = [momentum[c] * per_density for c in range(3)]
    share = [weight * inverse * (momentum[c] - density * solid_velocity[c]) for c in range(3)]
    relax = (1.0 - weight) * (1.0 / relax_time)
    keep = 1.0 - relax
    fluid_base = equilibrium_base(fluid_velocity)
    solid_base = equilibrium_base(solid_velocity)
    done = {}
    for member in [0] + list(range(1, 19, 2)):
        reverse = member + 1 if member else 0
        if member not in members and reverse not in members:
            continue
        part = WEIGHTS[member] * density
        if member == 0:
            fluid = [part * fluid_base] * 2
            settled = [part * solid_base] * 2
        else:
            ends = []
            for base, velocity in (
                (fluid_base, fluid_velocity),
                (solid_base, solid_velocity),
            ):
                along = dot_lattice(VELOCITIES[member], velocity)
                even = base + 4.5 * along * along
                odd = 3.0 * along
                ends.append([part * (even + odd), part * (even - odd)])
            fluid, settled = ends
        pair = [f[member], f[reverse]]
        for way, m in enumerate((member, reverse)[: 2 if member else 1]):
            if m in members:
                exchange = (pair[1 - way] - fluid[1 - way]) - (pair[way] - settled[way])
                done[m] = keep * pair[way] + relax * fluid[way] + weight * exchange
    return done, share


def deposit_terms(weight, base, spin, k):
    terms = [weight]
    for c in range(3):
        u, v = (c + 1) % 3, (c + 2) % 3
        speed = base[c]
        if k[v]:
            speed = speed + spin[u] if k[v] > 0 else speed - spin[u]
        if k[u]:
            speed = speed - spin[v] if k[u] > 0 else speed + spin[v]
        terms.append(weight * speed)
    return terms


def plus(totals, terms):
    return list(terms) if totals is None else [a + b for a, b in zip(totals, terms)]


class Moments:
    def __init__(self):
        self.force, self.moment = [None] * 3, [None] * 3

    def add(self, store, c, value, sign):
        if store[c] is None:
            store[c] = value if sign > 0 else -value
        else:
            store[c] = store[c] + value if sign > 0 else store[c] - value

    def turn(self, axis, forces, sign):
        u, v = (axis + 1) % 3, (axis + 2) % 3
        self.add(self.moment, v, forces[u], sign)
        self.add(self.moment, u, forces[v], -sign)

    def push(self, forces):
        for c in range(3):
            self.add(self.force, c, forces[c], 1)

    def loads(self, offset):
        turned = cross([0.5 - value for value in offset], self.force)
        return self.force + [self.moment[c] + turned[c] for c in range(3)]


def pair_force(gap, a_radius, a_speed, a_turn, other, keep=None):
    b_radius = other[0]
    distance = jnp.sqrt(gap[0] * gap[0] + gap[1] * gap[1] + gap[2] * gap[2])
    scale = 1.0 / jnp.maximum(distance, distance_floor)
    normal = [gap[c] * scale for c in range(3)]
    depth = jnp.maximum(a_radius + b_radius - distance, 0.0)
    strength = a_radius * b_radius * depth
    if keep is not None:
        strength = jnp.where(keep, strength, 0.0)
    turning = [a_turn[c] + b_radius * other[4 + c] for c in range(3)]
    swing = cross(turning, normal)
    relative = [a_speed[c] - other[1 + c] + swing[c] for c in range(3)]
    along = relative[0] * normal[0] + relative[1] * normal[1] + relative[2] * normal[2]
    factor = 1.0 + along
    pushed = [strength * (factor * normal[c] + relative[c]) for c in range(3)]
    return pushed, cross(normal, pushed)


def own_state(block):
    def rows(field):
        values = [block.slot(s, field) for s in range(2)]
        return jnp.concatenate([values[0], values[0], values[1], values[1]], axis=0)

    place = position(rows(CODE), [rows(6 + c) for c in range(3)])
    return place, [rows(RADIUS)] + [rows(c) for c in range(6)]


def end_lanes(high, inner):
    start = jnp.where(high, 12, 2)
    return (inner == start) | (inner == start + 1)


def end_contact(groups, tile, high, state):
    lane = iota((8, 128), 1)
    step_x, step_y = lane % 16 - 1, lane // 16 - 1
    place, a_radius, a_speed, a_spin = state[0:3], state[3], state[4:7], state[7:10]
    a_turn = [a_radius * value for value in a_spin]
    before = lane_groups(groups).index(groups - 1)
    run = 32 * jnp.where(step_x < 0, before, jnp.where(step_x == 0, 0, 1))
    other = [None] * 10
    for oy in (-1, 0, 1):
        at = 2 * (oy + 1)
        rows = jnp.concatenate([tile[at : at + 1], tile[at + 2 : at + 3]], axis=0)
        moved = roll(rows, -16, 1)
        rows = jnp.concatenate([rows, moved, rows, moved], axis=0)
        for q in range(10):
            value = pick_lanes(rows, run + q)
            other[q] = value if oy < 0 else jnp.where(step_y == oy, value, other[q])
    keep = (step_x < 2) & (step_y < 2)
    gap = [
        other[0] - place[0] + (2 * step_x).astype(F32),
        other[1] - place[1] + (2 * step_y).astype(F32),
        other[2] - place[2] + jnp.where(high, 2.0, -2.0),
    ]
    pushed, twisted = pair_force(gap, a_radius, a_speed, a_turn, other[3:], keep)
    contact = [-value for value in pushed] + [-a_radius * value for value in twisted]
    end = lane == jnp.where(high, 127, 0)
    result = []
    for value in contact:
        value = value + roll(value, -2, 0)
        value = value + roll(value, -1, 1) + roll(value, -2, 1)
        value = value + roll(value, -16, 1) + roll(value, -32, 1)
        result.append(jnp.where(end, jnp.where(high, roll(value, 127, 1), value), 0.0))
    return result


POPS_PARTS = [(0, 5), (5, 5), (10, 5), (15, 4)]
PARTS = [4, 9, 14, 18]
AT_LAYER = {0: 0, 1: 1, 2: 2, -1: 3}


def bulk_kernel(groups, paired, sides, *refs):
    flags = end_flags(sides)
    layers = 2 * groups
    wholes, (y_first, y_second) = refs[:groups], refs[groups : groups + 2]
    out_pops, out_loads = refs[groups + 2 : groups + 4]
    held, placed, solid, passed, share = refs[groups + 4 :]
    targets = [0, 1, 2, layers - 1]
    store_ends(groups, paired, flags[0], y_first, y_second, held)
    block = [Block(wholes[g], held, g) for g in range(groups)]
    lane8 = iota((8, 128), 1)
    half = lane8 // 2

    def spread(rows):
        return jnp.concatenate([pick_lanes(rows, half), pick_lanes(rows, half + 64)], axis=1)

    cell_code = (2 * (iota((8, 256), 0) % 2) + iota((8, 256), 1) % 2).astype(F32)
    masks = []
    codes = [[block[g].bins(s, CODE) for g in range(groups)] for s in range(2)]
    for g in range(groups):
        wide = [spread(codes[s][g]) for s in range(2)]
        for i in range(2):
            masks.append([wide[s] == cell_code + 4.0 * i for s in range(2)])
    for field in range(36):
        rows = [[block[g].bins(s, field) for g in range(groups)] for s in range(2)]
        for g in range(groups):
            values = [spread(rows[s][g]) for s in range(2)]
            for i in range(2):
                placed[field, 2 * g + i] = choose(masks[2 * g + i], values)
    for layer in range(layers):
        spin = [placed[3 + c, layer] for c in range(3)]
        turned = cross(spin, [0.5 - placed[6 + c, layer] for c in range(3)])
        for c in range(3):
            placed[c, layer] = placed[c, layer] + turned[c]

    for n, target in enumerate(targets):
        total = None
        for kz in (-1, 0, 1):
            along_z = None
            for ky in (-1, 0, 1):
                along_y = None
                for kx in (-1, 0, 1):
                    source = (target - kx) % layers
                    weight = placed[E0 + 9 * (kx + 1) + 3 * (ky + 1) + kz + 1, source]
                    spin = [placed[3 + c, source] for c in range(3)]
                    base = [placed[c, source] for c in range(3)]
                    along_y = plus(along_y, deposit_terms(weight, base, spin, (kx, ky, kz)))
                along_z = plus(along_z, [roll(a, ky, 0) for a in along_y])
            total = plus(total, [roll(a, kz, 1) for a in along_z])
        for f in range(4):
            solid[f, n] = total[f]

    for n, target in enumerate(targets):
        g, i = target // 2, target % 2
        if n < 2:
            members = list(range(19))
        else:
            members = [m for m in range(19) if VELOCITIES[m][0] == (-1 if n == 2 else 1)]
        for t in range(2):
            tile = slice(128 * t, 128 * t + 128)
            f = [block[g].cells(member, i, t) for member in range(19)]
            done, forces = collide(f, [solid[c, n, :, tile] for c in range(4)], members)
            for c in range(3):
                share[c, n, :, tile] = forces[c]
            for m, value in done.items():
                passed[m, n, :, tile] = value
    for member in range(19):
        vector = VELOCITIES[member]
        for i in range(2):
            value = roll(passed[member, AT_LAYER[i - vector[0]]], vector[2], 1)
            value = roll(value, vector[1] - 2, 0)
            for t in range(2):
                out_pops[2 * member + i, 4 * t : 4 * t + 4, :] = value[
                    0:4, 128 * t : 128 * t + 128
                ]

    moments = [Moments() for _ in range(2)]
    for kz in (-1, 0, 1):
        across = [[roll(share[c, n], -kz, 1) for c in range(3)] for n in range(4)]
        for ky in (-1, 0, 1):
            near = [[roll(across[n][c], -ky, 0) for c in range(3)] for n in range(4)]
            for i in range(2):
                together = None
                for kx in (-1, 0, 1):
                    weight = placed[E0 + 9 * (kx + 1) + 3 * (ky + 1) + kz + 1, i]
                    forces = [weight * near[AT_LAYER[i + kx]][c] for c in range(3)]
                    together = plus(together, forces)
                    if kx:
                        moments[i].turn(0, forces, kx)
                moments[i].push(together)
                if ky:
                    moments[i].turn(1, together, ky)
                if kz:
                    moments[i].turn(2, together, kz)
    hydro = [moments[i].loads([placed[6 + c, i] for c in range(3)]) for i in range(2)]

    even = (2 * lane8) % 128
    inside = (lane8 > 0) & (lane8 < 127)
    for f in range(6):
        for s in range(2):
            value = jnp.where(masks[0][s], hydro[0][f], 0.0) + jnp.where(
                masks[1][s], hydro[1][f], 0.0
            )
            value = value + roll(value, -1, 0)
            value = value + roll(value, -1, 1)
            value = jnp.where(
                lane8 < 64, pick_lanes(value[:, :128], even), pick_lanes(value[:, 128:], even)
            )
            value = jnp.where(inside, value, 0.0)
            both = jnp.concatenate([value[2:3], value[4:5]], axis=0)
            out_loads[f, 2 * s : 2 * s + 2, :] = both


def side_kernel(groups, paired, sides, *refs):
    flags = end_flags(sides)
    layers = 2 * groups
    wholes, (y_first, y_second, z_first) = refs[:groups], refs[groups : groups + 3]
    out_contact, out_edge, out_state, held = refs[groups + 3 :]
    high = flags[1] == 1
    store_ends(groups, paired, flags[0], y_first, y_second, held)
    block = [Block(wholes[g], held, g) for g in range(groups)]
    lane8, row8 = iota((8, 128), 1), iota((8, 128), 0)
    inner = lane8 % 16
    z_near = jnp.where(inner < 8, jnp.maximum(inner - 4, 0), jnp.minimum(inner + 116, 127))
    z_bin = jnp.where(inner < 8, z_near // 2, jnp.minimum(inner + 244, 255) // 2)

    def at_edge(s, field):
        rows = [pick_lanes(block[g].bins(s, field), z_bin) for g in range(groups)]
        return by_group(groups, rows, lane8)

    tiles = [
        jnp.where(high, roll(z_first[tile], 10, 1), z_first[tile]) for tile in range(CONTACT_TILE)
    ]
    filled = end_lanes(high, inner)

    def store(field, value):
        halo = roll(tiles[field // 8], 2 - 2 * (field % 8), 1)
        out_edge[field] = jnp.where(filled, halo, value)

    edge_code = cell_codes(lane8, row8)
    codes = [at_edge(s, CODE) for s in range(2)]
    for s in range(2):
        out_edge[CODE_AT + s] = codes[s]
    edge_masks = [value == edge_code for value in codes]
    for field in range(36):
        store(field, choose(edge_masks, [at_edge(s, field) for s in range(2)]))
    for member in range(19):
        near_tiles = []
        for layer in range(layers):
            near = [block[layer // 2].cells(member, layer % 2, t) for t in range(2)]
            near_tiles.append(
                jnp.where(inner < 8, pick_lanes(near[0], z_near), pick_lanes(near[1], z_near))
            )
        store(POPS_AT + member, by_layer(groups, near_tiles, lane8))

    place, state = own_state(block[0])
    a_radius, a_speed = state[0], state[1:4]
    a_turn = [a_radius * value for value in state[4:7]]
    push, twist = None, None
    for oy in (-1, 0, 1):
        for g in range(groups):
            steps = [0] if g == 0 else []
            if g == 1:
                steps = steps + [1]
            if g == groups - 1:
                steps = steps + [-1]
            states = []
            for field in [CODE, 6, 7, 8, RADIUS, 0, 1, 2, 3, 4, 5]:
                values = []
                for s in range(2):
                    value = block[g].slot(s, field)
                    if oy < 0:
                        value = jnp.concatenate(
                            [block[g].halo_slot(0, s, field), value[0:1]], axis=0
                        )
                    if oy > 0:
                        value = jnp.concatenate(
                            [value[1:2], block[g].halo_slot(1, s, field)], axis=0
                        )
                    values.append(value)
                states.append(jnp.concatenate(values + values, axis=0))
            states = position(states[0], states[1:4]) + states[4:]
            for oz in (-1, 0, 1):
                other = [roll(value, -oz, 1) for value in states]
                keep = lane8 != (0 if oz < 0 else 127) if oz else None
                gap = [other[c] - place[c] for c in range(3)]
                gap[1], gap[2] = gap[1] + 2.0 * oy, gap[2] + 2.0 * oz
                for ox in steps:
                    apart = [gap[0] + 2.0 * ox, gap[1], gap[2]]
                    pushed, twisted = pair_force(
                        apart, a_radius, a_speed, a_turn, other[3:], keep
                    )
                    push, twist = plus(push, pushed), plus(twist, twisted)
    contact = [-value for value in push] + [-a_radius * value for value in twist]
    contact = [value + roll(value, -2, 0) for value in contact]

    ends = [jnp.where(high, 127, 0), jnp.where(high, 0, 127)]
    ends = [jnp.full((8, 128), end, jnp.int32) for end in ends]
    picked = [pick_lanes(value, ends[0]) for value in place + state]
    touch = end_contact(groups, z_first[CONTACT_TILE], high, picked)
    for f in range(6):
        out_contact[f] = contact[f] + touch[f]
    for q, value in enumerate(place + state):
        out_state[q] = pick_lanes(value, ends[1])


def edge_kernel(
    groups, paired, sides, bulk_pops, bulk_loads, bulk_contact, edge, state, second, *refs
):
    final_pops, final_loads, out_pops, out_loads, sems = refs
    high = end_flags(sides)[1] == 0
    lane, row = iota((8, 128), 1), iota((8, 128), 0)
    tiles = [roll(second[tile], 32, 1) if paired else second[tile] for tile in range(Z_TILES)]
    moved = [jnp.where(high, roll(tiles[tile], 10, 1), tiles[tile]) for tile in range(CONTACT_TILE)]
    filled = end_lanes(high, lane % 16)

    def value_of(field):
        halo = roll(moved[field // 8], 2 - 2 * (field % 8), 1)
        return jnp.where(filled, halo, edge[field])

    speed, spin, offset = [[value_of(3 * n + c) for c in range(3)] for n in range(3)]
    weights = [value_of(E0 + k) for k in range(27)]
    turned = cross(spin, [0.5 - value for value in offset])
    base = [speed[c] + turned[c] for c in range(3)]
    sums = None
    for kx in (-1, 0, 1):
        for kz in (-1, 0, 1):
            along = None
            for ky in (-1, 0, 1):
                weight = weights[9 * (kx + 1) + 3 * (ky + 1) + kz + 1]
                terms = deposit_terms(weight, base, spin, (kx, ky, kz))
                along = plus(along, [roll(a, ky, 0) for a in terms])
            sums = plus(sums, [roll(a, 16 * kx + kz, 1) for a in along])
    f = [value_of(POPS_AT + member) for member in range(19)]
    done, share = collide(f, sums, list(range(19)))

    lane4 = iota((4, 128), 1)
    copies = []
    for member in range(19):
        vector = VELOCITIES[member]
        value = roll(done[member], vector[1] - 2, 0)
        shift = 16 * vector[0] + vector[2]
        for i in range(2):
            for t in range(2):
                home = shift - 16 * i + (116 if t else -4)
                moved = roll(value, home, 1)[0:4]
                bulk = bulk_pops[2 * member + i, 4 * t : 4 * t + 4, :]
                mask = lane4 >= 126 if t else lane4 < 2
                out_pops[member, i, :, 128 * t : 128 * t + 128] = jnp.where(mask, moved, bulk)
        if member in PARTS:
            n = PARTS.index(member)
            part = pl.ds(PARTS[n - 1] + 1 if n else 0, member - (PARTS[n - 1] if n else -1))
            copy = pltpu.make_async_copy(out_pops.at[part], final_pops.at[part], sems.at[n])
            copy.start()
            copies.append(copy)

    moments = Moments()
    for kx in (-1, 0, 1):
        for kz in (-1, 0, 1):
            near = [roll(share[c], -16 * kx - kz, 1) for c in range(3)]
            together = None
            for ky in (-1, 0, 1):
                weight = weights[9 * (kx + 1) + 3 * (ky + 1) + kz + 1]
                forces = [weight * roll(near[c], -ky, 0) for c in range(3)]
                together = plus(together, forces)
                if ky:
                    moments.turn(1, forces, ky)
            moments.push(together)
            if kx:
                moments.turn(0, together, kx)
            if kz:
                moments.turn(2, together, kz)
    hydro = moments.loads(offset)

    touch = end_contact(groups, tiles[CONTACT_TILE], high, [state[q] for q in range(10)])
    ends = lane == 0, lane == 127
    masks = [edge[CODE_AT + s] == cell_codes(lane, row) for s in range(2)]
    for f in range(6):
        for s in range(2):
            value = jnp.where(masks[s], hydro[f], 0.0)
            value = value + roll(value, -16, 1)
            value = value + roll(value, -1, 0)
            value = value + roll(value, -1, 1)
            value = jnp.where(
                ends[0], roll(value, -4, 1), jnp.where(ends[1], roll(value, 117, 1), 0.0)
            )
            both = jnp.concatenate([value[2:3], value[4:5]], axis=0)
            both = both + touch[f][4 * s : 4 * s + 2] + bulk_contact[f, 4 * s : 4 * s + 2, :]
            out_loads[f, s, 0] = bulk_loads[f, 2 * s : 2 * s + 2, :] + both
    copy = pltpu.make_async_copy(out_loads, final_loads, sems.at[len(PARTS)])
    copy.start()
    for copy in copies + [copy]:
        copy.wait()


PARAMS = pltpu.CompilerParams(vmem_limit_bytes=32 * 2**20)


def call(kernel, operands, shapes, scratch=(), spaces=(pltpu.VMEM, pltpu.VMEM)):
    return pl.pallas_call(
        kernel,
        out_shape=[jax.ShapeDtypeStruct(shape, F32) for shape in shapes],
        in_specs=[pl.BlockSpec(memory_space=spaces[0])] * len(operands),
        out_specs=[pl.BlockSpec(memory_space=spaces[1])] * len(shapes),
        scratch_shapes=[pltpu.VMEM(x, F32) if isinstance(x, tuple) else x for x in scratch],
        compiler_params=PARAMS,
    )(*operands)


def step(paired, sizes, *blocks):
    nx, ny, nz = sizes
    axes = ("gx", "gy", "gz")
    groups = 2 if paired else 3

    def permute(value, target):
        pairs = []
        for x in range(nx):
            for y in range(ny):
                for z in range(nz):
                    tx, ty, tz = target(x, y, z)
                    there = ((tx % nx) * ny + ty % ny) * nz + tz % nz
                    pairs.append(((x * ny + y) * nz + z, there))
        return lax.ppermute(value, axes, pairs)

    def swap(value):
        return permute(value, lambda x, y, z: (1 - x, y, z))

    def to_low(value):
        return permute(value, lambda x, y, z: (x - 1, y, z))

    def to_high(value):
        return permute(value, lambda x, y, z: (x + 1, y, z))

    ends_y = (Y_BLOCKS, 8, 128)
    shape_z = (Z_TILES, 8, 128)
    shape_y = (groups,) + ends_y
    sides = None if paired else (1, 1)
    held = [pltpu.VMEM(block.shape, block.dtype) for block in blocks]
    held[0] = pltpu.VMEM((22,) + blocks[0].shape[1:], F32)
    blocks = [pltpu.with_memory_space_constraint(block, pltpu.HBM) for block in blocks]
    whole, mine, theirs = call(
        functools.partial(pack_kernel, sides),
        blocks,
        [(W_BLOCKS, 8, 128), shape_y, ends_y],
        held + [pltpu.SemaphoreType.DMA((6 + len(POPS_PARTS),))],
        (pltpu.HBM, pltpu.VMEM),
    )

    def pack_z(sides, wholes, halos):
        kernel = functools.partial(z_pack_kernel, groups, paired, sides)
        return call(kernel, wholes + halos, [shape_z], [(2,) + shape_y])[0]

    def pack_bulk(wholes, halos):
        scratch = [
            (2,) + shape_y,
            (36, 2 * groups, 8, 256),
            (4, 4, 8, 256),
            (19, 4, 8, 256),
            (3, 4, 8, 256),
        ]
        return call(
            functools.partial(bulk_kernel, groups, paired, sides),
            wholes + halos,
            [(W_GRAIN, 8, 128), (6, 4, 128)],
            scratch,
        )

    if paired:
        rows = mine.at[1].set(swap(theirs))
        wholes = [whole, swap(whole)]
        first = permute(rows, lambda x, y, z: (x, y + (1 if (x + y) % 2 == 0 else -1), z))
        halos = [first, swap(first)]
        first = permute(
            pack_z(sides, wholes, halos),
            lambda x, y, z: (x, y, z + (1 if (x + z) % 2 == 0 else -1)),
        )
        bulk = pack_bulk(wholes, halos)
        first, bulk = lax.optimization_barrier((first, bulk))
        ends = [first, swap(first)]
    else:
        wholes = [whole, to_low(whole), to_high(whole)]
        up, down = [jnp.stack([v, to_low(v), to_high(v)]) for v in (mine[0], theirs)]
        halos = [
            permute(down, lambda x, y, z: (x, y - 1, z)),
            permute(up, lambda x, y, z: (x, y + 1, z)),
        ]
        low = (1, 0)
        ends = [
            permute(pack_z(low, wholes, halos), lambda x, y, z: (x, y, z - 1)),
            permute(pack_z(sides, wholes, halos), lambda x, y, z: (x, y, z + 1)),
        ]
        bulk = pack_bulk(wholes, halos)
    side = call(
        functools.partial(side_kernel, groups, paired, sides),
        wholes + halos + ends[:1],
        [(6, 8, 128), (EDGE_VALUES, 8, 128), (10, 8, 128)],
        [(2,) + shape_y],
    )
    populations, offset = blocks[0], blocks[2]
    shapes = [populations.shape, (6,) + offset.shape[1:]]
    return tuple(
        call(
            functools.partial(edge_kernel, groups, paired, sides),
            list(bulk) + list(side) + ends[1:],
            shapes,
            shapes + [pltpu.SemaphoreType.DMA((len(PARTS) + 1,))],
            (pltpu.VMEM, pltpu.HBM),
        )
    )


def solution(mesh, paired=None):
    sizes = tuple(mesh.shape[axis] for axis in ("gx", "gy", "gz"))
    if paired is None:
        paired = sizes[0] == 2 and sizes[1] % 2 == 0 and sizes[2] % 2 == 0
    cells, bins = P(None, "gx", "gy", "gz"), P(None, None, "gx", "gy", "gz")
    return jax.shard_map(
        functools.partial(step, paired, sizes),
        mesh=mesh,
        in_specs=(cells, cells, bins, cells, bins, bins, bins),
        out_specs=(cells, bins),
        check_vma=False,
    )
```

```python
import functools

import jax
import jax.numpy as jnp
from jax import lax
from jax.experimental import pallas as pl
from jax.experimental.pallas import tpu as pltpu
from jax.sharding import PartitionSpec as P

VELOCITIES = [
    (0, 0, 0),
    (1, 0, 0),
    (-1, 0, 0),
    (0, 1, 0),
    (0, -1, 0),
    (0, 0, 1),
    (0, 0, -1),
    (1, 1, 0),
    (-1, -1, 0),
    (1, -1, 0),
    (-1, 1, 0),
    (1, 0, 1),
    (-1, 0, -1),
    (1, 0, -1),
    (-1, 0, 1),
    (0, 1, 1),
    (0, -1, -1),
    (0, 1, -1),
    (0, -1, 1),
]
WEIGHTS = [1.0 / 3.0] + [1.0 / 18.0] * 6 + [1.0 / 36.0] * 12
relax_time = 0.8
fraction_floor = 0.1
distance_floor = 0.5

E0, RADIUS, CODE, PLACE = 9, 36, 37, 38
POPS_AT, CODE_AT, EDGE_VALUES = 36, 55, 57
Z_TILES, CONTACT_TILE = 8, 7
Y_FIELDS = list(range(9)) + [RADIUS, CODE]
Y_MEMBERS = [m for m in range(19) if VELOCITIES[m][1]] + [19, 20, 21]
Y_STANDS = {0: 10, 1: 11, 5: 12}
Y_GRAIN, Y_BLOCKS = 52, 14
W_GRAIN, W_BLOCKS = 38, 57
F32 = jnp.float32


def end_flags(sides):
    if sides is not None:
        return sides
    ix, iy, iz = [lax.axis_index(axis) for axis in ("gx", "gy", "gz")]
    return 1 - lax.rem(ix + iy, 2), 1 - lax.rem(ix + iz, 2)


def iota(shape, dim):
    return lax.broadcasted_iota(jnp.int32, shape, dim)


def pick_lanes(values, index):
    return jnp.take_along_axis(values, index, axis=1, mode="promise_in_bounds")


def roll(values, shift, axis):
    size = values.shape[axis]
    return pltpu.roll(values, shift % size, axis) if shift % size else values


def cross(a, b):
    return [
        a[1] * b[2] - a[2] * b[1],
        a[2] * b[0] - a[0] * b[2],
        a[0] * b[1] - a[1] * b[0],
    ]


def pack_kernel(sides, *refs):
    flags = end_flags(sides)
    sources, (whole, mine, theirs), held, sems = refs[:7], refs[7:10], refs[10:17], refs[17]
    copies = [
        pltpu.make_async_copy(source, target, sems.at[n])
        for n, (source, target) in enumerate(zip(sources[1:], held[1:]))
    ]
    for n, part in enumerate(POPS_PARTS):
        part = pl.ds(*part)
        copies.append(pltpu.make_async_copy(sources[0].at[part], held[0].at[part], sems.at[6 + n]))
    for copy in copies:
        copy.start()
    pops, cell, off, rad, vel, spin, inter = held
    for copy in copies[:6]:
        copy.wait()

    def slot(s, field, rows=slice(None)):
        if field < 3:
            return vel[field, s, 0, rows, :]
        if field < 6:
            return spin[field - 3, s, 0, rows, :]
        if field < 9:
            return off[field - 6, s, 0, rows, :]
        if field < RADIUS:
            return inter[field - E0, s, 0, rows, :]
        if field == RADIUS:
            return rad[s, 0, rows, :]
        return cell[s, 0, rows, :].astype(F32)

    for field in range(38):
        for s in range(2):
            at = 4 * (field % 2) + 2 * s
            whole[W_GRAIN + field // 2, at : at + 2, :] = slot(s, field)
    for out, end in ((mine.at[0], flags[0]), (theirs, 1 - flags[0])):
        for s in range(2):
            for f in range(29):
                if f < 11:
                    value = slot(s, Y_FIELDS[f], pl.ds(end, 1))
                else:
                    kx, q, kz = (f - 11) // 6, (f - 11) // 3 % 2, (f - 11) % 3
                    value = inter[9 * kx + 3 * (q + end) + kz, s, 0, pl.ds(end, 1), :]
                r = Y_GRAIN + 2 * f + s
                out[r // 8, r % 8 : r % 8 + 1, :] = value
        out[Y_BLOCKS - 1, 6:8, :] = jnp.zeros((2, 128), F32)
    for copy in copies[6:]:
        copy.wait()
    still = [m for m in range(19) if not VELOCITIES[m][1]]
    for i in range(2):
        sums = []
        for c in (0, 2):
            rising = [pops[m, i] for m in still if VELOCITIES[m][c] > 0]
            falling = [pops[m, i] for m in still if VELOCITIES[m][c] < 0]
            sums.append(sum(rising[1:], rising[0]) - sum(falling[1:], falling[0]))
        total = sum([pops[m, i] for m in still[1:]], pops[0, i])
        pops[19, i] = total - sums[0] - sums[1]
        pops[20, i] = sums[0]
        pops[21, i] = sums[1]
    for out, end in ((mine.at[0], flags[0]), (theirs, 1 - flags[0])):
        for n, member in enumerate(Y_MEMBERS):
            for i in range(2):
                row = pops[member, i, pl.ds(3 * end, 1), :]
                for t in range(2):
                    r = 4 * n + 2 * i + t
                    out[r // 8, r % 8 : r % 8 + 1, :] = row[:, 128 * t : 128 * t + 128]
    for member in range(19):
        for i in range(2):
            for t in range(2):
                tile = pops[member, i, :, 128 * t : 128 * t + 128]
                whole[2 * member + i, 4 * t : 4 * t + 4, :] = tile


class Block:
    def __init__(self, whole, halos, group):
        self.whole, self.halos, self.group = whole, halos, group

    def slot(self, s, field):
        at = 4 * (field % 2) + 2 * s
        return self.whole[W_GRAIN + field // 2, at : at + 2, :]

    def pops(self, member, i, t):
        return self.whole[2 * member + i, 4 * t : 4 * t + 4, :]

    def halo_pops(self, end, member, i, t):
        if VELOCITIES[member][1]:
            n = Y_MEMBERS.index(member)
        elif member in Y_STANDS:
            n = Y_STANDS[member]
        else:
            return jnp.zeros((1, 128), F32)
        r = 4 * n + 2 * i + t
        return self.halos[end, self.group, r // 8, r % 8 : r % 8 + 1, :]

    def halo_slot(self, end, s, field):
        if field in Y_FIELDS:
            f = Y_FIELDS.index(field)
        else:
            k = field - E0
            q = k // 3 % 3 - (1 - end)
            if q not in (0, 1):
                return jnp.zeros((1, 128), F32)
            f = 11 + 6 * (k // 9) + 3 * q + k % 3
        r = Y_GRAIN + 2 * f + s
        return self.halos[end, self.group, r // 8, r % 8 : r % 8 + 1, :]

    def bins(self, s, field):
        row = iota((8, 128), 0)
        n, at = W_GRAIN + field // 2, 4 * (field % 2) + 2 * s
        rows = [
            self.halo_slot(0, s, field),
            self.whole[n, at : at + 1, :],
            self.whole[n, at + 1 : at + 2, :],
            self.halo_slot(1, s, field),
        ]
        rows = [jnp.broadcast_to(value, (8, 128)) for value in rows]
        return jnp.where(
            row < 4,
            jnp.where(row < 2, rows[0], rows[1]),
            jnp.where(row < 6, rows[2], rows[3]),
        )

    def cells(self, member, i, t):
        row = iota((8, 128), 0)
        own = self.whole[2 * member + i]
        if isinstance(t, int):
            own = roll(own, 2 - 4 * t, 0)
            low, high = [self.halo_pops(end, member, i, t) for end in range(2)]
        else:
            own = jnp.where(t, roll(own, -2, 0), roll(own, 2, 0))
            low, high = [
                jnp.where(
                    t, self.halo_pops(end, member, i, 1), self.halo_pops(end, member, i, 0)
                )
                for end in range(2)
            ]
        low, high = jnp.broadcast_to(low, (8, 128)), jnp.broadcast_to(high, (8, 128))
        return jnp.where(row < 2, low, jnp.where(row > 5, high, own))


def position(code, offset):
    first = jnp.floor(code * 0.25)
    rest = code - 4.0 * first
    second = jnp.floor(rest * 0.5)
    corner = [first, second, rest - 2.0 * second]
    return [corner[c] + offset[c] for c in range(3)]


def store_ends(groups, paired, side, first, second, held):
    for g in range(groups):
        held[side, g] = first[g]
        held[1 - side, g] = second[(g + 1) % 2 if paired else g]


def lane_groups(groups):
    return [0, 1, 0, 1] if groups == 2 else [0, 1, 1, 2]


def by_group(groups, values, lane):
    order = lane_groups(groups)
    result = values[order[3]]
    for q in (2, 1, 0):
        if order[q] != order[q + 1] or q < 2:
            result = jnp.where(lane < 32 * (q + 1), values[order[q]], result)
    return result


def by_layer(groups, values, lane):
    odd = lane // 16 % 2 == 1
    pairs = [jnp.where(odd, values[2 * g + 1], values[2 * g]) for g in range(groups)]
    return by_group(groups, pairs, lane)


def cell_codes(lane, row):
    return (4 * (lane // 16 % 2) + 2 * (row % 2) + lane % 2).astype(F32)


def choose(masks, values):
    return jnp.where(masks[0], values[0], jnp.where(masks[1], values[1], 0.0))


def z_pack_kernel(groups, paired, sides, *refs):
    flags = end_flags(sides)
    wholes, (first, second, out, held) = refs[:groups], refs[groups:]
    store_ends(groups, paired, flags[0], first, second, held)
    high = flags[1] == 1
    lane, row = iota((8, 128), 1), iota((8, 128), 0)
    block = [Block(wholes[g], held, g) for g in range(groups)]
    start = jnp.where(high, 127, 0)
    index = jnp.full((8, 128), start, jnp.int32)
    pops_index = jnp.full((8, 128), jnp.where(high, 126, 0), jnp.int32) + lane % 2
    inner = lane % 16 // 2

    def picked(s, field):
        values = [pick_lanes(block[g].bins(s, field), index) for g in range(groups)]
        return by_group(groups, values, lane)

    slots = [[picked(s, field) for field in range(38)] for s in range(2)]
    code = cell_codes(lane, row)
    masks = [slots[s][CODE] == code for s in range(2)]
    values = [choose(masks, [slots[0][f], slots[1][f]]) for f in range(36)]
    for member in range(19):
        tiles = []
        for layer in range(2 * groups):
            g, i = layer // 2, layer % 2
            tile = block[g].cells(member, i, high)
            tiles.append(pick_lanes(tile, pops_index))
        values.append(by_layer(groups, tiles, lane))
    tiles_out = []
    for tile in range(CONTACT_TILE):
        packed = values[8 * tile]
        for q in range(1, 8):
            if 8 * tile + q < len(values):
                packed = jnp.where(inner == q, values[8 * tile + q], packed)
        tiles_out.append(packed)
    packed = jnp.zeros((8, 128), F32)
    for s in range(2):
        state = position(slots[s][CODE], slots[s][6:9]) + [slots[s][RADIUS]] + slots[s][0:6]
        for q, value in enumerate(state):
            packed = jnp.where(lane % 32 == 16 * s + q, value, packed)
    tiles_out.append(packed)
    if paired:
        tiles_out = [
            jnp.where(lane < 64, tiles_out[2 * n], tiles_out[2 * n + 1])
            for n in range(Z_TILES // 2)
        ]
    for n, value in enumerate(tiles_out):
        out[n] = value


def dot_lattice(vector, velocity):
    total = None
    for c in range(3):
        if vector[c]:
            if total is None:
                total = velocity[c] if vector[c] > 0 else -velocity[c]
            else:
                total = total + velocity[c] if vector[c] > 0 else total - velocity[c]
    return total


def equilibrium_base(velocity):
    return 1.0 - 1.5 * (
        velocity[0] * velocity[0] + velocity[1] * velocity[1] + velocity[2] * velocity[2]
    )


def collide(f, sums, members):
    fraction = 1.0 - jnp.exp(-sums[0])
    excess = relax_time - 0.5
    weight = fraction * excess / (1.0 - fraction + excess)
    inverse = 1.0 / jnp.maximum(sums[0], fraction_floor)
    solid_velocity = [sums[1 + c] * inverse for c in range(3)]
    density = sum(f[1:], f[0])
    momentum = []
    for c in range(3):
        plus = [f[m] for m in range(19) if VELOCITIES[m][c] > 0]
        minus = [f[m] for m in range(19) if VELOCITIES[m][c] < 0]
        momentum.append(sum(plus[1:], plus[0]) - sum(minus[1:], minus[0]))
    per_density = 1.0 / density
    fluid_velocity = [momentum[c] * per_density for c in range(3)]
    share = [weight * inverse * (momentum[c] - density * solid_velocity[c]) for c in range(3)]
    relax = (1.0 - weight) * (1.0 / relax_time)
    keep = 1.0 - relax
    fluid_base = equilibrium_base(fluid_velocity)
    solid_base = equilibrium_base(solid_velocity)
    done = {}
    for member in [0] + list(range(1, 19, 2)):
        reverse = member + 1 if member else 0
        if member not in members and reverse not in members:
            continue
        part = WEIGHTS[member] * density
        if member == 0:
            fluid = [part * fluid_base] * 2
            settled = [part * solid_base] * 2
        else:
            ends = []
            for base, velocity in (
                (fluid_base, fluid_velocity),
                (solid_base, solid_velocity),
            ):
                along = dot_lattice(VELOCITIES[member], velocity)
                even = base + 4.5 * along * along
                odd = 3.0 * along
                ends.append([part * (even + odd), part * (even - odd)])
            fluid, settled = ends
        pair = [f[member], f[reverse]]
        for way, m in enumerate((member, reverse)[: 2 if member else 1]):
            if m in members:
                exchange = (pair[1 - way] - fluid[1 - way]) - (pair[way] - settled[way])
                done[m] = keep * pair[way] + relax * fluid[way] + weight * exchange
    return done, share


def deposit_terms(weight, base, spin, k):
    terms = [weight]
    for c in range(3):
        u, v = (c + 1) % 3, (c + 2) % 3
        speed = base[c]
        if k[v]:
            speed = speed + spin[u] if k[v] > 0 else speed - spin[u]
        if k[u]:
            speed = speed - spin[v] if k[u] > 0 else speed + spin[v]
        terms.append(weight * speed)
    return terms


def plus(totals, terms):
    return list(terms) if totals is None else [a + b for a, b in zip(totals, terms)]


class Moments:
    def __init__(self):
        self.force, self.moment = [None] * 3, [None] * 3

    def add(self, store, c, value, sign):
        if store[c] is None:
            store[c] = value if sign > 0 else -value
        else:
            store[c] = store[c] + value if sign > 0 else store[c] - value

    def turn(self, axis, forces, sign):
        u, v = (axis + 1) % 3, (axis + 2) % 3
        self.add(self.moment, v, forces[u], sign)
        self.add(self.moment, u, forces[v], -sign)

    def push(self, forces):
        for c in range(3):
            self.add(self.force, c, forces[c], 1)

    def loads(self, offset):
        turned = cross([0.5 - value for value in offset], self.force)
        return self.force + [self.moment[c] + turned[c] for c in range(3)]


def pair_force(gap, a_radius, a_speed, a_turn, other, keep=None):
    b_radius = other[0]
    distance = jnp.sqrt(gap[0] * gap[0] + gap[1] * gap[1] + gap[2] * gap[2])
    scale = 1.0 / jnp.maximum(distance, distance_floor)
    normal = [gap[c] * scale for c in range(3)]
    depth = jnp.maximum(a_radius + b_radius - distance, 0.0)
    strength = a_radius * b_radius * depth
    if keep is not None:
        strength = jnp.where(keep, strength, 0.0)
    turning = [a_turn[c] + b_radius * other[4 + c] for c in range(3)]
    swing = cross(turning, normal)
    relative = [a_speed[c] - other[1 + c] + swing[c] for c in range(3)]
    along = relative[0] * normal[0] + relative[1] * normal[1] + relative[2] * normal[2]
    factor = 1.0 + along
    pushed = [strength * (factor * normal[c] + relative[c]) for c in range(3)]
    return pushed, cross(normal, pushed)


def own_state(block):
    def rows(field):
        values = [block.slot(s, field) for s in range(2)]
        return jnp.concatenate([values[0], values[0], values[1], values[1]], axis=0)

    place = position(rows(CODE), [rows(6 + c) for c in range(3)])
    return place, [rows(RADIUS)] + [rows(c) for c in range(6)]


def z_tiles(paired, sent):
    if not paired:
        return [sent[tile] for tile in range(Z_TILES)]
    left = iota((8, 128), 1) < 64
    tiles = []
    for n in range(Z_TILES // 2):
        turned = roll(sent[n], 64, 1)
        tiles += [jnp.where(left, sent[n], turned), jnp.where(left, turned, sent[n])]
    return tiles


def end_lanes(high, inner):
    start = jnp.where(high, 12, 2)
    return (inner == start) | (inner == start + 1)


def end_contact(groups, tile, high, state):
    lane = iota((8, 128), 1)
    step_x, step_y = lane % 16 - 1, lane // 16 - 1
    place, a_radius, a_speed, a_spin = state[0:3], state[3], state[4:7], state[7:10]
    a_turn = [a_radius * value for value in a_spin]
    before = lane_groups(groups).index(groups - 1)
    run = 32 * jnp.where(step_x < 0, before, jnp.where(step_x == 0, 0, 1))
    other = [None] * 10
    for oy in (-1, 0, 1):
        at = 2 * (oy + 1)
        rows = jnp.concatenate([tile[at : at + 1], tile[at + 2 : at + 3]], axis=0)
        moved = roll(rows, -16, 1)
        rows = jnp.concatenate([rows, moved, rows, moved], axis=0)
        for q in range(10):
            value = pick_lanes(rows, run + q)
            other[q] = value if oy < 0 else jnp.where(step_y == oy, value, other[q])
    keep = (step_x < 2) & (step_y < 2)
    gap = [
        other[0] - place[0] + (2 * step_x).astype(F32),
        other[1] - place[1] + (2 * step_y).astype(F32),
        other[2] - place[2] + jnp.where(high, 2.0, -2.0),
    ]
    pushed, twisted = pair_force(gap, a_radius, a_speed, a_turn, other[3:], keep)
    contact = [-value for value in pushed] + [-a_radius * value for value in twisted]
    end = lane == jnp.where(high, 127, 0)
    result = []
    for value in contact:
        value = value + roll(value, -2, 0)
        value = value + roll(value, -1, 1) + roll(value, -2, 1)
        value = value + roll(value, -16, 1) + roll(value, -32, 1)
        result.append(jnp.where(end, jnp.where(high, roll(value, 127, 1), value), 0.0))
    return result


POPS_PARTS = [(0, 5), (5, 5), (10, 5), (15, 4)]
PARTS = [4, 9, 14, 18]
AT_LAYER = {0: 0, 1: 1, 2: 2, -1: 3}


def bulk_kernel(groups, paired, sides, *refs):
    flags = end_flags(sides)
    layers = 2 * groups
    wholes, (y_first, y_second) = refs[:groups], refs[groups : groups + 2]
    out_pops, out_loads = refs[groups + 2 : groups + 4]
    held, placed, solid, passed, share = refs[groups + 4 :]
    targets = [0, 1, 2, layers - 1]
    store_ends(groups, paired, flags[0], y_first, y_second, held)
    block = [Block(wholes[g], held, g) for g in range(groups)]
    lane8 = iota((8, 128), 1)
    half = lane8 // 2

    def spread(rows):
        return jnp.concatenate([pick_lanes(rows, half), pick_lanes(rows, half + 64)], axis=1)

    cell_code = (2 * (iota((8, 256), 0) % 2) + iota((8, 256), 1) % 2).astype(F32)
    masks = []
    codes = [[block[g].bins(s, CODE) for g in range(groups)] for s in range(2)]
    for g in range(groups):
        wide = [spread(codes[s][g]) for s in range(2)]
        for i in range(2):
            masks.append([wide[s] == cell_code + 4.0 * i for s in range(2)])
    for field in range(36):
        rows = [[block[g].bins(s, field) for g in range(groups)] for s in range(2)]
        for g in range(groups):
            values = [spread(rows[s][g]) for s in range(2)]
            for i in range(2):
                placed[field, 2 * g + i] = choose(masks[2 * g + i], values)
    for layer in range(layers):
        spin = [placed[3 + c, layer] for c in range(3)]
        turned = cross(spin, [0.5 - placed[6 + c, layer] for c in range(3)])
        for c in range(3):
            placed[c, layer] = placed[c, layer] + turned[c]

    for n, target in enumerate(targets):
        total = None
        for kz in (-1, 0, 1):
            along_z = None
            for ky in (-1, 0, 1):
                along_y = None
                for kx in (-1, 0, 1):
                    source = (target - kx) % layers
                    weight = placed[E0 + 9 * (kx + 1) + 3 * (ky + 1) + kz + 1, source]
                    spin = [placed[3 + c, source] for c in range(3)]
                    base = [placed[c, source] for c in range(3)]
                    along_y = plus(along_y, deposit_terms(weight, base, spin, (kx, ky, kz)))
                along_z = plus(along_z, [roll(a, ky, 0) for a in along_y])
            total = plus(total, [roll(a, kz, 1) for a in along_z])
        for f in range(4):
            solid[f, n] = total[f]

    for n, target in enumerate(targets):
        g, i = target // 2, target % 2
        if n < 2:
            members = list(range(19))
        else:
            members = [m for m in range(19) if VELOCITIES[m][0] == (-1 if n == 2 else 1)]
        for t in range(2):
            tile = slice(128 * t, 128 * t + 128)
            f = [block[g].cells(member, i, t) for member in range(19)]
            done, forces = collide(f, [solid[c, n, :, tile] for c in range(4)], members)
            for c in range(3):
                share[c, n, :, tile] = forces[c]
            for m, value in done.items():
                passed[m, n, :, tile] = value
    for member in range(19):
        vector = VELOCITIES[member]
        for i in range(2):
            value = roll(passed[member, AT_LAYER[i - vector[0]]], vector[2], 1)
            value = roll(value, vector[1] - 2, 0)
            for t in range(2):
                out_pops[2 * member + i, 4 * t : 4 * t + 4, :] = value[
                    0:4, 128 * t : 128 * t + 128
                ]

    moments = [Moments() for _ in range(2)]
    for kz in (-1, 0, 1):
        across = [[roll(share[c, n], -kz, 1) for c in range(3)] for n in range(4)]
        for ky in (-1, 0, 1):
            near = [[roll(across[n][c], -ky, 0) for c in range(3)] for n in range(4)]
            for i in range(2):
                together = None
                for kx in (-1, 0, 1):
                    weight = placed[E0 + 9 * (kx + 1) + 3 * (ky + 1) + kz + 1, i]
                    forces = [weight * near[AT_LAYER[i + kx]][c] for c in range(3)]
                    together = plus(together, forces)
                    if kx:
                        moments[i].turn(0, forces, kx)
                moments[i].push(together)
                if ky:
                    moments[i].turn(1, together, ky)
                if kz:
                    moments[i].turn(2, together, kz)
    hydro = [moments[i].loads([placed[6 + c, i] for c in range(3)]) for i in range(2)]

    even = (2 * lane8) % 128
    inside = (lane8 > 0) & (lane8 < 127)
    for f in range(6):
        for s in range(2):
            value = jnp.where(masks[0][s], hydro[0][f], 0.0) + jnp.where(
                masks[1][s], hydro[1][f], 0.0
            )
            value = value + roll(value, -1, 0)
            value = value + roll(value, -1, 1)
            value = jnp.where(
                lane8 < 64, pick_lanes(value[:, :128], even), pick_lanes(value[:, 128:], even)
            )
            value = jnp.where(inside, value, 0.0)
            both = jnp.concatenate([value[2:3], value[4:5]], axis=0)
            out_loads[f, 2 * s : 2 * s + 2, :] = both


def side_kernel(groups, paired, sides, *refs):
    flags = end_flags(sides)
    layers = 2 * groups
    wholes, (y_first, y_second, z_first) = refs[:groups], refs[groups : groups + 3]
    out_contact, out_edge, out_state, held = refs[groups + 3 :]
    high = flags[1] == 1
    store_ends(groups, paired, flags[0], y_first, y_second, held)
    block = [Block(wholes[g], held, g) for g in range(groups)]
    lane8, row8 = iota((8, 128), 1), iota((8, 128), 0)
    inner = lane8 % 16
    z_near = jnp.where(inner < 8, jnp.maximum(inner - 4, 0), jnp.minimum(inner + 116, 127))
    z_bin = jnp.where(inner < 8, z_near // 2, jnp.minimum(inner + 244, 255) // 2)

    def at_edge(s, field):
        rows = [pick_lanes(block[g].bins(s, field), z_bin) for g in range(groups)]
        return by_group(groups, rows, lane8)

    halo_tiles = z_tiles(paired, z_first)
    tiles = [
        jnp.where(high, roll(halo_tiles[tile], 10, 1), halo_tiles[tile])
        for tile in range(CONTACT_TILE)
    ]
    filled = end_lanes(high, inner)

    def store(field, value):
        halo = roll(tiles[field // 8], 2 - 2 * (field % 8), 1)
        out_edge[field] = jnp.where(filled, halo, value)

    edge_code = cell_codes(lane8, row8)
    codes = [at_edge(s, CODE) for s in range(2)]
    for s in range(2):
        out_edge[CODE_AT + s] = codes[s]
    edge_masks = [value == edge_code for value in codes]
    for field in range(36):
        store(field, choose(edge_masks, [at_edge(s, field) for s in range(2)]))
    for member in range(19):
        near_tiles = []
        for layer in range(layers):
            near = [block[layer // 2].cells(member, layer % 2, t) for t in range(2)]
            near_tiles.append(
                jnp.where(inner < 8, pick_lanes(near[0], z_near), pick_lanes(near[1], z_near))
            )
        store(POPS_AT + member, by_layer(groups, near_tiles, lane8))

    place, state = own_state(block[0])
    a_radius, a_speed = state[0], state[1:4]
    a_turn = [a_radius * value for value in state[4:7]]
    push, twist = None, None
    for oy in (-1, 0, 1):
        for g in range(groups):
            steps = [0] if g == 0 else []
            if g == 1:
                steps = steps + [1]
            if g == groups - 1:
                steps = steps + [-1]
            states = []
            for field in [CODE, 6, 7, 8, RADIUS, 0, 1, 2, 3, 4, 5]:
                values = []
                for s in range(2):
                    value = block[g].slot(s, field)
                    if oy < 0:
                        value = jnp.concatenate(
                            [block[g].halo_slot(0, s, field), value[0:1]], axis=0
                        )
                    if oy > 0:
                        value = jnp.concatenate(
                            [value[1:2], block[g].halo_slot(1, s, field)], axis=0
                        )
                    values.append(value)
                states.append(jnp.concatenate(values + values, axis=0))
            states = position(states[0], states[1:4]) + states[4:]
            for oz in (-1, 0, 1):
                other = [roll(value, -oz, 1) for value in states]
                keep = lane8 != (0 if oz < 0 else 127) if oz else None
                gap = [other[c] - place[c] for c in range(3)]
                gap[1], gap[2] = gap[1] + 2.0 * oy, gap[2] + 2.0 * oz
                for ox in steps:
                    apart = [gap[0] + 2.0 * ox, gap[1], gap[2]]
                    pushed, twisted = pair_force(
                        apart, a_radius, a_speed, a_turn, other[3:], keep
                    )
                    push, twist = plus(push, pushed), plus(twist, twisted)
    contact = [-value for value in push] + [-a_radius * value for value in twist]
    contact = [value + roll(value, -2, 0) for value in contact]

    ends = [jnp.where(high, 127, 0), jnp.where(high, 0, 127)]
    ends = [jnp.full((8, 128), end, jnp.int32) for end in ends]
    picked = [pick_lanes(value, ends[0]) for value in place + state]
    touch = end_contact(groups, halo_tiles[CONTACT_TILE], high, picked)
    for f in range(6):
        out_contact[f] = contact[f] + touch[f]
    for q, value in enumerate(place + state):
        out_state[q] = pick_lanes(value, ends[1])


def edge_kernel(
    groups, paired, sides, bulk_pops, bulk_loads, bulk_contact, edge, state, second, *refs
):
    final_pops, final_loads, out_pops, out_loads, sems = refs
    high = end_flags(sides)[1] == 0
    lane, row = iota((8, 128), 1), iota((8, 128), 0)
    tiles = [roll(value, 32, 1) if paired else value for value in z_tiles(paired, second)]
    moved = [jnp.where(high, roll(tiles[tile], 10, 1), tiles[tile]) for tile in range(CONTACT_TILE)]
    filled = end_lanes(high, lane % 16)

    def value_of(field):
        halo = roll(moved[field // 8], 2 - 2 * (field % 8), 1)
        return jnp.where(filled, halo, edge[field])

    speed, spin, offset = [[value_of(3 * n + c) for c in range(3)] for n in range(3)]
    weights = [value_of(E0 + k) for k in range(27)]
    turned = cross(spin, [0.5 - value for value in offset])
    base = [speed[c] + turned[c] for c in range(3)]
    sums = None
    for kx in (-1, 0, 1):
        for kz in (-1, 0, 1):
            along = None
            for ky in (-1, 0, 1):
                weight = weights[9 * (kx + 1) + 3 * (ky + 1) + kz + 1]
                terms = deposit_terms(weight, base, spin, (kx, ky, kz))
                along = plus(along, [roll(a, ky, 0) for a in terms])
            sums = plus(sums, [roll(a, 16 * kx + kz, 1) for a in along])
    f = [value_of(POPS_AT + member) for member in range(19)]
    done, share = collide(f, sums, list(range(19)))

    lane4 = iota((4, 128), 1)
    copies = []
    for member in range(19):
        vector = VELOCITIES[member]
        value = roll(done[member], vector[1] - 2, 0)
        shift = 16 * vector[0] + vector[2]
        for i in range(2):
            for t in range(2):
                home = shift - 16 * i + (116 if t else -4)
                moved = roll(value, home, 1)[0:4]
                bulk = bulk_pops[2 * member + i, 4 * t : 4 * t + 4, :]
                mask = lane4 >= 126 if t else lane4 < 2
                out_pops[member, i, :, 128 * t : 128 * t + 128] = jnp.where(mask, moved, bulk)
        if member in PARTS:
            n = PARTS.index(member)
            part = pl.ds(PARTS[n - 1] + 1 if n else 0, member - (PARTS[n - 1] if n else -1))
            copy = pltpu.make_async_copy(out_pops.at[part], final_pops.at[part], sems.at[n])
            copy.start()
            copies.append(copy)

    moments = Moments()
    for kx in (-1, 0, 1):
        for kz in (-1, 0, 1):
            near = [roll(share[c], -16 * kx - kz, 1) for c in range(3)]
            together = None
            for ky in (-1, 0, 1):
                weight = weights[9 * (kx + 1) + 3 * (ky + 1) + kz + 1]
                forces = [weight * roll(near[c], -ky, 0) for c in range(3)]
                together = plus(together, forces)
                if ky:
                    moments.turn(1, forces, ky)
            moments.push(together)
            if kx:
                moments.turn(0, together, kx)
            if kz:
                moments.turn(2, together, kz)
    hydro = moments.loads(offset)

    touch = end_contact(groups, tiles[CONTACT_TILE], high, [state[q] for q in range(10)])
    ends = lane == 0, lane == 127
    masks = [edge[CODE_AT + s] == cell_codes(lane, row) for s in range(2)]
    for f in range(6):
        for s in range(2):
            value = jnp.where(masks[s], hydro[f], 0.0)
            value = value + roll(value, -16, 1)
            value = value + roll(value, -1, 0)
            value = value + roll(value, -1, 1)
            value = jnp.where(
                ends[0], roll(value, -4, 1), jnp.where(ends[1], roll(value, 117, 1), 0.0)
            )
            both = jnp.concatenate([value[2:3], value[4:5]], axis=0)
            both = both + touch[f][4 * s : 4 * s + 2] + bulk_contact[f, 4 * s : 4 * s + 2, :]
            out_loads[f, s, 0] = bulk_loads[f, 2 * s : 2 * s + 2, :] + both
    copy = pltpu.make_async_copy(out_loads, final_loads, sems.at[len(PARTS)])
    copy.start()
    for copy in copies + [copy]:
        copy.wait()


PARAMS = pltpu.CompilerParams(vmem_limit_bytes=32 * 2**20)


def call(kernel, operands, shapes, scratch=(), spaces=(pltpu.VMEM, pltpu.VMEM)):
    return pl.pallas_call(
        kernel,
        out_shape=[jax.ShapeDtypeStruct(shape, F32) for shape in shapes],
        in_specs=[pl.BlockSpec(memory_space=spaces[0])] * len(operands),
        out_specs=[pl.BlockSpec(memory_space=spaces[1])] * len(shapes),
        scratch_shapes=[pltpu.VMEM(x, F32) if isinstance(x, tuple) else x for x in scratch],
        compiler_params=PARAMS,
    )(*operands)


def step(paired, sizes, *blocks):
    nx, ny, nz = sizes
    axes = ("gx", "gy", "gz")
    groups = 2 if paired else 3

    def permute(value, target):
        pairs = []
        for x in range(nx):
            for y in range(ny):
                for z in range(nz):
                    tx, ty, tz = target(x, y, z)
                    there = ((tx % nx) * ny + ty % ny) * nz + tz % nz
                    pairs.append(((x * ny + y) * nz + z, there))
        return lax.ppermute(value, axes, pairs)

    def swap(value):
        return permute(value, lambda x, y, z: (1 - x, y, z))

    def to_low(value):
        return permute(value, lambda x, y, z: (x - 1, y, z))

    def to_high(value):
        return permute(value, lambda x, y, z: (x + 1, y, z))

    ends_y = (Y_BLOCKS, 8, 128)
    shape_z = (Z_TILES // 2 if paired else Z_TILES, 8, 128)
    shape_y = (groups,) + ends_y
    sides = None if paired else (1, 1)
    held = [pltpu.VMEM(block.shape, block.dtype) for block in blocks]
    held[0] = pltpu.VMEM((22,) + blocks[0].shape[1:], F32)
    blocks = [pltpu.with_memory_space_constraint(block, pltpu.HBM) for block in blocks]
    whole, mine, theirs = call(
        functools.partial(pack_kernel, sides),
        blocks,
        [(W_BLOCKS, 8, 128), shape_y, ends_y],
        held + [pltpu.SemaphoreType.DMA((6 + len(POPS_PARTS),))],
        (pltpu.HBM, pltpu.VMEM),
    )

    def pack_z(sides, wholes, halos):
        kernel = functools.partial(z_pack_kernel, groups, paired, sides)
        return call(kernel, wholes + halos, [shape_z], [(2,) + shape_y])[0]

    def pack_bulk(wholes, halos):
        scratch = [
            (2,) + shape_y,
            (36, 2 * groups, 8, 256),
            (4, 4, 8, 256),
            (19, 4, 8, 256),
            (3, 4, 8, 256),
        ]
        return call(
            functools.partial(bulk_kernel, groups, paired, sides),
            wholes + halos,
            [(W_GRAIN, 8, 128), (6, 4, 128)],
            scratch,
        )

    if paired:
        rows = mine.at[1].set(swap(theirs))
        wholes = [whole, swap(whole)]
        first = permute(rows, lambda x, y, z: (x, y + (1 if (x + y) % 2 == 0 else -1), z))
        halos = [first, swap(first)]
        first = permute(
            pack_z(sides, wholes, halos),
            lambda x, y, z: (x, y, z + (1 if (x + z) % 2 == 0 else -1)),
        )
        bulk = pack_bulk(wholes, halos)
        first, bulk = lax.optimization_barrier((first, bulk))
        ends = [first, swap(first)]
    else:
        wholes = [whole, to_low(whole), to_high(whole)]
        up, down = [jnp.stack([v, to_low(v), to_high(v)]) for v in (mine[0], theirs)]
        halos = [
            permute(down, lambda x, y, z: (x, y - 1, z)),
            permute(up, lambda x, y, z: (x, y + 1, z)),
        ]
        low = (1, 0)
        ends = [
            permute(pack_z(low, wholes, halos), lambda x, y, z: (x, y, z - 1)),
            permute(pack_z(sides, wholes, halos), lambda x, y, z: (x, y, z + 1)),
        ]
        bulk = pack_bulk(wholes, halos)
    side = call(
        functools.partial(side_kernel, groups, paired, sides),
        wholes + halos + ends[:1],
        [(6, 8, 128), (EDGE_VALUES, 8, 128), (10, 8, 128)],
        [(2,) + shape_y],
    )
    populations, offset = blocks[0], blocks[2]
    shapes = [populations.shape, (6,) + offset.shape[1:]]
    return tuple(
        call(
            functools.partial(edge_kernel, groups, paired, sides),
            list(bulk) + list(side) + ends[1:],
            shapes,
            shapes + [pltpu.SemaphoreType.DMA((len(PARTS) + 1,))],
            (pltpu.VMEM, pltpu.HBM),
        )
    )


def solution(mesh, paired=None):
    sizes = tuple(mesh.shape[axis] for axis in ("gx", "gy", "gz"))
    if paired is None:
        paired = sizes[0] == 2 and sizes[1] % 2 == 0 and sizes[2] % 2 == 0
    cells, bins = P(None, "gx", "gy", "gz"), P(None, None, "gx", "gy", "gz")
    return jax.shard_map(
        functools.partial(step, paired, sizes),
        mesh=mesh,
        in_specs=(cells, cells, bins, cells, bins, bins, bins),
        out_specs=(cells, bins),
        check_vma=False,
    )
```

```python
import functools

import jax
import jax.numpy as jnp
from jax import lax
from jax.experimental import pallas as pl
from jax.experimental.pallas import tpu as pltpu
from jax.sharding import PartitionSpec as P

VELOCITIES = [
    (0, 0, 0),
    (1, 0, 0),
    (-1, 0, 0),
    (0, 1, 0),
    (0, -1, 0),
    (0, 0, 1),
    (0, 0, -1),
    (1, 1, 0),
    (-1, -1, 0),
    (1, -1, 0),
    (-1, 1, 0),
    (1, 0, 1),
    (-1, 0, -1),
    (1, 0, -1),
    (-1, 0, 1),
    (0, 1, 1),
    (0, -1, -1),
    (0, 1, -1),
    (0, -1, 1),
]
WEIGHTS = [1.0 / 3.0] + [1.0 / 18.0] * 6 + [1.0 / 36.0] * 12
relax_time = 0.8
fraction_floor = 0.1
distance_floor = 0.5

E0, RADIUS, CODE, PLACE = 9, 36, 37, 38
POPS_AT, CODE_AT, EDGE_VALUES = 36, 55, 57
Z_TILES, CONTACT_TILE = 8, 7
Y_FIELDS = list(range(9)) + [RADIUS, CODE]
Y_MEMBERS = [m for m in range(19) if VELOCITIES[m][1]] + [19, 20, 21]
Y_STANDS = {0: 10, 1: 11, 5: 12}
Y_GRAIN, Y_BLOCKS = 52, 14
W_GRAIN, W_BLOCKS = 38, 57
F32 = jnp.float32


def end_flags(sides):
    if sides is not None:
        return sides
    ix, iy, iz = [lax.axis_index(axis) for axis in ("gx", "gy", "gz")]
    return 1 - lax.rem(ix + iy, 2), 1 - lax.rem(ix + iz, 2)


def iota(shape, dim):
    return lax.broadcasted_iota(jnp.int32, shape, dim)


def pick_lanes(values, index):
    return jnp.take_along_axis(values, index, axis=1, mode="promise_in_bounds")


def roll(values, shift, axis):
    size = values.shape[axis]
    return pltpu.roll(values, shift % size, axis) if shift % size else values


def cross(a, b):
    return [
        a[1] * b[2] - a[2] * b[1],
        a[2] * b[0] - a[0] * b[2],
        a[0] * b[1] - a[1] * b[0],
    ]


def pack_kernel(sides, *refs):
    flags = end_flags(sides)
    sources, (whole, mine, theirs), held, sems = refs[:7], refs[7:10], refs[10:17], refs[17]
    copies = [
        pltpu.make_async_copy(source, target, sems.at[n])
        for n, (source, target) in enumerate(zip(sources[1:], held[1:]))
    ]
    for n, part in enumerate(POPS_PARTS):
        part = pl.ds(*part)
        copies.append(pltpu.make_async_copy(sources[0].at[part], held[0].at[part], sems.at[6 + n]))
    for copy in copies:
        copy.start()
    pops, cell, off, rad, vel, spin, inter = held
    for copy in copies[:6]:
        copy.wait()

    def slot(s, field, rows=slice(None)):
        if field < 3:
            return vel[field, s, 0, rows, :]
        if field < 6:
            return spin[field - 3, s, 0, rows, :]
        if field < 9:
            return off[field - 6, s, 0, rows, :]
        if field < RADIUS:
            return inter[field - E0, s, 0, rows, :]
        if field == RADIUS:
            return rad[s, 0, rows, :]
        return cell[s, 0, rows, :].astype(F32)

    for field in range(38):
        for s in range(2):
            at = 4 * (field % 2) + 2 * s
            whole[W_GRAIN + field // 2, at : at + 2, :] = slot(s, field)
    for out, end in ((mine.at[0], flags[0]), (theirs, 1 - flags[0])):
        for s in range(2):
            for f in range(29):
                if f < 11:
                    value = slot(s, Y_FIELDS[f], pl.ds(end, 1))
                else:
                    kx, q, kz = (f - 11) // 6, (f - 11) // 3 % 2, (f - 11) % 3
                    value = inter[9 * kx + 3 * (q + end) + kz, s, 0, pl.ds(end, 1), :]
                r = Y_GRAIN + 2 * f + s
                out[r // 8, r % 8 : r % 8 + 1, :] = value
        out[Y_BLOCKS - 1, 6:8, :] = jnp.zeros((2, 128), F32)
    for copy in copies[6:]:
        copy.wait()
    still = [m for m in range(19) if not VELOCITIES[m][1]]
    for i in range(2):
        sums = []
        for c in (0, 2):
            rising = [pops[m, i] for m in still if VELOCITIES[m][c] > 0]
            falling = [pops[m, i] for m in still if VELOCITIES[m][c] < 0]
            sums.append(sum(rising[1:], rising[0]) - sum(falling[1:], falling[0]))
        total = sum([pops[m, i] for m in still[1:]], pops[0, i])
        pops[19, i] = total - sums[0] - sums[1]
        pops[20, i] = sums[0]
        pops[21, i] = sums[1]
    for out, end in ((mine.at[0], flags[0]), (theirs, 1 - flags[0])):
        for n, member in enumerate(Y_MEMBERS):
            for i in range(2):
                row = pops[member, i, pl.ds(3 * end, 1), :]
                for t in range(2):
                    r = 4 * n + 2 * i + t
                    out[r // 8, r % 8 : r % 8 + 1, :] = row[:, 128 * t : 128 * t + 128]
    for member in range(19):
        for i in range(2):
            for t in range(2):
                tile = pops[member, i, :, 128 * t : 128 * t + 128]
                whole[2 * member + i, 4 * t : 4 * t + 4, :] = tile


class Block:
    def __init__(self, whole, halos, group):
        self.whole, self.halos, self.group = whole, halos, group

    def slot(self, s, field):
        at = 4 * (field % 2) + 2 * s
        return self.whole[W_GRAIN + field // 2, at : at + 2, :]

    def pops(self, member, i, t):
        return self.whole[2 * member + i, 4 * t : 4 * t + 4, :]

    def halo_pops(self, end, member, i, t):
        if VELOCITIES[member][1]:
            n = Y_MEMBERS.index(member)
        elif member in Y_STANDS:
            n = Y_STANDS[member]
        else:
            return jnp.zeros((1, 128), F32)
        r = 4 * n + 2 * i + t
        return self.halos[end, self.group, r // 8, r % 8 : r % 8 + 1, :]

    def halo_slot(self, end, s, field):
        if field in Y_FIELDS:
            f = Y_FIELDS.index(field)
        else:
            k = field - E0
            q = k // 3 % 3 - (1 - end)
            if q not in (0, 1):
                return jnp.zeros((1, 128), F32)
            f = 11 + 6 * (k // 9) + 3 * q + k % 3
        r = Y_GRAIN + 2 * f + s
        return self.halos[end, self.group, r // 8, r % 8 : r % 8 + 1, :]

    def bins(self, s, field):
        row = iota((8, 128), 0)
        n, at = W_GRAIN + field // 2, 4 * (field % 2) + 2 * s
        rows = [
            self.halo_slot(0, s, field),
            self.whole[n, at : at + 1, :],
            self.whole[n, at + 1 : at + 2, :],
            self.halo_slot(1, s, field),
        ]
        rows = [jnp.broadcast_to(value, (8, 128)) for value in rows]
        return jnp.where(
            row < 4,
            jnp.where(row < 2, rows[0], rows[1]),
            jnp.where(row < 6, rows[2], rows[3]),
        )

    def cells(self, member, i, t):
        row = iota((8, 128), 0)
        own = self.whole[2 * member + i]
        if isinstance(t, int):
            own = roll(own, 2 - 4 * t, 0)
            low, high = [self.halo_pops(end, member, i, t) for end in range(2)]
        else:
            own = jnp.where(t, roll(own, -2, 0), roll(own, 2, 0))
            low, high = [
                jnp.where(
                    t, self.halo_pops(end, member, i, 1), self.halo_pops(end, member, i, 0)
                )
                for end in range(2)
            ]
        low, high = jnp.broadcast_to(low, (8, 128)), jnp.broadcast_to(high, (8, 128))
        return jnp.where(row < 2, low, jnp.where(row > 5, high, own))


def position(code, offset):
    first = jnp.floor(code * 0.25)
    rest = code - 4.0 * first
    second = jnp.floor(rest * 0.5)
    corner = [first, second, rest - 2.0 * second]
    return [corner[c] + offset[c] for c in range(3)]


def store_ends(groups, paired, side, first, second, held):
    for g in range(groups):
        held[side, g] = first[g]
        held[1 - side, g] = second[(g + 1) % 2 if paired else g]


def lane_groups(groups):
    return [0, 1, 0, 1] if groups == 2 else [0, 1, 1, 2]


def by_group(groups, values, lane):
    order = lane_groups(groups)
    result = values[order[3]]
    for q in (2, 1, 0):
        if order[q] != order[q + 1] or q < 2:
            result = jnp.where(lane < 32 * (q + 1), values[order[q]], result)
    return result


def by_layer(groups, values, lane):
    odd = lane // 16 % 2 == 1
    pairs = [jnp.where(odd, values[2 * g + 1], values[2 * g]) for g in range(groups)]
    return by_group(groups, pairs, lane)


def cell_codes(lane, row):
    return (4 * (lane // 16 % 2) + 2 * (row % 2) + lane % 2).astype(F32)


def choose(masks, values):
    return jnp.where(masks[0], values[0], jnp.where(masks[1], values[1], 0.0))


def z_pack_kernel(groups, paired, sides, *refs):
    flags = end_flags(sides)
    wholes, (first, second, out, held) = refs[:groups], refs[groups:]
    store_ends(groups, paired, flags[0], first, second, held)
    high = flags[1] == 1
    lane, row = iota((8, 128), 1), iota((8, 128), 0)
    block = [Block(wholes[g], held, g) for g in range(groups)]
    start = jnp.where(high, 127, 0)
    index = jnp.full((8, 128), start, jnp.int32)
    pops_index = jnp.full((8, 128), jnp.where(high, 126, 0), jnp.int32) + lane % 2
    inner = lane % 16 // 2

    def picked(s, field):
        values = [pick_lanes(block[g].bins(s, field), index) for g in range(groups)]
        return by_group(groups, values, lane)

    slots = [[picked(s, field) for field in range(38)] for s in range(2)]
    code = cell_codes(lane, row)
    masks = [slots[s][CODE] == code for s in range(2)]
    values = [choose(masks, [slots[0][f], slots[1][f]]) for f in range(36)]
    for member in range(19):
        tiles = []
        for layer in range(2 * groups):
            g, i = layer // 2, layer % 2
            tile = block[g].cells(member, i, high)
            tiles.append(pick_lanes(tile, pops_index))
        values.append(by_layer(groups, tiles, lane))
    for tile in range(CONTACT_TILE):
        packed = values[8 * tile]
        for q in range(1, 8):
            if 8 * tile + q < len(values):
                packed = jnp.where(inner == q, values[8 * tile + q], packed)
        out[tile] = packed
    packed = jnp.zeros((8, 128), F32)
    for s in range(2):
        state = position(slots[s][CODE], slots[s][6:9]) + [slots[s][RADIUS]] + slots[s][0:6]
        for q, value in enumerate(state):
            packed = jnp.where(lane % 32 == 16 * s + q, value, packed)
    out[CONTACT_TILE] = packed


def dot_lattice(vector, velocity):
    total = None
    for c in range(3):
        if vector[c]:
            if total is None:
                total = velocity[c] if vector[c] > 0 else -velocity[c]
            else:
                total = total + velocity[c] if vector[c] > 0 else total - velocity[c]
    return total


def equilibrium_base(velocity):
    return 1.0 - 1.5 * (
        velocity[0] * velocity[0] + velocity[1] * velocity[1] + velocity[2] * velocity[2]
    )


def collide(f, sums, members):
    fraction = 1.0 - jnp.exp(-sums[0])
    excess = relax_time - 0.5
    weight = fraction * excess / (1.0 - fraction + excess)
    inverse = 1.0 / jnp.maximum(sums[0], fraction_floor)
    solid_velocity = [sums[1 + c] * inverse for c in range(3)]
    density = sum(f[1:], f[0])
    momentum = []
    for c in range(3):
        plus = [f[m] for m in range(19) if VELOCITIES[m][c] > 0]
        minus = [f[m] for m in range(19) if VELOCITIES[m][c] < 0]
        momentum.append(sum(plus[1:], plus[0]) - sum(minus[1:], minus[0]))
    per_density = 1.0 / density
    fluid_velocity = [momentum[c] * per_density for c in range(3)]
    share = [weight * inverse * (momentum[c] - density * solid_velocity[c]) for c in range(3)]
    relax = (1.0 - weight) * (1.0 / relax_time)
    keep = 1.0 - relax
    fluid_base = equilibrium_base(fluid_velocity)
    solid_base = equilibrium_base(solid_velocity)
    done = {}
    for member in [0] + list(range(1, 19, 2)):
        reverse = member + 1 if member else 0
        if member not in members and reverse not in members:
            continue
        part = WEIGHTS[member] * density
        if member == 0:
            fluid = [part * fluid_base] * 2
            settled = [part * solid_base] * 2
        else:
            ends = []
            for base, velocity in (
                (fluid_base, fluid_velocity),
                (solid_base, solid_velocity),
            ):
                along = dot_lattice(VELOCITIES[member], velocity)
                even = base + 4.5 * along * along
                odd = 3.0 * along
                ends.append([part * (even + odd), part * (even - odd)])
            fluid, settled = ends
        pair = [f[member], f[reverse]]
        for way, m in enumerate((member, reverse)[: 2 if member else 1]):
            if m in members:
                exchange = (pair[1 - way] - fluid[1 - way]) - (pair[way] - settled[way])
                done[m] = keep * pair[way] + relax * fluid[way] + weight * exchange
    return done, share


def deposit_terms(weight, base, spin, k):
    terms = [weight]
    for c in range(3):
        u, v = (c + 1) % 3, (c + 2) % 3
        speed = base[c]
        if k[v]:
            speed = speed + spin[u] if k[v] > 0 else speed - spin[u]
        if k[u]:
            speed = speed - spin[v] if k[u] > 0 else speed + spin[v]
        terms.append(weight * speed)
    return terms


def plus(totals, terms):
    return list(terms) if totals is None else [a + b for a, b in zip(totals, terms)]


class Moments:
    def __init__(self):
        self.force, self.moment = [None] * 3, [None] * 3

    def add(self, store, c, value, sign):
        if store[c] is None:
            store[c] = value if sign > 0 else -value
        else:
            store[c] = store[c] + value if sign > 0 else store[c] - value

    def turn(self, axis, forces, sign):
        u, v = (axis + 1) % 3, (axis + 2) % 3
        self.add(self.moment, v, forces[u], sign)
        self.add(self.moment, u, forces[v], -sign)

    def push(self, forces):
        for c in range(3):
            self.add(self.force, c, forces[c], 1)

    def loads(self, offset):
        turned = cross([0.5 - value for value in offset], self.force)
        return self.force + [self.moment[c] + turned[c] for c in range(3)]


def pair_force(gap, a_radius, a_speed, a_turn, other, keep=None):
    b_radius = other[0]
    distance = jnp.sqrt(gap[0] * gap[0] + gap[1] * gap[1] + gap[2] * gap[2])
    scale = 1.0 / jnp.maximum(distance, distance_floor)
    normal = [gap[c] * scale for c in range(3)]
    depth = jnp.maximum(a_radius + b_radius - distance, 0.0)
    strength = a_radius * b_radius * depth
    if keep is not None:
        strength = jnp.where(keep, strength, 0.0)
    turning = [a_turn[c] + b_radius * other[4 + c] for c in range(3)]
    swing = cross(turning, normal)
    relative = [a_speed[c] - other[1 + c] + swing[c] for c in range(3)]
    along = relative[0] * normal[0] + relative[1] * normal[1] + relative[2] * normal[2]
    factor = 1.0 + along
    pushed = [strength * (factor * normal[c] + relative[c]) for c in range(3)]
    return pushed, cross(normal, pushed)


def own_state(block):
    def rows(field):
        values = [block.slot(s, field) for s in range(2)]
        return jnp.concatenate([values[0], values[0], values[1], values[1]], axis=0)

    place = position(rows(CODE), [rows(6 + c) for c in range(3)])
    return place, [rows(RADIUS)] + [rows(c) for c in range(6)]


def end_lanes(high, inner):
    start = jnp.where(high, 12, 2)
    return (inner == start) | (inner == start + 1)


def end_contact(groups, tile, high, state):
    lane = iota((8, 128), 1)
    step_x, step_y = lane % 16 - 1, lane // 16 - 1
    place, a_radius, a_speed, a_spin = state[0:3], state[3], state[4:7], state[7:10]
    a_turn = [a_radius * value for value in a_spin]
    before = lane_groups(groups).index(groups - 1)
    run = 32 * jnp.where(step_x < 0, before, jnp.where(step_x == 0, 0, 1))
    other = [None] * 10
    for oy in (-1, 0, 1):
        at = 2 * (oy + 1)
        rows = jnp.concatenate([tile[at : at + 1], tile[at + 2 : at + 3]], axis=0)
        moved = roll(rows, -16, 1)
        rows = jnp.concatenate([rows, moved, rows, moved], axis=0)
        for q in range(10):
            value = pick_lanes(rows, run + q)
            other[q] = value if oy < 0 else jnp.where(step_y == oy, value, other[q])
    keep = (step_x < 2) & (step_y < 2)
    gap = [
        other[0] - place[0] + (2 * step_x).astype(F32),
        other[1] - place[1] + (2 * step_y).astype(F32),
        other[2] - place[2] + jnp.where(high, 2.0, -2.0),
    ]
    pushed, twisted = pair_force(gap, a_radius, a_speed, a_turn, other[3:], keep)
    contact = [-value for value in pushed] + [-a_radius * value for value in twisted]
    end = lane == jnp.where(high, 127, 0)
    result = []
    for value in contact:
        value = value + roll(value, -2, 0)
        value = value + roll(value, -1, 1) + roll(value, -2, 1)
        value = value + roll(value, -16, 1) + roll(value, -32, 1)
        result.append(jnp.where(end, jnp.where(high, roll(value, 127, 1), value), 0.0))
    return result


POPS_PARTS = [(0, 5), (5, 5), (10, 5), (15, 4)]
PARTS = [18]
AT_LAYER = {0: 0, 1: 1, 2: 2, -1: 3}


def bulk_kernel(groups, paired, sides, *refs):
    flags = end_flags(sides)
    layers = 2 * groups
    wholes, (y_first, y_second) = refs[:groups], refs[groups : groups + 2]
    out_pops, out_loads = refs[groups + 2 : groups + 4]
    held, placed, solid, passed, share = refs[groups + 4 :]
    targets = [0, 1, 2, layers - 1]
    store_ends(groups, paired, flags[0], y_first, y_second, held)
    block = [Block(wholes[g], held, g) for g in range(groups)]
    lane8 = iota((8, 128), 1)
    half = lane8 // 2

    def spread(rows):
        return jnp.concatenate([pick_lanes(rows, half), pick_lanes(rows, half + 64)], axis=1)

    cell_code = (2 * (iota((8, 256), 0) % 2) + iota((8, 256), 1) % 2).astype(F32)
    masks = []
    codes = [[block[g].bins(s, CODE) for g in range(groups)] for s in range(2)]
    for g in range(groups):
        wide = [spread(codes[s][g]) for s in range(2)]
        for i in range(2):
            masks.append([wide[s] == cell_code + 4.0 * i for s in range(2)])
    for field in range(36):
        rows = [[block[g].bins(s, field) for g in range(groups)] for s in range(2)]
        for g in range(groups):
            values = [spread(rows[s][g]) for s in range(2)]
            for i in range(2):
                placed[field, 2 * g + i] = choose(masks[2 * g + i], values)
    for layer in range(layers):
        spin = [placed[3 + c, layer] for c in range(3)]
        turned = cross(spin, [0.5 - placed[6 + c, layer] for c in range(3)])
        for c in range(3):
            placed[c, layer] = placed[c, layer] + turned[c]

    for n, target in enumerate(targets):
        total = None
        for kz in (-1, 0, 1):
            along_z = None
            for ky in (-1, 0, 1):
                along_y = None
                for kx in (-1, 0, 1):
                    source = (target - kx) % layers
                    weight = placed[E0 + 9 * (kx + 1) + 3 * (ky + 1) + kz + 1, source]
                    spin = [placed[3 + c, source] for c in range(3)]
                    base = [placed[c, source] for c in range(3)]
                    along_y = plus(along_y, deposit_terms(weight, base, spin, (kx, ky, kz)))
                along_z = plus(along_z, [roll(a, ky, 0) for a in along_y])
            total = plus(total, [roll(a, kz, 1) for a in along_z])
        for f in range(4):
            solid[f, n] = total[f]

    for n, target in enumerate(targets):
        g, i = target // 2, target % 2
        if n < 2:
            members = list(range(19))
        else:
            members = [m for m in range(19) if VELOCITIES[m][0] == (-1 if n == 2 else 1)]
        for t in range(2):
            tile = slice(128 * t, 128 * t + 128)
            f = [block[g].cells(member, i, t) for member in range(19)]
            done, forces = collide(f, [solid[c, n, :, tile] for c in range(4)], members)
            for c in range(3):
                share[c, n, :, tile] = forces[c]
            for m, value in done.items():
                passed[m, n, :, tile] = value
    for member in range(19):
        vector = VELOCITIES[member]
        for i in range(2):
            value = roll(passed[member, AT_LAYER[i - vector[0]]], vector[2], 1)
            value = roll(value, vector[1] - 2, 0)
            for t in range(2):
                out_pops[2 * member + i, 4 * t : 4 * t + 4, :] = value[
                    0:4, 128 * t : 128 * t + 128
                ]

    moments = [Moments() for _ in range(2)]
    for kz in (-1, 0, 1):
        across = [[roll(share[c, n], -kz, 1) for c in range(3)] for n in range(4)]
        for ky in (-1, 0, 1):
            near = [[roll(across[n][c], -ky, 0) for c in range(3)] for n in range(4)]
            for i in range(2):
                together = None
                for kx in (-1, 0, 1):
                    weight = placed[E0 + 9 * (kx + 1) + 3 * (ky + 1) + kz + 1, i]
                    forces = [weight * near[AT_LAYER[i + kx]][c] for c in range(3)]
                    together = plus(together, forces)
                    if kx:
                        moments[i].turn(0, forces, kx)
                moments[i].push(together)
                if ky:
                    moments[i].turn(1, together, ky)
                if kz:
                    moments[i].turn(2, together, kz)
    hydro = [moments[i].loads([placed[6 + c, i] for c in range(3)]) for i in range(2)]

    even = (2 * lane8) % 128
    inside = (lane8 > 0) & (lane8 < 127)
    for f in range(6):
        for s in range(2):
            value = jnp.where(masks[0][s], hydro[0][f], 0.0) + jnp.where(
                masks[1][s], hydro[1][f], 0.0
            )
            value = value + roll(value, -1, 0)
            value = value + roll(value, -1, 1)
            value = jnp.where(
                lane8 < 64, pick_lanes(value[:, :128], even), pick_lanes(value[:, 128:], even)
            )
            value = jnp.where(inside, value, 0.0)
            both = jnp.concatenate([value[2:3], value[4:5]], axis=0)
            out_loads[f, 2 * s : 2 * s + 2, :] = both


def side_kernel(groups, paired, sides, *refs):
    flags = end_flags(sides)
    layers = 2 * groups
    wholes, (y_first, y_second, z_first) = refs[:groups], refs[groups : groups + 3]
    out_contact, out_edge, out_state, held = refs[groups + 3 :]
    high = flags[1] == 1
    store_ends(groups, paired, flags[0], y_first, y_second, held)
    block = [Block(wholes[g], held, g) for g in range(groups)]
    lane8, row8 = iota((8, 128), 1), iota((8, 128), 0)
    inner = lane8 % 16
    z_near = jnp.where(inner < 8, jnp.maximum(inner - 4, 0), jnp.minimum(inner + 116, 127))
    z_bin = jnp.where(inner < 8, z_near // 2, jnp.minimum(inner + 244, 255) // 2)

    def at_edge(s, field):
        rows = [pick_lanes(block[g].bins(s, field), z_bin) for g in range(groups)]
        return by_group(groups, rows, lane8)

    tiles = [
        jnp.where(high, roll(z_first[tile], 10, 1), z_first[tile]) for tile in range(CONTACT_TILE)
    ]
    filled = end_lanes(high, inner)

    def store(field, value):
        halo = roll(tiles[field // 8], 2 - 2 * (field % 8), 1)
        out_edge[field] = jnp.where(filled, halo, value)

    edge_code = cell_codes(lane8, row8)
    codes = [at_edge(s, CODE) for s in range(2)]
    for s in range(2):
        out_edge[CODE_AT + s] = codes[s]
    edge_masks = [value == edge_code for value in codes]
    for field in range(36):
        store(field, choose(edge_masks, [at_edge(s, field) for s in range(2)]))
    for member in range(19):
        near_tiles = []
        for layer in range(layers):
            near = [block[layer // 2].cells(member, layer % 2, t) for t in range(2)]
            near_tiles.append(
                jnp.where(inner < 8, pick_lanes(near[0], z_near), pick_lanes(near[1], z_near))
            )
        store(POPS_AT + member, by_layer(groups, near_tiles, lane8))

    place, state = own_state(block[0])
    a_radius, a_speed = state[0], state[1:4]
    a_turn = [a_radius * value for value in state[4:7]]
    push, twist = None, None
    for oy in (-1, 0, 1):
        for g in range(groups):
            steps = [0] if g == 0 else []
            if g == 1:
                steps = steps + [1]
            if g == groups - 1:
                steps = steps + [-1]
            states = []
            for field in [CODE, 6, 7, 8, RADIUS, 0, 1, 2, 3, 4, 5]:
                values = []
                for s in range(2):
                    value = block[g].slot(s, field)
                    if oy < 0:
                        value = jnp.concatenate(
                            [block[g].halo_slot(0, s, field), value[0:1]], axis=0
                        )
                    if oy > 0:
                        value = jnp.concatenate(
                            [value[1:2], block[g].halo_slot(1, s, field)], axis=0
                        )
                    values.append(value)
                states.append(jnp.concatenate(values + values, axis=0))
            states = position(states[0], states[1:4]) + states[4:]
            for oz in (-1, 0, 1):
                other = [roll(value, -oz, 1) for value in states]
                keep = lane8 != (0 if oz < 0 else 127) if oz else None
                gap = [other[c] - place[c] for c in range(3)]
                gap[1], gap[2] = gap[1] + 2.0 * oy, gap[2] + 2.0 * oz
                for ox in steps:
                    apart = [gap[0] + 2.0 * ox, gap[1], gap[2]]
                    pushed, twisted = pair_force(
                        apart, a_radius, a_speed, a_turn, other[3:], keep
                    )
                    push, twist = plus(push, pushed), plus(twist, twisted)
    contact = [-value for value in push] + [-a_radius * value for value in twist]
    contact = [value + roll(value, -2, 0) for value in contact]

    ends = [jnp.where(high, 127, 0), jnp.where(high, 0, 127)]
    ends = [jnp.full((8, 128), end, jnp.int32) for end in ends]
    picked = [pick_lanes(value, ends[0]) for value in place + state]
    touch = end_contact(groups, z_first[CONTACT_TILE], high, picked)
    for f in range(6):
        out_contact[f] = contact[f] + touch[f]
    for q, value in enumerate(place + state):
        out_state[q] = pick_lanes(value, ends[1])


def edge_kernel(
    groups, paired, sides, bulk_pops, bulk_loads, bulk_contact, edge, state, second, *refs
):
    final_pops, final_loads, out_pops, out_loads, sems = refs
    high = end_flags(sides)[1] == 0
    lane, row = iota((8, 128), 1), iota((8, 128), 0)
    tiles = [roll(second[tile], 32, 1) if paired else second[tile] for tile in range(Z_TILES)]
    moved = [jnp.where(high, roll(tiles[tile], 10, 1), tiles[tile]) for tile in range(CONTACT_TILE)]
    filled = end_lanes(high, lane % 16)

    def value_of(field):
        halo = roll(moved[field // 8], 2 - 2 * (field % 8), 1)
        return jnp.where(filled, halo, edge[field])

    speed, spin, offset = [[value_of(3 * n + c) for c in range(3)] for n in range(3)]
    weights = [value_of(E0 + k) for k in range(27)]
    turned = cross(spin, [0.5 - value for value in offset])
    base = [speed[c] + turned[c] for c in range(3)]
    sums = None
    for kx in (-1, 0, 1):
        for kz in (-1, 0, 1):
            along = None
            for ky in (-1, 0, 1):
                weight = weights[9 * (kx + 1) + 3 * (ky + 1) + kz + 1]
                terms = deposit_terms(weight, base, spin, (kx, ky, kz))
                along = plus(along, [roll(a, ky, 0) for a in terms])
            sums = plus(sums, [roll(a, 16 * kx + kz, 1) for a in along])
    f = [value_of(POPS_AT + member) for member in range(19)]
    done, share = collide(f, sums, list(range(19)))

    lane4 = iota((4, 128), 1)
    copies = []
    for member in range(19):
        vector = VELOCITIES[member]
        value = roll(done[member], vector[1] - 2, 0)
        shift = 16 * vector[0] + vector[2]
        for i in range(2):
            for t in range(2):
                home = shift - 16 * i + (116 if t else -4)
                moved = roll(value, home, 1)[0:4]
                bulk = bulk_pops[2 * member + i, 4 * t : 4 * t + 4, :]
                mask = lane4 >= 126 if t else lane4 < 2
                out_pops[member, i, :, 128 * t : 128 * t + 128] = jnp.where(mask, moved, bulk)
        if member in PARTS:
            n = PARTS.index(member)
            part = pl.ds(PARTS[n - 1] + 1 if n else 0, member - (PARTS[n - 1] if n else -1))
            copy = pltpu.make_async_copy(out_pops.at[part], final_pops.at[part], sems.at[n])
            copy.start()
            copies.append(copy)

    moments = Moments()
    for kx in (-1, 0, 1):
        for kz in (-1, 0, 1):
            near = [roll(share[c], -16 * kx - kz, 1) for c in range(3)]
            together = None
            for ky in (-1, 0, 1):
                weight = weights[9 * (kx + 1) + 3 * (ky + 1) + kz + 1]
                forces = [weight * roll(near[c], -ky, 0) for c in range(3)]
                together = plus(together, forces)
                if ky:
                    moments.turn(1, forces, ky)
            moments.push(together)
            if kx:
                moments.turn(0, together, kx)
            if kz:
                moments.turn(2, together, kz)
    hydro = moments.loads(offset)

    touch = end_contact(groups, tiles[CONTACT_TILE], high, [state[q] for q in range(10)])
    ends = lane == 0, lane == 127
    masks = [edge[CODE_AT + s] == cell_codes(lane, row) for s in range(2)]
    for f in range(6):
        for s in range(2):
            value = jnp.where(masks[s], hydro[f], 0.0)
            value = value + roll(value, -16, 1)
            value = value + roll(value, -1, 0)
            value = value + roll(value, -1, 1)
            value = jnp.where(
                ends[0], roll(value, -4, 1), jnp.where(ends[1], roll(value, 117, 1), 0.0)
            )
            both = jnp.concatenate([value[2:3], value[4:5]], axis=0)
            both = both + touch[f][4 * s : 4 * s + 2] + bulk_contact[f, 4 * s : 4 * s + 2, :]
            out_loads[f, s, 0] = bulk_loads[f, 2 * s : 2 * s + 2, :] + both
    copy = pltpu.make_async_copy(out_loads, final_loads, sems.at[len(PARTS)])
    copy.start()
    for copy in copies + [copy]:
        copy.wait()


PARAMS = pltpu.CompilerParams(vmem_limit_bytes=32 * 2**20)


def call(kernel, operands, shapes, scratch=(), spaces=(pltpu.VMEM, pltpu.VMEM)):
    return pl.pallas_call(
        kernel,
        out_shape=[jax.ShapeDtypeStruct(shape, F32) for shape in shapes],
        in_specs=[pl.BlockSpec(memory_space=spaces[0])] * len(operands),
        out_specs=[pl.BlockSpec(memory_space=spaces[1])] * len(shapes),
        scratch_shapes=[pltpu.VMEM(x, F32) if isinstance(x, tuple) else x for x in scratch],
        compiler_params=PARAMS,
    )(*operands)


def step(paired, sizes, *blocks):
    nx, ny, nz = sizes
    axes = ("gx", "gy", "gz")
    groups = 2 if paired else 3

    def permute(value, target):
        pairs = []
        for x in range(nx):
            for y in range(ny):
                for z in range(nz):
                    tx, ty, tz = target(x, y, z)
                    there = ((tx % nx) * ny + ty % ny) * nz + tz % nz
                    pairs.append(((x * ny + y) * nz + z, there))
        return lax.ppermute(value, axes, pairs)

    def swap(value):
        return permute(value, lambda x, y, z: (1 - x, y, z))

    def to_low(value):
        return permute(value, lambda x, y, z: (x - 1, y, z))

    def to_high(value):
        return permute(value, lambda x, y, z: (x + 1, y, z))

    ends_y = (Y_BLOCKS, 8, 128)
    shape_z = (Z_TILES, 8, 128)
    shape_y = (groups,) + ends_y
    sides = None if paired else (1, 1)
    held = [pltpu.VMEM(block.shape, block.dtype) for block in blocks]
    held[0] = pltpu.VMEM((22,) + blocks[0].shape[1:], F32)
    blocks = [pltpu.with_memory_space_constraint(block, pltpu.HBM) for block in blocks]
    whole, mine, theirs = call(
        functools.partial(pack_kernel, sides),
        blocks,
        [(W_BLOCKS, 8, 128), shape_y, ends_y],
        held + [pltpu.SemaphoreType.DMA((6 + len(POPS_PARTS),))],
        (pltpu.HBM, pltpu.VMEM),
    )

    def pack_z(sides, wholes, halos):
        kernel = functools.partial(z_pack_kernel, groups, paired, sides)
        return call(kernel, wholes + halos, [shape_z], [(2,) + shape_y])[0]

    def pack_bulk(wholes, halos):
        scratch = [
            (2,) + shape_y,
            (36, 2 * groups, 8, 256),
            (4, 4, 8, 256),
            (19, 4, 8, 256),
            (3, 4, 8, 256),
        ]
        return call(
            functools.partial(bulk_kernel, groups, paired, sides),
            wholes + halos,
            [(W_GRAIN, 8, 128), (6, 4, 128)],
            scratch,
        )

    if paired:
        rows = mine.at[1].set(swap(theirs))
        wholes = [whole, swap(whole)]
        first = permute(rows, lambda x, y, z: (x, y + (1 if (x + y) % 2 == 0 else -1), z))
        halos = [first, swap(first)]
        first = permute(
            pack_z(sides, wholes, halos),
            lambda x, y, z: (x, y, z + (1 if (x + z) % 2 == 0 else -1)),
        )
        bulk = pack_bulk(wholes, halos)
        first, bulk = lax.optimization_barrier((first, bulk))
        ends = [first, swap(first)]
    else:
        wholes = [whole, to_low(whole), to_high(whole)]
        up, down = [jnp.stack([v, to_low(v), to_high(v)]) for v in (mine[0], theirs)]
        halos = [
            permute(down, lambda x, y, z: (x, y - 1, z)),
            permute(up, lambda x, y, z: (x, y + 1, z)),
        ]
        low = (1, 0)
        ends = [
            permute(pack_z(low, wholes, halos), lambda x, y, z: (x, y, z - 1)),
            permute(pack_z(sides, wholes, halos), lambda x, y, z: (x, y, z + 1)),
        ]
        bulk = pack_bulk(wholes, halos)
    side = call(
        functools.partial(side_kernel, groups, paired, sides),
        wholes + halos + ends[:1],
        [(6, 8, 128), (EDGE_VALUES, 8, 128), (10, 8, 128)],
        [(2,) + shape_y],
    )
    populations, offset = blocks[0], blocks[2]
    shapes = [populations.shape, (6,) + offset.shape[1:]]
    return tuple(
        call(
            functools.partial(edge_kernel, groups, paired, sides),
            list(bulk) + list(side) + ends[1:],
            shapes,
            shapes + [pltpu.SemaphoreType.DMA((len(PARTS) + 1,))],
            (pltpu.VMEM, pltpu.HBM),
        )
    )


def solution(mesh, paired=None):
    sizes = tuple(mesh.shape[axis] for axis in ("gx", "gy", "gz"))
    if paired is None:
        paired = sizes[0] == 2 and sizes[1] % 2 == 0 and sizes[2] % 2 == 0
    cells, bins = P(None, "gx", "gy", "gz"), P(None, None, "gx", "gy", "gz")
    return jax.shard_map(
        functools.partial(step, paired, sizes),
        mesh=mesh,
        in_specs=(cells, cells, bins, cells, bins, bins, bins),
        out_specs=(cells, bins),
        check_vma=False,
    )
```
